32 devices in a mesh: shard: 8 (over z, x), replica: 4 (over y, core).
Axes of the slice: x: 2, y: 2, z: 4, core: 2. Of those that a mesh axis runs over, the one named last changes fastest.
Arguments:
- tokens: bfloat16 [4096, 1024], P(('shard', 'replica')), may hold values from -6 to 6
- cotangent: bfloat16 [4096, 1024], P(('shard', 'replica')), may hold values from -6 to 6
- seq_lengths: int32 [32, 4], P(('shard', 'replica')), may hold values from 0 to 128, as said below
- seq_starts: int32 [32, 4], P(('shard', 'replica')), may hold values from 0 to 128, as said below
- in_gain: bfloat16 [1024], P('shard'), may hold values from 0.5 to 1.5
- w_in: bfloat16 [1024, 3352], P('shard'), may hold values from -0.1875 to 0.1875
- conv_w: bfloat16 [4, 1792], P(None, 'shard'), may hold values from -3 to 3
- conv_b: bfloat16 [1792], P('shard'), may hold values from -0.5 to 0.5
- a_log: float32 [24], replicated, may hold values from -3 to 1
- dt_bias: float32 [24], replicated, may hold values from -5 to -1
- skip_d: float32 [24], replicated, may hold values from 0.5 to 1.5
- ssm_gain: bfloat16 [1536], P('shard'), may hold values from 0.5 to 1.5
- w_out: bfloat16 [1536, 1024], P('shard'), may hold values from -0.15625 to 0.15625
- w_query: bfloat16 [1024, 512], P('shard'), may hold values from -0.1875 to 0.1875
- w_key: bfloat16 [1024, 128], P('shard'), may hold values from -0.1875 to 0.1875
- w_value: bfloat16 [1024, 128], P('shard'), may hold values from -0.1875 to 0.1875
- w_attn_out: bfloat16 [512, 1024], P('shard'), may hold values from -1 to 1
- ff_gain: bfloat16 [1024], P('shard'), may hold values from 0.5 to 1.5
- w_gate: bfloat16 [1024, 2048], P('shard'), may hold values from -0.1875 to 0.1875
- w_up: bfloat16 [1024, 2048], P('shard'), may hold values from -0.1875 to 0.1875
- w_down: bfloat16 [2048, 1024], P('shard'), may hold values from -0.125 to 0.125
Outputs:
- block_out: bfloat16 [4096, 1024], P(('shard', 'replica'))
- tokens_grad: bfloat16 [4096, 1024], P(('shard', 'replica'))
- in_gain_grad: float32 [1024], P('shard')
- w_in_grad: float32 [1024, 3352], P('shard')
- conv_w_grad: float32 [4, 1792], P(None, 'shard')
- conv_b_grad: float32 [1792], P('shard')
- a_log_grad: float32 [24], replicated
- dt_bias_grad: float32 [24], replicated
- skip_d_grad: float32 [24], replicated
- ssm_gain_grad: float32 [1536], P('shard')
- w_out_grad: float32 [1536, 1024], P('shard')
- w_query_grad: float32 [1024, 512], P('shard')
- w_key_grad: float32 [1024, 128], P('shard')
- w_value_grad: float32 [1024, 128], P('shard')
- w_attn_out_grad: float32 [512, 1024], P('shard')
- ff_gain_grad: float32 [1024], P('shard')
- w_gate_grad: float32 [1024, 2048], P('shard')
- w_up_grad: float32 [1024, 2048], P('shard')
- w_down_grad: float32 [2048, 1024], P('shard')
The draws below stay inside these ranges and needn't reach their ends.
Inputs may be any that keep to these rules, and one draw needn't show every extreme that they name: `seq_lengths`: in each row the sequences lie in order, without intersection, inside the 128 slots; empty slots have length 0; some device holds one sequence of exactly 128 tokens. `seq_starts`: start of each slot's sequence in its row; starts do not fall along a row.
All inputs are finite; a program needn't handle non-finite values.
Results may differ from the reference program's by a relative error of at most 0.019.
Values may be sent and summed in bfloat16 or wider, within the bound.
No kernel may reach another device: no remote copies, remote signals or barrier semaphores. Data moves between devices by JAX's collectives and lax.ppermute only.
A program may use at most 192 MiB of HBM per device.

```python
import jax
import jax.numpy as jnp
from jax import lax

D = 1024
FF = 2048
MH = 24
HD = 64
NS = 128
QH = 8
KVH = 2
ATTENTION_HEAD = 64
CONV_K = 4
CAP = 128
SEQS = 4
NBLOCKS = 32
TOKENS = 4096


def sequence_layout(key):
    used_key, cut_key, gap_key, pick_key = jax.random.split(key, 4)
    used = jax.random.randint(used_key, (NBLOCKS,), CAP // 2, CAP + 1)
    cuts = jax.random.randint(cut_key, (NBLOCKS, SEQS - 1), 0, CAP + 1) % (used[:, None] + 1)
    cuts = jnp.sort(cuts, axis=1)
    edges = jnp.concatenate([jnp.zeros((NBLOCKS, 1), jnp.int32), cuts, used[:, None]], axis=1)
    lengths = edges[:, 1:] - edges[:, :-1]
    gap_size = jax.random.randint(gap_key, (NBLOCKS,), 0, CAP + 1) % (CAP - used + 1)
    starts = edges[:, :-1] + gap_size[:, None]
    chosen = jax.random.randint(pick_key, (), 0, NBLOCKS)
    slot_index = jnp.arange(SEQS)
    full_lengths = jnp.where(slot_index == 0, CAP, 0)
    full_starts = jnp.where(slot_index == 0, 0, CAP)
    picked = (jnp.arange(NBLOCKS) == chosen)[:, None]
    lengths = jnp.where(picked, full_lengths[None, :], lengths).astype(jnp.int32)
    starts = jnp.where(picked, full_starts[None, :], starts).astype(jnp.int32)
    return (lengths, starts)


def draw_seq_lengths(key, part):
    return sequence_layout(key)[0]


def draw_seq_starts(key, part):
    return sequence_layout(key)[1]


def shard_levels(own_key, shape, pieces, smallest, top_value):
    def one(dim, shards_of):
        draws = jax.random.uniform(jax.random.fold_in(jax.random.fold_in(own_key, 6), dim), (shards_of,), jnp.float32, smallest / len(pieces), top_value / len(pieces))
        return jnp.repeat(jnp.exp(draws), shape[dim] // shards_of).reshape((-1,) + (1,) * (len(shape) - dim - 1))

    loudness = one(*pieces[0])
    for cut in pieces[1:]:
        loudness = loudness * one(*cut)
    return loudness


def gaussian(own_key, shape, deviation, most, shards=(), kind=jnp.bfloat16):
    factor_of = shard_levels(own_key, shape, shards, -0.22, 0.18) if shards else 1.0
    values = jax.random.normal(own_key, shape, jnp.float32) * deviation * factor_of
    return jnp.minimum(jnp.maximum(values, -most), most).astype(kind)


def setup_inputs(seed: int = 0) -> dict:
    key_list = jax.random.split(jax.random.key(seed), 22)
    return {
        "tokens": gaussian(key_list[0], (TOKENS, D), 1.0, 6.0, ((0, 32),)),
        "cotangent": gaussian(key_list[1], (TOKENS, D), 1.0, 6.0, ((0, 32),)),
        "seq_lengths": draw_seq_lengths(jax.random.fold_in(key_list[21], 71), 0),
        "seq_starts": draw_seq_starts(jax.random.fold_in(key_list[21], 71), 0),
        "in_gain": jnp.clip(1.0 + 0.1 * jax.random.normal(key_list[4], (D,), jnp.float32), 0.5, 1.5).astype(jnp.bfloat16),
        "w_in": gaussian(key_list[5], (D, 2 * MH * HD + 2 * NS + MH), D ** -0.5, 0.1875, ((0, 8),)),
        "conv_w": gaussian(key_list[6], (CONV_K, MH * HD + 2 * NS), CONV_K ** -0.5, 3.0, ((1, 8),)),
        "conv_b": jnp.clip(jax.random.uniform(key_list[7], (MH * HD + 2 * NS,), jnp.float32, -0.5, 0.5) * shard_levels(key_list[7], (MH * HD + 2 * NS,), ((0, 8),), -0.4, 0.0), -0.5, 0.5).astype(jnp.bfloat16),
        "a_log": jnp.clip(jax.random.uniform(key_list[8], (MH,), jnp.float32, -3.0, 1.0), -3.0, 1.0),
        "dt_bias": jnp.clip(jax.random.uniform(key_list[9], (MH,), jnp.float32, -5.0, -1.0), -5.0, -1.0),
        "skip_d": jnp.clip(jax.random.uniform(key_list[10], (MH,), jnp.float32, 0.5, 1.5), 0.5, 1.5),
        "ssm_gain": jnp.clip(1.0 + 0.1 * jax.random.normal(key_list[11], (MH * HD,), jnp.float32), 0.5, 1.5).astype(jnp.bfloat16),
        "w_out": gaussian(key_list[12], (MH * HD, D), (MH * HD) ** -0.5, 0.15625, ((0, 8),)),
        "w_query": gaussian(key_list[13], (D, QH * ATTENTION_HEAD), D ** -0.5, 0.1875, ((0, 8),)),
        "w_key": gaussian(key_list[14], (D, KVH * ATTENTION_HEAD), D ** -0.5, 0.1875, ((0, 8),)),
        "w_value": gaussian(key_list[15], (D, KVH * ATTENTION_HEAD), D ** -0.5, 0.1875, ((0, 8),)),
        "w_attn_out": gaussian(key_list[16], (QH * ATTENTION_HEAD, D), (QH * ATTENTION_HEAD // 16) ** -0.5, 1.0, ((0, 8),)),
        "ff_gain": jnp.clip(1.0 + 0.1 * jax.random.normal(key_list[17], (D,), jnp.float32), 0.5, 1.5).astype(jnp.bfloat16),
        "w_gate": gaussian(key_list[18], (D, FF), D ** -0.5, 0.1875, ((0, 8),)),
        "w_up": gaussian(key_list[19], (D, FF), D ** -0.5, 0.1875, ((0, 8),)),
        "w_down": gaussian(key_list[20], (FF, D), FF ** -0.5, 0.125, ((0, 8),)),
    }


EPSILON = 1e-05
ROPE_BASE = 100000000000.0

@jax.custom_vjp
def low(v):
    return lax.optimization_barrier(v.astype(jnp.bfloat16)).astype(jnp.float32)

@jax.custom_vjp
def low_back(v):
    return v

def low_keep(v):
    return (low(v), None)

def low_pass(kept, grad):
    return (grad,)

def back_keep(v):
    return (v, None)

def back_low(kept, grad):
    return (low(grad),)
low.defvjp(low_keep, low_pass)
low_back.defvjp(back_keep, back_low)

def matmul_high(left, right):
    return jnp.dot(left, right, precision=lax.Precision.HIGHEST)

def rms_scale(values, gain):
    return values * lax.rsqrt(lax.optimization_barrier(jnp.mean(values * values, axis=-1, keepdims=True)) + EPSILON) * gain

def layout(lengths, starts, extent):
    position = jnp.arange(extent, dtype=jnp.int32)
    inside = (position[:, None] >= starts[None, :]) & (position[:, None] < starts[None, :] + lengths[None, :])
    number = jnp.arange(1, lengths.shape[0] + 1, dtype=jnp.int32)
    segment = lax.optimization_barrier(jnp.sum(jnp.where(inside, number[None, :], 0), axis=1)).astype(jnp.int32) - 1
    first = lax.optimization_barrier(jnp.sum(jnp.where(inside, starts[None, :], 0), axis=1)).astype(jnp.int32)
    return (segment, position - first)

def causal_allowed(segment):
    position = jnp.arange(segment.shape[0], dtype=jnp.int32)
    return (segment[:, None] == segment[None, :]) & (position[:, None] >= position[None, :])

def mixer_front(conv_in, raw_step, conv_w, conv_b, dt_bias, a_log, segment):
    extent = conv_in.shape[0]
    summed = conv_b[None, :] + conv_w[CONV_K - 1][None, :] * conv_in
    for offset in range(1, CONV_K):
        shifted = jnp.concatenate([jnp.zeros((offset, conv_in.shape[1]), conv_in.dtype), conv_in[:extent - offset]], axis=0)
        seg_moved = jnp.concatenate([jnp.full((offset,), -2, jnp.int32), segment[:extent - offset]])
        summed = summed + conv_w[CONV_K - 1 - offset][None, :] * jnp.where((seg_moved == segment)[:, None], shifted, 0.0)
    conv_act = jax.nn.silu(summed)
    time_step = jax.nn.softplus(raw_step + dt_bias[None, :])
    log_decay = jnp.cumsum(time_step * (-jnp.exp(a_log))[None, :], axis=0).T
    allowed = causal_allowed(segment)[None]
    spread = log_decay[:, :, None] - log_decay[:, None, :]
    decay_mat = jnp.where(allowed, jnp.exp(jnp.where(allowed, spread, 0.0)), 0.0)
    return (conv_act, time_step, decay_mat)

def rotate(values, position, heads):
    half_size = ATTENTION_HEAD // 2
    inverse = ROPE_BASE ** (-jnp.arange(half_size, dtype=jnp.float32) / half_size)
    angle = position.astype(jnp.float32)[:, None] * inverse[None, :]
    cosine = jnp.cos(angle)[:, None, :]
    sine_val = jnp.sin(angle)[:, None, :]
    shaped = values.reshape(values.shape[0], heads, ATTENTION_HEAD)
    first_half = shaped[..., :half_size]
    second_half = shaped[..., half_size:]
    return jnp.concatenate([first_half * cosine - second_half * sine_val, second_half * cosine + first_half * sine_val], axis=-1)

def block_forward(tokens_f, in_gain, w_in, conv_w, conv_b, a_log, dt_bias, skip_d, ssm_gain, w_out, w_query, w_key, w_value, w_attn_out, ff_gain, w_gate, w_up, w_down, segment, position):
    highest_precision = lax.Precision.HIGHEST
    extent = tokens_f.shape[0]
    width = MH * HD
    normed = low(rms_scale(tokens_f, in_gain))
    mixed_in = low_back(matmul_high(normed, w_in))
    gate_z = mixed_in[:, :width]
    conv_in = mixed_in[:, width:2 * width + 2 * NS]
    raw_step = mixed_in[:, 2 * width + 2 * NS:]
    conv_act, time_step, decay_mat = mixer_front(conv_in, raw_step, conv_w, conv_b, dt_bias, a_log, segment)
    conv_act = low(conv_act)
    x_heads = conv_act[:, :width].reshape(extent, MH, HD)
    b_state = conv_act[:, width:width + NS]
    c_state = conv_act[:, width + NS:]
    inner_bc = low_back(matmul_high(c_state, b_state.T))
    mixer_weights = low(decay_mat * inner_bc[None])
    scaled_x = low(x_heads * time_step[:, :, None])
    scan_out = jnp.einsum('hts,shd->thd', mixer_weights, scaled_x, precision=highest_precision)
    scan_out = low_back(scan_out + skip_d[None, :, None] * x_heads).reshape(extent, width)
    gated = low(rms_scale(scan_out * jax.nn.silu(gate_z), ssm_gain))
    mixer_out = low_back(matmul_high(gated, w_out))
    query = low_back(matmul_high(normed, w_query))
    key_proj = low_back(matmul_high(normed, w_key))
    value_proj = low(low_back(matmul_high(normed, w_value)))
    query_reduced = low(rotate(query, position, QH)).reshape(extent, KVH, QH // KVH, ATTENTION_HEAD)
    key_reduced = low(rotate(key_proj, position, KVH))
    value_reduced = value_proj.reshape(extent, KVH, ATTENTION_HEAD)
    attention_scores = low_back(jnp.einsum('khei,whi->hekw', query_reduced, key_reduced, precision=highest_precision) * ATTENTION_HEAD ** (-0.5))
    attention_scores = jnp.where(causal_allowed(segment), attention_scores, -1e+30)
    row_max = lax.optimization_barrier(jnp.max(attention_scores, axis=-1, keepdims=True))
    exp_scores = jnp.exp(attention_scores - row_max)
    probability_reduced = low(exp_scores / lax.optimization_barrier(jnp.sum(exp_scores, axis=-1, keepdims=True)))
    head_rows_out = jnp.einsum('lwmi,ilu->mlwu', probability_reduced, value_reduced, precision=highest_precision)
    head_rows_out = low(low_back(head_rows_out)).reshape(extent, QH * ATTENTION_HEAD)
    attn_out = low_back(matmul_high(head_rows_out, w_attn_out))
    residual = tokens_f + mixer_out + attn_out
    normed_two = low(rms_scale(residual, ff_gain))
    gate_val = low_back(matmul_high(normed_two, w_gate))
    up_val = low_back(matmul_high(normed_two, w_up))
    hidden = low(jax.nn.silu(gate_val) * up_val)
    feed_out = low_back(matmul_high(hidden, w_down))
    return jnp.where((segment >= 0)[:, None], residual + feed_out, 0.0)

def add_pair(first, second):
    return first + second

def reference(tokens, cotangent, seq_lengths, seq_starts, in_gain, w_in, conv_w, conv_b, a_log, dt_bias, skip_d, ssm_gain, w_out, w_query, w_key, w_value, w_attn_out, ff_gain, w_gate, w_up, w_down):
    params = tuple((p.astype(jnp.float32) for p in (in_gain, w_in, conv_w, conv_b, a_log, dt_bias, skip_d, ssm_gain, w_out, w_query, w_key, w_value, w_attn_out, ff_gain, w_gate, w_up, w_down)))

    def one_block(totals, block_in):
        rows_x, rows_grad, lengths, starts = block_in
        segment, position = layout(lengths, starts, CAP)

        def forward(tokens_f, *weights):
            return block_forward(tokens_f, *weights, segment, position)
        result, pull = jax.vjp(forward, rows_x.astype(jnp.float32), *params)
        grads = pull(rows_grad.astype(jnp.float32))
        totals = jax.tree.map(add_pair, totals, tuple(grads[1:]))
        return (totals, (result.astype(jnp.bfloat16), grads[0].astype(jnp.bfloat16)))
    zeros = tuple((jnp.zeros_like(p) for p in params))
    inputs = (tokens.reshape(NBLOCKS, CAP, D), cotangent.reshape(NBLOCKS, CAP, D), seq_lengths, seq_starts)
    totals, (outputs, input_grads) = lax.scan(one_block, zeros, inputs)
    return (outputs.reshape(TOKENS, D), input_grads.reshape(TOKENS, D), totals[0], totals[1], totals[2], totals[3], totals[4], totals[5], totals[6], totals[7], totals[8], totals[9], totals[10], totals[11], totals[12], totals[13], totals[14], totals[15], totals[16])
```

```python
import jax
import jax.numpy as jnp
from jax import lax
from jax.experimental import pallas as pl
from jax.experimental.pallas import tpu as pltpu
from jax.sharding import PartitionSpec as P

FF = 2048
MH = 24
HD = 64
NS = 128
QH = 8
KVH = 2
ATTENTION_HEAD = 64
CONV_K = 4


EPSILON = 1e-05
ROPE_BASE = 100000000000.0


def matmul_plain(left, right):
    return jnp.dot(left, right, preferred_element_type=jnp.float32)


def matmul_left(left, right):
    return lax.dot_general(
        left, right, (((0,), (0,)), ((), ())), preferred_element_type=jnp.float32
    )


def matmul_right(left, right):
    return lax.dot_general(
        left, right, (((1,), (1,)), ((), ())), preferred_element_type=jnp.float32
    )


def rms_scale(values, gain):
    return values * lax.rsqrt(jnp.mean(values * values, axis=-1, keepdims=True) + EPSILON) * gain


def layout(lengths, starts, extent):
    position = jnp.arange(extent, dtype=jnp.int32)
    inside = (position[:, None] >= starts[None, :]) & (
        position[:, None] < starts[None, :] + lengths[None, :]
    )
    number = jnp.arange(1, lengths.shape[0] + 1, dtype=jnp.int32)
    segment = jnp.sum(jnp.where(inside, number[None, :], 0), axis=1) - 1
    first = jnp.sum(jnp.where(inside, starts[None, :], 0), axis=1)
    return (segment, position - first)


def causal_allowed(segment):
    position = jnp.arange(segment.shape[0], dtype=jnp.int32)
    return (segment[:, None] == segment[None, :]) & (position[:, None] >= position[None, :])


def mixer_front(conv_in, raw_step, conv_w, conv_b, dt_bias, a_log, segment):
    extent = conv_in.shape[0]
    summed = conv_b[None, :] + conv_w[CONV_K - 1][None, :] * conv_in
    for offset in range(1, CONV_K):
        shifted = jnp.concatenate(
            [jnp.zeros((offset, conv_in.shape[1]), conv_in.dtype), conv_in[: extent - offset]],
            axis=0,
        )
        seg_moved = jnp.concatenate(
            [jnp.full((offset,), -2, jnp.int32), segment[: extent - offset]]
        )
        summed = summed + conv_w[CONV_K - 1 - offset][None, :] * jnp.where(
            (seg_moved == segment)[:, None], shifted, 0.0
        )
    conv_act = jax.nn.silu(summed)
    time_step = jax.nn.softplus(raw_step + dt_bias[None, :])
    log_decay = jnp.cumsum(time_step * (-jnp.exp(a_log))[None, :], axis=0).T
    allowed = causal_allowed(segment)[None]
    spread = log_decay[:, :, None] - log_decay[:, None, :]
    decay_mat = jnp.where(allowed, jnp.exp(jnp.where(allowed, spread, 0.0)), 0.0)
    return (conv_act, time_step, decay_mat)


def rotate(values, position, heads):
    half_size = ATTENTION_HEAD // 2
    inverse = ROPE_BASE ** (-jnp.arange(half_size, dtype=jnp.float32) / half_size)
    angle = position.astype(jnp.float32)[:, None] * inverse[None, :]
    cosine = jnp.cos(angle)[:, None, :]
    sine_val = jnp.sin(angle)[:, None, :]
    shaped = values.reshape(values.shape[0], heads, ATTENTION_HEAD)
    first_half = shaped[..., :half_size]
    second_half = shaped[..., half_size:]
    return jnp.concatenate(
        [
            first_half * cosine - second_half * sine_val,
            second_half * cosine + first_half * sine_val,
        ],
        axis=-1,
    )


def gate_norm(scan_out, gate_z, gain):
    return rms_scale(scan_out * jax.nn.silu(gate_z), gain)


def swiglu(gate_val, up_val):
    return jax.nn.silu(gate_val) * up_val


def attention_probs(query_reduced, key_reduced, allowed):
    attention_scores = jnp.einsum(
        "khei,whi->hekw", query_reduced, key_reduced, preferred_element_type=jnp.float32
    ) * ATTENTION_HEAD ** (-0.5)
    attention_scores = jnp.where(allowed, attention_scores, -1e30)
    row_max = jnp.max(attention_scores, axis=-1, keepdims=True)
    exp_scores = jnp.exp(attention_scores - row_max)
    return exp_scores / jnp.sum(exp_scores, axis=-1, keepdims=True)


def join_rows(gated, heads, parts):
    extent = gated.shape[0]
    return jnp.concatenate(
        [gated.reshape(extent, parts, -1), heads.reshape(extent, parts, -1)], axis=2
    ).reshape(extent, -1)


def split_rows(joined, parts):
    extent = joined.shape[0]
    shaped = joined.reshape(extent, parts, -1)
    cut = MH * HD // parts
    return shaped[:, :, :cut].reshape(extent, -1), shaped[:, :, cut:].reshape(extent, -1)


def forward_pass(tokens_f, gains, mats, a_log, dt_bias, skip_d, segment, position, parts):
    in_gain, conv_w, conv_b, ssm_gain, ff_gain, w_raw = gains
    w_conv, w_z, w_qkv, w_cat, w_gate, w_up, w_down = mats
    extent = tokens_f.shape[0]
    width = MH * HD
    q_cols = QH * ATTENTION_HEAD
    k_cols = KVH * ATTENTION_HEAD
    normed_f, pull_norm_one = jax.vjp(rms_scale, tokens_f, in_gain.astype(jnp.float32))
    normed = normed_f.astype(jnp.bfloat16)
    conv_in = matmul_plain(normed, w_conv)
    raw_step = matmul_right(normed, w_raw)

    def front(conv_value, step_value, tap_value, bias_value, shift_value, rate_value):
        return mixer_front(
            conv_value, step_value, tap_value, bias_value, shift_value, rate_value, segment
        )

    (conv_act, time_step, decay_mat), pull_front = jax.vjp(
        front,
        conv_in,
        raw_step,
        conv_w.astype(jnp.float32),
        conv_b.astype(jnp.float32),
        dt_bias,
        a_log,
    )
    act_low = conv_act.astype(jnp.bfloat16)
    x_heads = act_low[:, :width].reshape(extent, MH, HD)
    b_state = act_low[:, width : width + NS]
    c_state = act_low[:, width + NS :]
    inner_bc = matmul_right(c_state, b_state)
    mixer_weights = (decay_mat * inner_bc[None]).astype(jnp.bfloat16)
    scaled_x = (x_heads.astype(jnp.float32) * time_step[:, :, None]).astype(jnp.bfloat16)
    scan_out = jnp.einsum(
        "hts,shd->thd", mixer_weights, scaled_x, preferred_element_type=jnp.float32
    )
    scan_out = (scan_out + skip_d[None, :, None] * x_heads.astype(jnp.float32)).reshape(
        extent, width
    )
    gate_z = matmul_plain(normed, w_z)
    gated_f, pull_gate = jax.vjp(gate_norm, scan_out, gate_z, ssm_gain.astype(jnp.float32))
    gated = gated_f.astype(jnp.bfloat16)
    qkv = matmul_plain(normed, w_qkv)
    query = qkv[:, :q_cols]
    key_proj = qkv[:, q_cols : q_cols + k_cols]
    value_proj = qkv[:, q_cols + k_cols :]

    def turn(query_value, key_value):
        return (rotate(query_value, position, QH), rotate(key_value, position, KVH))

    (q_rot, k_rot), pull_rotate = jax.vjp(turn, query, key_proj)
    query_reduced = q_rot.astype(jnp.bfloat16).reshape(extent, KVH, QH // KVH, ATTENTION_HEAD)
    key_reduced = k_rot.astype(jnp.bfloat16)
    value_reduced = value_proj.astype(jnp.bfloat16).reshape(extent, KVH, ATTENTION_HEAD)
    prob_all = attention_probs(query_reduced, key_reduced, causal_allowed(segment))
    probability_reduced = prob_all.astype(jnp.bfloat16)
    head_rows_out = jnp.einsum(
        "lwmi,ilu->mlwu", probability_reduced, value_reduced, preferred_element_type=jnp.float32
    )
    head_rows_out = head_rows_out.astype(jnp.bfloat16).reshape(extent, QH * ATTENTION_HEAD)
    joined = join_rows(gated, head_rows_out, parts)
    residual = tokens_f + matmul_plain(joined, w_cat)
    normed_two_f, pull_norm_two = jax.vjp(rms_scale, residual, ff_gain.astype(jnp.float32))
    normed_two = normed_two_f.astype(jnp.bfloat16)
    gate_val = matmul_plain(normed_two, w_gate)
    up_val = matmul_plain(normed_two, w_up)
    hidden_f, pull_swiglu = jax.vjp(swiglu, gate_val, up_val)
    hidden = hidden_f.astype(jnp.bfloat16)
    feed_out = matmul_plain(hidden, w_down)
    valid_mask = (segment >= 0)[:, None]
    result = jnp.where(valid_mask, residual + feed_out, 0.0).astype(jnp.bfloat16)
    kept = (
        pull_norm_one,
        normed,
        pull_front,
        x_heads,
        b_state,
        c_state,
        inner_bc,
        decay_mat,
        mixer_weights,
        scaled_x,
        time_step,
        pull_gate,
        joined,
        pull_rotate,
        query_reduced,
        key_reduced,
        value_reduced,
        prob_all,
        probability_reduced,
        pull_norm_two,
        normed_two,
        pull_swiglu,
        hidden,
        valid_mask,
    )
    return (result, kept)


def backward_pass(cotangent, w_raw, mats, skip_d, kept, parts):
    w_conv, w_z, w_qkv, w_cat, w_gate, w_up, w_down = mats
    (
        pull_norm_one,
        normed,
        pull_front,
        x_heads,
        b_state,
        c_state,
        inner_bc,
        decay_mat,
        mixer_weights,
        scaled_x,
        time_step,
        pull_gate,
        joined,
        pull_rotate,
        query_reduced,
        key_reduced,
        value_reduced,
        prob_all,
        probability_reduced,
        pull_norm_two,
        normed_two,
        pull_swiglu,
        hidden,
        valid_mask,
    ) = kept
    extent = cotangent.shape[0]
    out_grad = jnp.where(valid_mask, cotangent.astype(jnp.float32), 0.0)
    feed_grad = out_grad.astype(jnp.bfloat16)
    hidden_grad = matmul_right(feed_grad, w_down)
    gate_grad, up_grad = pull_swiglu(hidden_grad)
    gate_low = gate_grad.astype(jnp.bfloat16)
    up_low = up_grad.astype(jnp.bfloat16)
    normed_two_grad = matmul_right(gate_low, w_gate) + matmul_right(up_low, w_up)
    residual_part, grad_ff_gain = pull_norm_two(normed_two_grad)
    residual_grad = out_grad + residual_part
    branch_grad = residual_grad.astype(jnp.bfloat16)
    gated_grad, heads_grad = split_rows(matmul_right(branch_grad, w_cat), parts)
    head_rows_grad = heads_grad.astype(jnp.bfloat16).reshape(
        extent, KVH, QH // KVH, ATTENTION_HEAD
    )
    probability_grad = jnp.einsum(
        "khei,whi->hekw", head_rows_grad, value_reduced, preferred_element_type=jnp.float32
    )
    value_grad = jnp.einsum(
        "muhi,hmuy->imy", probability_reduced, head_rows_grad, preferred_element_type=jnp.float32
    )
    scores_gradient = prob_all * (
        probability_grad - jnp.sum(prob_all * probability_grad, axis=-1, keepdims=True)
    )
    scores_gradient = scores_gradient.astype(jnp.bfloat16)
    q_rot_grad = jnp.einsum(
        "lwmi,ilu->mlwu", scores_gradient, key_reduced, preferred_element_type=jnp.float32
    ) * ATTENTION_HEAD ** (-0.5)
    k_rot_grad = jnp.einsum(
        "muhi,hmuy->imy", scores_gradient, query_reduced, preferred_element_type=jnp.float32
    ) * ATTENTION_HEAD ** (-0.5)
    query_grad, key_grad = pull_rotate((q_rot_grad.reshape(extent, QH, ATTENTION_HEAD), k_rot_grad))
    query_low = query_grad.astype(jnp.bfloat16)
    key_low = key_grad.astype(jnp.bfloat16)
    value_low = value_grad.reshape(extent, KVH * ATTENTION_HEAD).astype(jnp.bfloat16)
    qkv_low = jnp.concatenate([query_low, key_low, value_low], axis=1)
    normed_grad = matmul_right(qkv_low, w_qkv)
    scan_grad, gate_z_grad, grad_ssm_gain = pull_gate(gated_grad)
    scan_low = scan_grad.astype(jnp.bfloat16).reshape(extent, MH, HD)
    weight_grad = jnp.einsum("thd,shd->hts", scan_low, scaled_x, preferred_element_type=jnp.float32)
    scaled_grad = jnp.einsum(
        "hts,thd->shd", mixer_weights, scan_low, preferred_element_type=jnp.float32
    )
    inner_low = jnp.sum(weight_grad * decay_mat, axis=0).astype(jnp.bfloat16)
    decay_grad = weight_grad * inner_bc[None]
    c_grad = matmul_plain(inner_low, b_state)
    b_grad = matmul_left(inner_low, c_state)
    heads_f = x_heads.astype(jnp.float32)
    scan_f = scan_low.astype(jnp.float32)
    x_grad = scaled_grad * time_step[:, :, None] + skip_d[None, :, None] * scan_f
    step_grad = jnp.sum(scaled_grad * heads_f, axis=2)
    grad_skip = jnp.sum(scan_f * heads_f, axis=(0, 2))
    act_grad = jnp.concatenate([x_grad.reshape(extent, MH * HD), b_grad, c_grad], axis=1)
    conv_grad, raw_grad, grad_conv_w, grad_conv_b, grad_dt_bias, grad_a_log = pull_front(
        (act_grad, step_grad, decay_grad)
    )
    z_low = gate_z_grad.astype(jnp.bfloat16)
    conv_low = conv_grad.astype(jnp.bfloat16)
    raw_low = raw_grad.astype(jnp.bfloat16)
    normed_grad = (
        normed_grad
        + matmul_right(z_low, w_z)
        + matmul_right(conv_low, w_conv)
        + matmul_plain(raw_low, w_raw)
    )
    token_part, grad_in_gain = pull_norm_one(normed_grad)
    tokens_grad = (residual_grad + token_part).astype(jnp.bfloat16)
    raw_rows = matmul_left(raw_low, normed)
    pairs = (
        (hidden, feed_grad),
        (normed_two, jnp.concatenate([gate_low, up_low], axis=1)),
        (joined, branch_grad),
        (normed, jnp.concatenate([z_low, query_low], axis=1)),
        (normed, jnp.concatenate([conv_low, key_low, value_low], axis=1)),
    )
    small = (
        grad_in_gain,
        grad_conv_w,
        grad_conv_b,
        grad_ssm_gain,
        grad_ff_gain,
        raw_rows,
        grad_a_log,
        grad_dt_bias,
        grad_skip,
    )
    return (tokens_grad, pairs, small)


AXES = ("shard", "replica")


def place(pieces, positions, dim, count):
    shape = list(pieces[0].shape)
    shape[dim] = count
    total = len(pieces)

    def body(where, *refs):
        out, sems = refs[total], refs[total + 1]
        copies = []
        for number in range(total):
            spot = (slice(None),) * dim + (pl.ds(where[number], 1),)
            copies.append(
                pltpu.make_async_copy(refs[number], out.at[spot], sems.at[number])
            )
        for copy in copies:
            copy.start()
        for copy in copies:
            copy.wait()

    moved = 2 * sum(piece.size * piece.dtype.itemsize for piece in pieces)
    return pl.pallas_call(
        body,
        out_shape=jax.ShapeDtypeStruct(tuple(shape), pieces[0].dtype),
        in_specs=[pl.BlockSpec(memory_space=pltpu.SMEM)]
        + [pl.BlockSpec(memory_space=pl.ANY)] * total,
        out_specs=pl.BlockSpec(memory_space=pl.ANY),
        scratch_shapes=[pltpu.SemaphoreType.DMA((total,))],
        cost_estimate=pl.CostEstimate(flops=0, bytes_accessed=moved, transcendentals=0),
        name="place",
    )(jnp.stack(positions).astype(jnp.int32), *pieces)


class Links:
    def __init__(self, shards_of, copies):
        self.z_size = shards_of // 2
        shard = lax.axis_index("shard")
        replica = lax.axis_index("replica")
        self.z, self.x = shard // 2, shard % 2
        self.y, self.c = replica // 2, replica % 2
        everyone = [(s, r) for s in range(shards_of) for r in range(copies)]

        def table(step):
            return [(s * copies + r, step(s, r)) for s, r in everyone]

        self.tables = {
            "x": table(lambda s, r: (s ^ 1) * copies + r),
            "y": table(lambda s, r: s * copies + (r ^ 2)),
            "c": table(lambda s, r: s * copies + (r ^ 1)),
            "z": table(lambda s, r: ((s + 2) % shards_of) * copies + r),
        }

    def send(self, value, axis):
        return lax.ppermute(value, AXES, self.tables[axis])

    def spread(self, value, axis):
        if axis == "z":
            pieces, spots = [value], [self.z]
            for step in range(1, self.z_size):
                pieces.append(self.send(pieces[-1], "z"))
                spots.append((self.z + self.z_size - step) % self.z_size)
            return place(pieces, spots, 0, self.z_size)
        spot = {"x": self.x, "y": self.y, "c": self.c}[axis]
        return place([value, self.send(value, axis)], [spot, 1 - spot], "zxyc".index(axis), 2)

    def gather(self, own, order):
        rows, columns = own.shape
        cut = own.reshape(1, 1, 2, 2, rows // 4, columns)
        cut = lax.dynamic_slice_in_dim(cut, self.c, 1, 3)
        if "y" in order:
            cut = lax.dynamic_slice_in_dim(cut, self.y, 1, 2)
        for axis in order:
            cut = self.spread(cut, axis)
        return cut.reshape(-1, columns)

    def gather_small(self, own):
        other = self.send(own, "x")
        pair = jnp.stack(
            [jnp.where(self.x == 0, own, other), jnp.where(self.x == 0, other, own)]
        )
        pieces = [pair]
        for _ in range(1, self.z_size):
            pieces.append(self.send(pieces[-1], "z"))
        stacked = jnp.stack(pieces)
        return jnp.concatenate(
            [
                lax.dynamic_index_in_dim(stacked, (self.z + self.z_size - at) % self.z_size, 0, False)
                for at in range(self.z_size)
            ]
        )

    def share_rows(self, left):
        tokens, width = left.shape
        rows = width // (2 * self.z_size)
        halves = left.reshape(tokens, self.z_size, 2, rows).transpose(2, 0, 1, 3)
        halves = halves.reshape(2, tokens, self.z_size * rows)
        for axis in "yc":
            halves = jnp.concatenate([halves, self.send(halves, axis)], axis=1)
        return halves

    def share_columns(self, right):
        for axis, spot in (("y", self.y), ("c", self.c)):
            tokens, columns = right.shape
            halves = jnp.stack([right[:, : columns // 2], right[:, columns // 2 :]])
            mine = lax.dynamic_index_in_dim(halves, spot, 0, False)
            theirs = lax.dynamic_index_in_dim(halves, 1 - spot, 0, False)
            right = jnp.concatenate([mine, self.send(theirs, axis)], axis=0)
        return right

    def reduce(self, halves, right):
        theirs = lax.dynamic_index_in_dim(halves, 1 - self.x, 0, False)
        mine = lax.dynamic_index_in_dim(halves, self.x, 0, False)
        moved = self.send(matmul_left(theirs, right).astype(jnp.bfloat16), "x")
        partial = (matmul_left(mine, right) + moved.astype(jnp.float32)).astype(jnp.bfloat16)
        partial = partial.reshape(self.z_size, -1, partial.shape[1])

        def block(step):
            at = (self.z + 2 * self.z_size - 1 - step) % self.z_size
            return lax.dynamic_index_in_dim(partial, at, 0, False)

        total = block(0)
        for step in range(1, self.z_size):
            arrived = self.send(total, "z")
            total = (arrived.astype(jnp.float32) + block(step).astype(jnp.float32)).astype(
                jnp.bfloat16
            )
        by_y = self.send(total, "y")
        by_c = self.send(total, "c")
        by_yc = self.send(by_y, "c")
        first_y, first_c = self.y == 0, self.c == 0
        near = (jnp.where(first_c, total, by_c), jnp.where(first_c, by_c, total))
        far = (jnp.where(first_c, by_y, by_yc), jnp.where(first_c, by_yc, by_y))
        quarters = [jnp.where(first_y, a, b) for a, b in zip(near, far)] + [
            jnp.where(first_y, b, a) for a, b in zip(near, far)
        ]
        return jnp.concatenate([part.astype(jnp.float32) for part in quarters], axis=1)


def pack_small(in_gain, conv_w, conv_b, ssm_gain, ff_gain, raw):
    def rows(value):
        flat = value.reshape(-1)
        return jnp.pad(flat, (0, -flat.shape[0] % 128)).reshape(-1, 128)

    packed = jnp.concatenate([rows(v) for v in (raw.T, in_gain, conv_w, conv_b, ssm_gain, ff_gain)])
    return jnp.pad(packed, ((0, -packed.shape[0] % 16), (0, 0)))


def unpack_small(gathered, own):
    in_gain, conv_w, conv_b, ssm_gain, ff_gain, raw = own
    parts = gathered.shape[0]
    at = 0
    out = []
    for value in (raw.T, in_gain, conv_w, conv_b, ssm_gain, ff_gain):
        count = -(-value.size // 128)
        flat = gathered[:, at : at + count].reshape(parts, -1)[:, : value.size]
        at += count
        shaped = flat.reshape((parts,) + value.shape)
        if value.ndim == 1:
            out.append(shaped.reshape(-1))
        else:
            out.append(shaped.transpose(1, 0, 2).reshape(value.shape[0], -1))
    return tuple(out[1:]) + (out[0],)


def shards(
    copies,
    tokens,
    cotangent,
    seq_lengths,
    seq_starts,
    in_gain,
    w_in,
    conv_w,
    conv_b,
    a_log,
    dt_bias,
    skip_d,
    ssm_gain,
    w_out,
    w_query,
    w_key,
    w_value,
    w_attn_out,
    ff_gain,
    w_gate,
    w_up,
    w_down,
):
    parts = MH * HD // w_out.shape[0]
    width = MH * HD
    channels = width + 2 * NS
    quick = parts == 8 and copies == 4
    links = Links(parts, copies)
    own_small = (in_gain, conv_w, conv_b, ssm_gain, ff_gain, w_in[:, width + channels :])
    own = (
        w_in[:, width : width + channels],
        w_in[:, :width],
        jnp.concatenate([w_query, w_key, w_value], axis=1),
        jnp.concatenate([w_out, w_attn_out], axis=0),
        w_gate,
        w_up,
        w_down,
    )
    if quick:
        orders = ("zxyc", "zyxc", "xzc", "xzc", "zxyc", "zyxc", "zyxc")
        small_all = links.gather_small(pack_small(*own_small))
        mats = tuple(links.gather(value, order) for value, order in zip(own, orders))
    else:
        small_all = lax.all_gather(pack_small(*own_small), "shard", axis=0)
        mats = tuple(lax.all_gather(value, "shard", axis=0, tiled=True) for value in own)
    gains = unpack_small(small_all, own_small)
    segment, position = layout(seq_lengths[0], seq_starts[0], tokens.shape[0])
    result, kept = forward_pass(
        tokens.astype(jnp.float32), gains, mats, a_log, dt_bias, skip_d, segment, position, parts
    )
    tokens_grad, pairs, small = backward_pass(cotangent, gains[5], mats, skip_d, kept, parts)
    if quick:
        shared = {}
        summed = []
        for left, right in pairs:
            if id(left) not in shared:
                shared[id(left)] = links.share_rows(left)
            summed.append(links.reduce(shared[id(left)], links.share_columns(right)))
    else:
        summed = []
        for left, right in pairs:
            share = lax.psum_scatter(
                matmul_left(left, right).astype(jnp.bfloat16),
                "shard",
                scatter_dimension=0,
                tiled=True,
            )
            summed.append(lax.psum(share, "replica").astype(jnp.float32))
    down, feed, joined, first, second = summed
    flat = jnp.concatenate([value.reshape(-1) for value in small])
    flat = jnp.pad(flat, (0, -flat.shape[0] % 1024)).reshape(-1, 128)
    flat = lax.psum(flat, AXES).reshape(-1)
    totals = []
    at = 0
    for value in small:
        totals.append(flat[at : at + value.size].reshape(value.shape))
        at += value.size
    here = lax.axis_index("shard")

    def mine(value):
        size = value.shape[-1] // parts
        return lax.dynamic_slice_in_dim(value, here * size, size, value.ndim - 1)

    q_cols = QH * ATTENTION_HEAD
    k_cols = KVH * ATTENTION_HEAD
    out_rows = width // parts
    return (
        result,
        tokens_grad,
        mine(totals[0]),
        jnp.concatenate([first[:, :width], second[:, :channels], mine(totals[5]).T], axis=1),
        mine(totals[1]),
        mine(totals[2]),
        totals[6],
        totals[7],
        totals[8],
        mine(totals[3]),
        joined[:out_rows],
        first[:, width : width + q_cols],
        second[:, channels : channels + k_cols],
        second[:, channels + k_cols :],
        joined[out_rows:],
        mine(totals[4]),
        feed[:, :FF],
        feed[:, FF:],
        down,
    )


def solution(mesh):
    in_specs = (
        P(("shard", "replica"), None),
        P(("shard", "replica"), None),
        P(("shard", "replica"), None),
        P(("shard", "replica"), None),
        P("shard"),
        P("shard", None),
        P(None, "shard"),
        P("shard"),
        P(),
        P(),
        P(),
        P("shard"),
        P("shard", None),
        P("shard", None),
        P("shard", None),
        P("shard", None),
        P("shard", None),
        P("shard"),
        P("shard", None),
        P("shard", None),
        P("shard", None),
    )
    out_specs = (
        P(("shard", "replica"), None),
        P(("shard", "replica"), None),
        P("shard"),
        P("shard", None),
        P(None, "shard"),
        P("shard"),
        P(),
        P(),
        P(),
        P("shard"),
        P("shard", None),
        P("shard", None),
        P("shard", None),
        P("shard", None),
        P("shard", None),
        P("shard"),
        P("shard", None),
        P("shard", None),
        P("shard", None),
    )

    def local(*args):
        return shards(mesh.shape["replica"], *args)

    return jax.shard_map(local, mesh=mesh, in_specs=in_specs, out_specs=out_specs, check_vma=False)
```

```python
import jax
import jax.numpy as jnp
from jax import lax
from jax.experimental import pallas as pl
from jax.experimental.pallas import tpu as pltpu
from jax.sharding import PartitionSpec as P

FF = 2048
MH = 24
HD = 64
NS = 128
QH = 8
KVH = 2
ATTENTION_HEAD = 64
CONV_K = 4
MIXED = 2 * MH * HD + 2 * NS + (QH + 2 * KVH) * ATTENTION_HEAD
BLOCK = 1024


EPSILON = 1e-05
ROPE_BASE = 100000000000.0


def matmul_plain(left, right):
    return jnp.dot(left, right, preferred_element_type=jnp.float32)


def matmul_left(left, right):
    return lax.dot_general(
        left, right, (((0,), (0,)), ((), ())), preferred_element_type=jnp.float32
    )


def matmul_right(left, right):
    return lax.dot_general(
        left, right, (((1,), (1,)), ((), ())), preferred_element_type=jnp.float32
    )


def rms_scale(values, gain):
    return values * lax.rsqrt(jnp.mean(values * values, axis=-1, keepdims=True) + EPSILON) * gain


def layout(lengths, starts, extent):
    position = jnp.arange(extent, dtype=jnp.int32)
    inside = (position[:, None] >= starts[None, :]) & (
        position[:, None] < starts[None, :] + lengths[None, :]
    )
    number = jnp.arange(1, lengths.shape[0] + 1, dtype=jnp.int32)
    segment = jnp.sum(jnp.where(inside, number[None, :], 0), axis=1) - 1
    first = jnp.sum(jnp.where(inside, starts[None, :], 0), axis=1)
    return (segment, position - first)


def causal_allowed(segment):
    position = jnp.arange(segment.shape[0], dtype=jnp.int32)
    return (segment[:, None] == segment[None, :]) & (position[:, None] >= position[None, :])


def swiglu(gate_val, up_val):
    return jax.nn.silu(gate_val) * up_val


def sigmoid(value):
    return 1.0 / (1.0 + jnp.exp(-value))


def dot_exact(left, right, dims):
    return lax.dot_general(
        left,
        right,
        (dims, ((), ())),
        precision=lax.Precision.HIGHEST,
        preferred_element_type=jnp.float32,
    )


def lane_half(rows):
    return lax.broadcasted_iota(jnp.int32, (rows, 2 * HD), 1) < HD


def pick(half, first, second):
    return jnp.where(half, first, second)


def call_whole(body, outs, args, flops, scratch=(), name="kernel"):
    moved = sum(arg.size * arg.dtype.itemsize for arg in args)
    moved += sum(out.size * out.dtype.itemsize for out in outs)
    return pl.pallas_call(
        body,
        out_shape=outs,
        in_specs=[
            pl.BlockSpec(memory_space=pltpu.SMEM if arg.dtype == jnp.int32 else pltpu.VMEM)
            for arg in args
        ],
        out_specs=[pl.BlockSpec(memory_space=pltpu.VMEM)] * len(outs),
        scratch_shapes=list(scratch),
        compiler_params=pltpu.CompilerParams(vmem_limit_bytes=40 * 1024 * 1024),
        cost_estimate=pl.CostEstimate(flops=flops, bytes_accessed=moved, transcendentals=0),
        name=name,
    )(*args)


def shape(dims, kind=jnp.float32):
    return jax.ShapeDtypeStruct(dims, kind)


def turned(values, cosine, sine, back):
    width = values.shape[1]
    quarter = lax.broadcasted_iota(jnp.int32, values.shape, 1) % ATTENTION_HEAD
    half = ATTENTION_HEAD // 2
    swapped = jnp.where(
        quarter < half,
        -pltpu.roll(values, width - half, 1),
        pltpu.roll(values, half, 1),
    )
    return values * cosine - swapped * sine if back else values * cosine + swapped * sine


def doubled(values, half):
    moved = pltpu.roll(values, ATTENTION_HEAD, 1)
    return (pick(half, values, moved), pick(half, moved, values))


def masked_dot(pair, half, keep_first, other):
    zero = jnp.zeros_like(pair)
    chosen = jnp.where(half, pair, zero) if keep_first else jnp.where(half, zero, pair)
    return matmul_right(chosen, other)


def softmax_rows(scores, allowed):
    scores = jnp.where(allowed, scores * ATTENTION_HEAD ** (-0.5), -1e30)
    raised = jnp.exp(scores - jnp.max(scores, axis=-1, keepdims=True))
    return raised / jnp.sum(raised, axis=-1, keepdims=True)


def attention_front(qkv, cosine, sine, allowed):
    extent = qkv.shape[0]
    pair = 2 * ATTENTION_HEAD
    pairs = QH // 2

    def body(qkv_ref, cos_ref, sin_ref, allowed_ref, low_ref, out_ref):
        half = lane_half(extent)
        can = allowed_ref[...] > 0.0
        cos_val, sin_val = cos_ref[...], sin_ref[...]
        key = turned(qkv_ref[:, pairs * pair : (pairs + 1) * pair], cos_val, sin_val, False)
        key = key.astype(jnp.bfloat16)
        value = qkv_ref[:, (pairs + 1) * pair :].astype(jnp.bfloat16)
        low_ref[:, pairs * pair : (pairs + 1) * pair] = key
        low_ref[:, (pairs + 1) * pair :] = value
        keys = [k.astype(jnp.bfloat16) for k in doubled(key.astype(jnp.float32), half)]
        values = [v.astype(jnp.bfloat16) for v in doubled(value.astype(jnp.float32), half)]
        for number in range(pairs):
            spot = slice(number * pair, (number + 1) * pair)
            query = turned(qkv_ref[:, spot], cos_val, sin_val, False).astype(jnp.bfloat16)
            low_ref[:, spot] = query
            group = number * KVH // pairs
            results = []
            for first in (True, False):
                scores = masked_dot(query, half, first, keys[group])
                probs = softmax_rows(scores, can).astype(jnp.bfloat16)
                results.append(matmul_plain(probs, values[group]))
            out_ref[:, spot] = pick(half, *results).astype(jnp.bfloat16)

    return call_whole(
        body,
        (shape(qkv.shape, jnp.bfloat16), shape((extent, pairs * pair), jnp.bfloat16)),
        (qkv, cosine, sine, allowed),
        QH * 8 * extent**3,
        name="attention_front",
    )


def attention_back(low, heads_grad, cosine, sine, allowed):
    extent = low.shape[0]
    pair = 2 * ATTENTION_HEAD
    pairs = QH // 2
    scale = ATTENTION_HEAD ** (-0.5)

    def body(low_ref, grad_ref, cos_ref, sin_ref, allowed_ref, out_ref):
        half = lane_half(extent)
        can = allowed_ref[...] > 0.0
        cos_val, sin_val = cos_ref[...], sin_ref[...]
        key = low_ref[:, pairs * pair : (pairs + 1) * pair].astype(jnp.float32)
        value = low_ref[:, (pairs + 1) * pair :].astype(jnp.float32)
        keys = [k.astype(jnp.bfloat16) for k in doubled(key, half)]
        values = [v.astype(jnp.bfloat16) for v in doubled(value, half)]
        key_sums = [jnp.zeros((extent, pair), jnp.float32) for _ in range(KVH)]
        value_sums = [jnp.zeros((extent, pair), jnp.float32) for _ in range(KVH)]
        for number in range(pairs):
            spot = slice(number * pair, (number + 1) * pair)
            query = low_ref[:, spot]
            grad = grad_ref[:, spot]
            group = number * KVH // pairs
            q_parts, k_parts, v_parts = [], [], []
            for first in (True, False):
                probs = softmax_rows(masked_dot(query, half, first, keys[group]), can)
                prob_grad = masked_dot(grad, half, first, values[group])
                v_parts.append(matmul_left(probs.astype(jnp.bfloat16), grad))
                inner = jnp.sum(probs * prob_grad, axis=-1, keepdims=True)
                score_grad = (probs * (prob_grad - inner)).astype(jnp.bfloat16)
                q_parts.append(matmul_plain(score_grad, keys[group]))
                k_parts.append(matmul_left(score_grad, query))
            key_sums[group] = key_sums[group] + pick(half, *k_parts)
            value_sums[group] = value_sums[group] + pick(half, *v_parts)
            query_grad = turned(pick(half, *q_parts) * scale, cos_val, sin_val, True)
            out_ref[:, spot] = query_grad.astype(jnp.bfloat16)

        def both(sums):
            return pick(half, *[s + pltpu.roll(s, ATTENTION_HEAD, 1) for s in sums])

        key_grad = turned(both(key_sums) * scale, cos_val, sin_val, True)
        out_ref[:, pairs * pair : (pairs + 1) * pair] = key_grad.astype(jnp.bfloat16)
        out_ref[:, (pairs + 1) * pair :] = both(value_sums).astype(jnp.bfloat16)

    (out,) = call_whole(
        body,
        (shape(low.shape, jnp.bfloat16),),
        (low, heads_grad, cosine, sine, allowed),
        QH * 14 * extent**3,
        name="attention_back",
    )
    return out


def conv_sum(conv_ref, taps_ref, bias_ref, moves_ref, spot):
    value = conv_ref[:, spot]
    total = bias_ref[:, spot] + taps_ref[CONV_K - 1 : CONV_K, spot] * value
    for offset in range(1, CONV_K):
        moved = pltpu.roll(value, offset, 0) * moves_ref[:, offset : offset + 1]
        total = total + taps_ref[CONV_K - 1 - offset : CONV_K - offset, spot] * moved
    return total


def steps_of(raw_ref, shift_ref, rate_ref):
    moved = raw_ref[...] + shift_ref[...]
    step = jnp.maximum(moved, 0.0) + jnp.log1p(jnp.exp(-jnp.abs(moved)))
    rate = -jnp.exp(rate_ref[...])
    return moved, step, rate


def decay_sums(decay, extent):
    row = lax.broadcasted_iota(jnp.int32, (extent, extent), 0)
    column = lax.broadcasted_iota(jnp.int32, (extent, extent), 1)
    lower = jnp.where(row >= column, 1.0, 0.0)
    by_column = dot_exact(lower, decay, ((1,), (0,)))
    by_row = dot_exact(decay, lower, ((0,), (1,)))
    return by_column, by_row, lower


def decay_of(by_column, by_row, head, can):
    spread = by_column[:, head : head + 1] - by_row[head : head + 1, :]
    return jnp.where(can, jnp.exp(jnp.where(can, spread, 0.0)), 0.0)


def mixer_front(conv_in, raw_step, gate_z, taps, bias, shift, rate, skip, gain, moves, allowed):
    extent = conv_in.shape[0]
    width = MH * HD
    pair = 2 * HD

    def body(
        conv_ref,
        raw_ref,
        gate_ref,
        taps_ref,
        bias_ref,
        shift_ref,
        rate_ref,
        skip_ref,
        gain_ref,
        moves_ref,
        allowed_ref,
        act_ref,
        scan_ref,
        gated_ref,
    ):
        half = lane_half(extent)
        can = allowed_ref[...] > 0.0
        for at in range(0, width + 2 * NS, 256):
            spot = slice(at, at + 256)
            total = conv_sum(conv_ref, taps_ref, bias_ref, moves_ref, spot)
            act_ref[:, spot] = (total * sigmoid(total)).astype(jnp.bfloat16)
        _, step, step_rate = steps_of(raw_ref, shift_ref, rate_ref)
        by_column, by_row, _ = decay_sums(step * step_rate, extent)
        inner = matmul_right(act_ref[:, width + NS :], act_ref[:, width : width + NS])
        squares = jnp.zeros((extent, 1), jnp.float32)
        for number in range(MH // 2):
            spot = slice(number * pair, (number + 1) * pair)
            heads = act_ref[:, spot].astype(jnp.float32)
            steps = pick(half, step[:, 2 * number : 2 * number + 1], step[:, 2 * number + 1 : 2 * number + 2])
            scaled = (heads * steps).astype(jnp.bfloat16)
            results = []
            for head in (2 * number, 2 * number + 1):
                weights = (decay_of(by_column, by_row, head, can) * inner).astype(jnp.bfloat16)
                results.append(matmul_plain(weights, scaled))
            scan = pick(half, *results) + skip_ref[:, spot] * heads
            scan_ref[:, spot] = scan
            gate = gate_ref[:, spot]
            value = scan * (gate * sigmoid(gate))
            squares = squares + jnp.sum(value * value, axis=-1, keepdims=True)
        scale = lax.rsqrt(squares / width + EPSILON)
        for number in range(MH // 2):
            spot = slice(number * pair, (number + 1) * pair)
            gate = gate_ref[:, spot]
            value = scan_ref[:, spot] * (gate * sigmoid(gate))
            gated_ref[:, spot] = (value * scale * gain_ref[:, spot]).astype(jnp.bfloat16)

    return call_whole(
        body,
        (
            shape((extent, width + 2 * NS), jnp.bfloat16),
            shape((extent, width)),
            shape((extent, width), jnp.bfloat16),
        ),
        (conv_in, raw_step, gate_z, taps, bias, shift, rate, skip, gain, moves, allowed),
        MH * 16 * extent**3,
        name="mixer_front",
    )


def mixed_columns(z_ref, low_ref, qkv_ref, at):
    for ref in (z_ref, low_ref, qkv_ref):
        if at < ref.shape[1]:
            return ref[:, at : at + 256]
        at -= ref.shape[1]


def mixer_back(
    side,
    qkv_low,
    gated_grad,
    scan,
    act,
    conv_in,
    raw_step,
    gate_z,
    taps,
    bias,
    shift,
    rate,
    skip,
    gain,
    moves,
    allowed,
):
    extent = conv_in.shape[0]
    width = MH * HD
    channels = width + 2 * NS
    pair = 2 * HD

    def body(
        side_ref,
        qkv_ref,
        grad_ref,
        scan_ref,
        act_ref,
        conv_ref,
        raw_ref,
        gate_ref,
        taps_ref,
        bias_ref,
        shift_ref,
        rate_ref,
        skip_ref,
        gain_ref,
        moves_ref,
        allowed_ref,
        z_ref,
        low_ref,
        raw_low_ref,
        mine_ref,
        theirs_ref,
        gain_out,
        taps_out,
        bias_out,
        skip_out,
        shift_out,
        rate_out,
        scan_grad_ref,
        act_grad_ref,
        row_ref,
    ):
        half = lane_half(extent)
        can = allowed_ref[...] > 0.0
        squares = jnp.zeros((extent, 1), jnp.float32)
        dots = jnp.zeros((extent, 1), jnp.float32)
        for at in range(0, width, 256):
            spot = slice(at, at + 256)
            gate = gate_ref[:, spot]
            value = scan_ref[:, spot] * (gate * sigmoid(gate))
            squares = squares + jnp.sum(value * value, axis=-1, keepdims=True)
            dots = dots + jnp.sum(value * gain_ref[:, spot] * grad_ref[:, spot], axis=-1, keepdims=True)
        scale = lax.rsqrt(squares / width + EPSILON)
        common = scale * scale * scale * (dots / width)
        for at in range(0, width, 256):
            spot = slice(at, at + 256)
            gate = gate_ref[:, spot]
            sig = sigmoid(gate)
            silu = gate * sig
            scanned = scan_ref[:, spot]
            value = scanned * silu
            grad = grad_ref[:, spot]
            gain_out[:, spot] = jnp.sum(grad * value * scale, axis=0, keepdims=True)
            value_grad = scale * (gain_ref[:, spot] * grad) - value * common
            z_ref[:, spot] = (value_grad * scanned * (sig * (1.0 + gate * (1.0 - sig)))).astype(
                jnp.bfloat16
            )
            scan_grad_ref[:, spot] = (value_grad * silu).astype(jnp.bfloat16)
        moved, step, step_rate = steps_of(raw_ref, shift_ref, rate_ref)
        by_column, by_row, lower = decay_sums(step * step_rate, extent)
        b_state = act_ref[:, width : width + NS]
        c_state = act_ref[:, width + NS :]
        inner = matmul_right(c_state, b_state)
        inner_grad = jnp.zeros((extent, extent), jnp.float32)
        lane = lax.broadcasted_iota(jnp.int32, (extent, MH), 1)
        by_column_grad = jnp.zeros((extent, MH), jnp.float32)
        step_grad = jnp.zeros((extent, MH), jnp.float32)
        for number in range(MH // 2):
            spot = slice(number * pair, (number + 1) * pair)
            heads = act_ref[:, spot].astype(jnp.float32)
            steps = pick(half, step[:, 2 * number : 2 * number + 1], step[:, 2 * number + 1 : 2 * number + 2])
            scaled = (heads * steps).astype(jnp.bfloat16)
            grad = scan_grad_ref[:, spot]
            results = []
            for first in (True, False):
                head = 2 * number + (0 if first else 1)
                decay = decay_of(by_column, by_row, head, can)
                weight_grad = masked_dot(grad, half, first, scaled)
                mixed = decay * inner
                results.append(matmul_left(mixed.astype(jnp.bfloat16), grad))
                inner_grad = inner_grad + weight_grad * decay
                spread_grad = weight_grad * mixed
                column = jnp.sum(spread_grad, axis=1, keepdims=True)
                by_column_grad = by_column_grad + jnp.where(lane == head, column, 0.0)
                row_ref[head : head + 1, :] = jnp.sum(spread_grad, axis=0, keepdims=True)
            scaled_grad = pick(half, *results)
            grad = grad.astype(jnp.float32)
            act_grad_ref[:, spot] = scaled_grad * steps + skip_ref[:, spot] * grad
            product = scaled_grad * heads
            for first in (True, False):
                head = 2 * number + (0 if first else 1)
                chosen = jnp.where(half, product, 0.0) if first else jnp.where(half, 0.0, product)
                column = jnp.sum(chosen, axis=1, keepdims=True)
                step_grad = step_grad + jnp.where(lane == head, column, 0.0)
            skip_out[:, spot] = jnp.sum(grad * heads, axis=0, keepdims=True)
        inner_low = inner_grad.astype(jnp.bfloat16)
        act_grad_ref[:, width : width + NS] = matmul_left(inner_low, c_state)
        act_grad_ref[:, width + NS :] = matmul_plain(inner_low, b_state)
        decay_grad = dot_exact(lower, by_column_grad, ((0,), (0,))) - dot_exact(
            lower, row_ref[...], ((0,), (1,))
        )
        rate_out[...] = jnp.sum(decay_grad * step * step_rate, axis=0, keepdims=True)
        raw_grad = (step_grad + decay_grad * step_rate) * sigmoid(moved)
        shift_out[...] = jnp.sum(raw_grad, axis=0, keepdims=True)
        raw_low_ref[...] = raw_grad.astype(jnp.bfloat16)
        for at in range(0, channels, 256):
            spot = slice(at, at + 256)
            total = conv_sum(conv_ref, taps_ref, bias_ref, moves_ref, spot)
            sig = sigmoid(total)
            grad = act_grad_ref[:, spot] * (sig * (1.0 + total * (1.0 - sig)))
            bias_out[:, spot] = jnp.sum(grad, axis=0, keepdims=True)
            value = conv_ref[:, spot]
            taps_out[CONV_K - 1 : CONV_K, spot] = jnp.sum(grad * value, axis=0, keepdims=True)
            sums = taps_ref[CONV_K - 1 : CONV_K, spot] * grad
            for offset in range(1, CONV_K):
                kept = grad * moves_ref[:, offset : offset + 1]
                tap = slice(CONV_K - 1 - offset, CONV_K - offset)
                taps_out[tap, spot] = jnp.sum(
                    kept * pltpu.roll(value, offset, 0), axis=0, keepdims=True
                )
                sums = sums + taps_ref[tap, spot] * pltpu.roll(kept, extent - offset, 0)
            low_ref[:, spot] = sums.astype(jnp.bfloat16)
        first = side_ref[0] == 0
        for at in range(0, MIXED // 2, 256):
            spot = slice(at, at + 256)
            near = mixed_columns(z_ref, low_ref, qkv_ref, at)
            far = mixed_columns(z_ref, low_ref, qkv_ref, at + MIXED // 2)
            mine_ref[:, spot] = jnp.where(first, near, far)
            theirs_ref[:, spot] = jnp.where(first, far, near)

    return call_whole(
        body,
        (
            shape((extent, width), jnp.bfloat16),
            shape((extent, channels), jnp.bfloat16),
            shape((extent, MH), jnp.bfloat16),
            shape((extent, MIXED // 2), jnp.bfloat16),
            shape((extent, MIXED // 2), jnp.bfloat16),
            shape((1, width)),
            shape((CONV_K, channels)),
            shape((1, channels)),
            shape((1, width)),
            shape((1, MH)),
            shape((1, MH)),
        ),
        (
            side,
            qkv_low,
            gated_grad,
            scan,
            act,
            conv_in,
            raw_step,
            gate_z,
            taps,
            bias,
            shift,
            rate,
            skip,
            gain,
            moves,
            allowed,
        ),
        MH * 24 * extent**3,
        scratch=(
            pltpu.VMEM((extent, width), jnp.bfloat16),
            pltpu.VMEM((extent, channels), jnp.float32),
            pltpu.VMEM((MH, extent), jnp.float32),
        ),
        name="mixer_back",
    )


def middle(side, pack, spans, tokens, gated, heads, cotangent, valid, gain):
    extent, model = tokens.shape
    width = gated.shape[1]
    q_cols = heads.shape[1]
    groups = pack.shape[0]
    half_ff = FF // 2

    def body(
        side_ref,
        pack_ref,
        tokens_ref,
        gated_ref,
        heads_ref,
        cot_ref,
        valid_ref,
        gain_ref,
        result_ref,
        normed_ref,
        hidden_ref,
        feed_mine,
        feed_theirs,
        gu_mine,
        gu_theirs,
        branch_mine,
        branch_theirs,
        grad_ref,
        gain_out,
        gated_out,
        heads_out,
        *rest,
    ):
        held, sems = rest[:-1], rest[-1]
        loads = []
        for number, (start, count) in enumerate(spans):
            load = pltpu.make_async_copy(
                pack_ref.at[:, pl.ds(start, count), :], held[number], sems.at[number]
            )
            load.start()
            loads.append(load)

        def matrix(number):
            return held[number][...].reshape(groups * spans[number][1], BLOCK)

        first = side_ref[0] == 0

        def split(value, mine, theirs, at):
            half = value.shape[1] // 2
            low, high = value[:, :half], value[:, half:]
            mine[:, at : at + half] = jnp.where(first, low, high)
            theirs[:, at : at + half] = jnp.where(first, high, low)

        is_valid = valid_ref[...] > 0.0
        out_grad = jnp.where(is_valid, cot_ref[...].astype(jnp.float32), 0.0)
        feed_grad = out_grad.astype(jnp.bfloat16)
        split(feed_grad, feed_mine, feed_theirs, 0)
        loads[0].wait()
        loads[1].wait()
        residual = tokens_ref[...].astype(jnp.float32) + (
            matmul_plain(gated_ref[...], matrix(0)) + matmul_plain(heads_ref[...], matrix(1))
        )
        scale = lax.rsqrt(jnp.mean(residual * residual, axis=-1, keepdims=True) + EPSILON)
        gain_val = gain_ref[...]
        normed = (residual * scale * gain_val).astype(jnp.bfloat16)
        normed_ref[...] = normed
        loads[6].wait()
        hidden_grad = matmul_right(feed_grad, matrix(6))
        normed_grad = jnp.zeros((extent, model), jnp.float32)
        feed_out = jnp.zeros((extent, model), jnp.float32)
        gates, ups = [], []
        for part in range(2):
            loads[2 + part].wait()
            loads[4 + part].wait()
            columns = slice(part * half_ff, (part + 1) * half_ff)
            gate = matmul_plain(normed, matrix(2 + part))
            up = matmul_plain(normed, matrix(4 + part))
            sig = sigmoid(gate)
            silu = gate * sig
            hidden = (silu * up).astype(jnp.bfloat16)
            hidden_ref[:, columns] = hidden
            grad = hidden_grad[:, columns]
            gate_low = (grad * up * (sig * (1.0 + gate * (1.0 - sig)))).astype(jnp.bfloat16)
            up_low = (grad * silu).astype(jnp.bfloat16)
            gates.append(gate_low)
            ups.append(up_low)
            normed_grad = normed_grad + (
                matmul_right(gate_low, matrix(2 + part)) + matmul_right(up_low, matrix(4 + part))
            )
            feed_out = feed_out + matmul_plain(hidden, matrix(6)[columns])
        gu_mine[:, :half_ff] = jnp.where(first, gates[0], gates[1])
        gu_theirs[:, :half_ff] = jnp.where(first, gates[1], gates[0])
        gu_mine[:, half_ff:] = jnp.where(first, ups[0], ups[1])
        gu_theirs[:, half_ff:] = jnp.where(first, ups[1], ups[0])
        result_ref[...] = jnp.where(is_valid, residual + feed_out, 0.0).astype(jnp.bfloat16)
        gain_out[...] = jnp.sum(normed_grad * residual * scale, axis=0, keepdims=True)
        scaled = gain_val * normed_grad
        dots = jnp.mean(scaled * residual, axis=-1, keepdims=True)
        residual_grad = out_grad + (scale * scaled - residual * (scale * scale * scale * dots))
        grad_ref[...] = residual_grad
        branch = residual_grad.astype(jnp.bfloat16)
        split(branch, branch_mine, branch_theirs, 0)
        gated_out[...] = matmul_right(branch, matrix(0))
        heads_out[...] = matmul_right(branch, matrix(1)).astype(jnp.bfloat16)

    low = jnp.bfloat16
    outs = (
        shape((extent, model), low),
        shape((extent, model), low),
        shape((extent, FF), low),
        shape((extent, model // 2), low),
        shape((extent, model // 2), low),
        shape((extent, FF), low),
        shape((extent, FF), low),
        shape((extent, model // 2), low),
        shape((extent, model // 2), low),
        shape((extent, model)),
        shape((1, model)),
        shape((extent, width)),
        shape((extent, q_cols), low),
    )
    args = (side, pack, tokens, gated, heads, cotangent, valid, gain)
    spaces = [pltpu.SMEM, pl.ANY] + [pltpu.VMEM] * 6
    return pl.pallas_call(
        body,
        out_shape=outs,
        in_specs=[pl.BlockSpec(memory_space=space) for space in spaces],
        out_specs=[pl.BlockSpec(memory_space=pltpu.VMEM)] * len(outs),
        scratch_shapes=[pltpu.VMEM((groups, count, BLOCK), low) for _, count in spans]
        + [pltpu.SemaphoreType.DMA((len(spans),))],
        compiler_params=pltpu.CompilerParams(vmem_limit_bytes=52 * 1024 * 1024),
        cost_estimate=pl.CostEstimate(
            flops=4 * extent * pack.size, bytes_accessed=2 * pack.size, transcendentals=0
        ),
        name="middle",
    )(*args)


def outer(spots, lefts, rights, segments, z_size):
    widths = [group[0].shape[1] for group in lefts]
    rows = [width // (2 * z_size) for width in widths]
    columns = sum(width for _, width in segments)
    total = len(rights)
    count = len(lefts)

    def body(spots_ref, *refs):
        left_refs = [refs[at * total : (at + 1) * total] for at in range(count)]
        right_refs = refs[count * total : (count + 1) * total]
        mine_ref, theirs_ref = refs[-2], refs[-1]
        first = spots_ref[0] == 0
        quarter = spots_ref[1]
        right = jnp.concatenate(
            [
                jnp.concatenate(
                    [
                        ref[:, pl.ds(pl.multiple_of(start + quarter * size, 128), size)]
                        for start, size in segments
                    ],
                    axis=1,
                )
                for ref in right_refs
            ],
            axis=0,
        )
        at = 0
        for group, size in zip(left_refs, rows):
            for z in range(z_size):
                left = jnp.concatenate(
                    [ref[:, 2 * z * size : 2 * (z + 1) * size] for ref in group], axis=0
                )
                both = matmul_left(left, right).astype(jnp.bfloat16)
                near, far = both[:size], both[size:]
                mine_ref[z, at : at + size, :] = jnp.where(first, near, far)
                theirs_ref[z, at : at + size, :] = jnp.where(first, far, near)
            at += size

    out = shape((z_size, sum(rows), columns), jnp.bfloat16)
    args = (spots,) + tuple(ref for group in lefts for ref in group) + tuple(rights)
    tokens = total * rights[0].shape[0]
    return call_whole(
        body, (out, out), args, 2 * tokens * sum(widths) * columns, name="outer"
    )


def finish(spots, pieces, outs, extra=None):
    size = pieces[0].shape[1]

    def body(spots_ref, *refs):
        pieces_ref = refs[:4]
        out_refs = refs[4 + (extra is not None) :]
        y, c = spots_ref[0], spots_ref[1]
        for quarter in range(4):
            same_y = y == quarter // 2
            same_c = c == quarter % 2
            for out_ref, (_, _, moves) in zip(out_refs, outs):
                for source, rows, column, count in moves[quarter]:
                    own, by_c, by_y, by_yc = [
                        ref[rows, source : source + count] for ref in pieces_ref
                    ]
                    value = jnp.where(
                        same_y,
                        jnp.where(same_c, own, by_c),
                        jnp.where(same_c, by_y, by_yc),
                    )
                    out_ref[:, column : column + count] = value.astype(jnp.float32)
        if extra is not None:
            out_refs[0][:, outs[0][1] - extra.shape[1] :] = refs[4][...]

    args = (spots,) + tuple(pieces) + (() if extra is None else (extra,))
    return call_whole(
        body, tuple(shape((rows, columns)) for rows, columns, _ in outs), args, 0, name="finish"
    )


def block_masks(segment, position):
    extent = segment.shape[0]
    slot = jnp.arange(extent, dtype=jnp.int32)
    moves = [jnp.ones((extent,), jnp.bool_)]
    for offset in range(1, CONV_K):
        moves.append((slot >= offset) & (jnp.roll(segment, offset) == segment))
    half = ATTENTION_HEAD // 2
    inverse = ROPE_BASE ** (-jnp.arange(half, dtype=jnp.float32) / half)
    angle = position.astype(jnp.float32)[:, None] * inverse[None, :]
    return (
        jnp.stack(moves, axis=1).astype(jnp.float32),
        causal_allowed(segment).astype(jnp.float32),
        jnp.tile(jnp.cos(angle), (1, 4)),
        jnp.tile(jnp.sin(angle), (1, 4)),
    )


def forward_pass(tokens_f, gains, mats, a_log, dt_bias, skip_d, segment, position):
    in_gain, conv_w, conv_b, ssm_gain, _, w_raw = gains
    w_conv, w_z, w_qkv = mats
    moves, allowed, cosine, sine = block_masks(segment, position)
    normed_f, pull_norm_one = jax.vjp(rms_scale, tokens_f, in_gain.astype(jnp.float32))
    normed = normed_f.astype(jnp.bfloat16)
    qkv = matmul_plain(normed, w_qkv)
    low, heads_out = attention_front(qkv, cosine, sine, allowed)
    conv_in = matmul_plain(normed, w_conv)
    raw_step = matmul_right(normed, w_raw)
    gate_z = matmul_plain(normed, w_z)
    mixer_args = (
        conv_in,
        raw_step,
        gate_z,
        conv_w.astype(jnp.float32),
        conv_b.astype(jnp.float32)[None],
        dt_bias[None],
        a_log[None],
        jnp.repeat(skip_d, HD)[None],
        ssm_gain.astype(jnp.float32)[None],
        moves,
        allowed,
    )
    act, scan, gated = mixer_front(*mixer_args)
    kept = (pull_norm_one, normed, mixer_args, act, scan, low, (cosine, sine, allowed))
    return (gated, heads_out, kept)


def backward_pass(side, grads, w_raw, mats, kept):
    w_conv, w_z, w_qkv = mats
    pull_norm_one, normed, mixer_args, act, scan, low, turn_args = kept
    residual_grad, gated_grad, heads_grad = grads
    qkv_low = attention_back(low, heads_grad, *turn_args)
    (
        z_low,
        conv_low,
        raw_low,
        mixed_mine,
        mixed_theirs,
        grad_ssm_gain,
        grad_conv_w,
        grad_conv_b,
        skip_lanes,
        grad_dt_bias,
        grad_a_log,
    ) = mixer_back(side, qkv_low, gated_grad, scan, act, *mixer_args)
    grad_skip = jnp.sum(skip_lanes.reshape(MH, HD), axis=1)
    normed_grad = (
        matmul_right(qkv_low, w_qkv)
        + matmul_right(z_low, w_z)
        + matmul_right(conv_low, w_conv)
        + matmul_plain(raw_low, w_raw)
    )
    token_part, grad_in_gain = pull_norm_one(normed_grad)
    tokens_grad = (residual_grad + token_part).astype(jnp.bfloat16)
    raw_rows = matmul_left(raw_low, normed)
    small = (
        grad_in_gain,
        grad_conv_w,
        grad_conv_b[0],
        grad_ssm_gain[0],
        raw_rows,
        grad_a_log[0],
        grad_dt_bias[0],
        grad_skip,
    )
    return (tokens_grad, (mixed_mine, mixed_theirs), small)


AXES = ("shard", "replica")


def place(pieces, positions, dim, count):
    shape = list(pieces[0].shape)
    shape[dim] = count
    total = len(pieces)

    def body(where, *refs):
        out, held, sems = refs[total], refs[total + 1 : 2 * total + 1], refs[-1]
        loads, stores = [], []
        for number in range(total):
            spot = (slice(None),) * dim + (pl.ds(where[number], 1),)
            loads.append(
                pltpu.make_async_copy(refs[number], held[number], sems.at[0, number])
            )
            stores.append(
                pltpu.make_async_copy(held[number], out.at[spot], sems.at[1, number])
            )
        for load in loads:
            load.start()
        for load, store in zip(loads, stores):
            load.wait()
            store.start()
        for store in stores:
            store.wait()

    moved = 2 * sum(piece.size * piece.dtype.itemsize for piece in pieces)
    return pl.pallas_call(
        body,
        out_shape=jax.ShapeDtypeStruct(tuple(shape), pieces[0].dtype),
        in_specs=[pl.BlockSpec(memory_space=pltpu.SMEM)]
        + [pl.BlockSpec(memory_space=pl.ANY)] * total,
        out_specs=pl.BlockSpec(memory_space=pl.ANY),
        scratch_shapes=[pltpu.VMEM(piece.shape, piece.dtype) for piece in pieces]
        + [pltpu.SemaphoreType.DMA((2, total))],
        compiler_params=pltpu.CompilerParams(vmem_limit_bytes=24 * 1024 * 1024),
        cost_estimate=pl.CostEstimate(flops=0, bytes_accessed=moved, transcendentals=0),
        name="place",
    )(jnp.stack(positions).astype(jnp.int32), *pieces)


class Links:
    def __init__(self, shards_of, copies):
        self.z_size = shards_of // 2
        shard = lax.axis_index("shard")
        replica = lax.axis_index("replica")
        self.z, self.x = shard // 2, shard % 2
        self.y, self.c = replica // 2, replica % 2
        everyone = [(s, r) for s in range(shards_of) for r in range(copies)]

        def table(step):
            return [(s * copies + r, step(s, r)) for s, r in everyone]

        self.tables = {
            "x": table(lambda s, r: (s ^ 1) * copies + r),
            "y": table(lambda s, r: s * copies + (r ^ 2)),
            "c": table(lambda s, r: s * copies + (r ^ 1)),
            "z": table(lambda s, r: ((s + 2) % shards_of) * copies + r),
            "z_one": table(lambda s, r: (s ^ 2) * copies + r),
            "z_two": table(lambda s, r: (s ^ 4) * copies + r),
        }

    def send(self, value, axis):
        return lax.ppermute(value, AXES, self.tables[axis])

    def spread(self, value, axis):
        if axis == "z":
            pieces, spots = [value], [self.z]
            for step in range(1, self.z_size):
                pieces.append(self.send(pieces[-1], "z"))
                spots.append((self.z + self.z_size - step) % self.z_size)
            return place(pieces, spots, 0, self.z_size)
        spot = {"x": self.x, "y": self.y, "c": self.c}[axis]
        return place([value, self.send(value, axis)], [spot, 1 - spot], "zxyc".index(axis), 2)

    def gather(self, own, order):
        rows, columns = own.shape
        cut = own.reshape(1, 1, 2, 2, rows // 4, columns)
        cut = lax.dynamic_slice_in_dim(cut, self.c, 1, 3)
        if "y" in order:
            cut = lax.dynamic_slice_in_dim(cut, self.y, 1, 2)
        for axis in order:
            cut = self.spread(cut, axis)
        return cut.reshape(-1, columns)

    def gather_small(self, own):
        other = self.send(own, "x")
        pair = jnp.stack(
            [jnp.where(self.x == 0, own, other), jnp.where(self.x == 0, other, own)]
        )
        pieces = [pair]
        for _ in range(1, self.z_size):
            pieces.append(self.send(pieces[-1], "z"))
        stacked = jnp.stack(pieces)
        return jnp.concatenate(
            [
                lax.dynamic_index_in_dim(stacked, (self.z + self.z_size - at) % self.z_size, 0, False)
                for at in range(self.z_size)
            ]
        )

    def exchange(self, lefts, mine, theirs, segments):
        rights = [mine, self.send(theirs, "y")]
        rights = rights + [self.send(value, "c") for value in rights]
        groups = []
        for left in lefts:
            group = [left, self.send(left, "y")]
            groups.append(group + [self.send(value, "c") for value in group])
        spots = jnp.stack([self.x, self.c]).astype(jnp.int32)
        return outer(spots, groups, rights, segments, self.z_size)

    def reduce(self, mine, theirs):
        moved = self.send(theirs, "x")

        def block(step):
            at = (self.z + 2 * self.z_size - 1 - step) % self.z_size
            return lax.dynamic_index_in_dim(mine, at, 0, False).astype(
                jnp.float32
            ) + lax.dynamic_index_in_dim(moved, at, 0, False).astype(jnp.float32)

        total = block(0).astype(jnp.bfloat16)
        for step in range(1, self.z_size):
            arrived = self.send(total, "z")
            total = (arrived.astype(jnp.float32) + block(step)).astype(jnp.bfloat16)
        by_y = self.send(total, "y")
        return (total, self.send(total, "c"), by_y, self.send(by_y, "c"))

    def total(self, value):
        for axis in ("c", "y", "x", "z_one", "z_two"):
            value = value + self.send(value, axis)
        return value


def pack_small(in_gain, conv_w, conv_b, ssm_gain, ff_gain, raw):
    def rows(value):
        flat = value.reshape(-1)
        return jnp.pad(flat, (0, -flat.shape[0] % 128)).reshape(-1, 128)

    packed = jnp.concatenate([rows(v) for v in (raw.T, in_gain, conv_w, conv_b, ssm_gain, ff_gain)])
    return jnp.pad(packed, ((0, -packed.shape[0] % 16), (0, 0)))


def unpack_small(gathered, own):
    in_gain, conv_w, conv_b, ssm_gain, ff_gain, raw = own
    parts = gathered.shape[0]
    at = 0
    out = []
    for value in (raw.T, in_gain, conv_w, conv_b, ssm_gain, ff_gain):
        count = -(-value.size // 128)
        flat = gathered[:, at : at + count].reshape(parts, -1)[:, : value.size]
        at += count
        shaped = flat.reshape((parts,) + value.shape)
        if value.ndim == 1:
            out.append(shaped.reshape(-1))
        else:
            out.append(shaped.transpose(1, 0, 2).reshape(value.shape[0], -1))
    return tuple(out[1:]) + (out[0],)


def shards(
    copies,
    tokens,
    cotangent,
    seq_lengths,
    seq_starts,
    in_gain,
    w_in,
    conv_w,
    conv_b,
    a_log,
    dt_bias,
    skip_d,
    ssm_gain,
    w_out,
    w_query,
    w_key,
    w_value,
    w_attn_out,
    ff_gain,
    w_gate,
    w_up,
    w_down,
):
    parts = MH * HD // w_out.shape[0]
    width = MH * HD
    channels = width + 2 * NS
    quick = parts == 8 and copies == 4
    links = Links(parts, copies)
    own_small = (in_gain, conv_w, conv_b, ssm_gain, ff_gain, w_in[:, width + channels :])
    own = (
        w_in[:, width : width + channels],
        w_in[:, :width],
        jnp.concatenate([w_query, w_key, w_value], axis=1),
    )
    blocks = (
        w_out,
        w_attn_out,
        w_gate[:, :BLOCK],
        w_gate[:, BLOCK:],
        w_up[:, :BLOCK],
        w_up[:, BLOCK:],
        w_down,
    )
    pieces = 4 if quick else 1
    turn = links.y * 2 + links.c if quick else 0
    cuts, spans, at = [], [], 0
    for value in blocks:
        count = value.shape[0] // pieces
        cuts.append(lax.dynamic_slice_in_dim(value, turn * count, count, 0))
        spans.append((at, count))
        at += count
    pack = jnp.concatenate(cuts, axis=0)
    if quick:
        orders = ("zxyc", "zyxc", "xzc")
        small_all = links.gather_small(pack_small(*own_small))
        mats = tuple(links.gather(value, order) for value, order in zip(own, orders))
        pack = lax.all_gather(pack, AXES, axis=0)
    else:
        small_all = lax.all_gather(pack_small(*own_small), "shard", axis=0)
        mats = tuple(lax.all_gather(value, "shard", axis=0, tiled=True) for value in own)
        pack = lax.all_gather(pack, "shard", axis=0)
    gains = unpack_small(small_all, own_small)
    segment, position = layout(seq_lengths[0], seq_starts[0], tokens.shape[0])
    gated, heads_out, kept = forward_pass(
        tokens.astype(jnp.float32), gains, mats, a_log, dt_bias, skip_d, segment, position
    )
    side = jnp.stack([links.y if quick else jnp.int32(0)]).astype(jnp.int32)
    valid = (segment >= 0).astype(jnp.float32)[:, None]
    (
        result,
        normed_two,
        hidden,
        feed_mine,
        feed_theirs,
        gu_mine,
        gu_theirs,
        branch_mine,
        branch_theirs,
        residual_grad,
        grad_ff_gain,
        gated_grad,
        heads_grad,
    ) = middle(
        side, pack, spans, tokens, gated, heads_out, cotangent, valid, gains[4].astype(jnp.float32)[None]
    )
    tokens_grad, (mixed_mine, mixed_theirs), small = backward_pass(
        side, (residual_grad, gated_grad, heads_grad), gains[5], mats, kept
    )
    small = small + (grad_ff_gain[0],)
    normed = kept[1]
    flat = jnp.concatenate([value.reshape(-1) for value in small])
    flat = jnp.pad(flat, (0, -flat.shape[0] % 1024)).reshape(-1, 128)
    flat = (links.total(flat) if quick else lax.psum(flat, AXES)).reshape(-1)
    totals = []
    at = 0
    for value in small:
        totals.append(flat[at : at + value.size].reshape(value.shape))
        at += value.size
    here = lax.axis_index("shard")

    def mine(value):
        size = value.shape[-1] // parts
        return lax.dynamic_slice_in_dim(value, here * size, size, value.ndim - 1)

    raw_part = mine(totals[4]).T
    q_cols = QH * ATTENTION_HEAD
    k_cols = KVH * ATTENTION_HEAD
    out_rows, attn_rows = w_out.shape[0], w_attn_out.shape[0]
    down_rows, model_rows = w_down.shape[0], w_in.shape[0]
    if quick:
        quarter = BLOCK // 4
        whole = slice(None)

        def plain(rows):
            return [[(0, rows, number * quarter, quarter)] for number in range(4)]

        half_ff, quarter_ff = FF // 2, FF // 4
        edges = (0, width + channels, width + channels + q_cols, MIXED - k_cols, MIXED)
        mixed_moves = [[[] for _ in range(4)] for _ in range(4)]
        for number in range(4):
            for index in range(4):
                low = max(edges[index], number * BLOCK)
                high = min(edges[index + 1], (number + 1) * BLOCK)
                if low < high:
                    mixed_moves[index][number].append(
                        (low - number * BLOCK, whole, low - edges[index], high - low)
                    )
        spots = jnp.stack([links.y, links.c]).astype(jnp.int32)
        down_parts = links.exchange([hidden], feed_mine, feed_theirs, [(0, quarter)])
        feed_parts = links.exchange(
            [normed_two], gu_mine, gu_theirs, [(0, quarter_ff), (half_ff, quarter_ff)]
        )
        out_parts = links.exchange([gated, heads_out], branch_mine, branch_theirs, [(0, quarter)])
        mixed_parts = links.exchange([normed], mixed_mine, mixed_theirs, [(0, BLOCK)])
        (down,) = finish(
            spots, links.reduce(*down_parts), [(down_rows, BLOCK, plain(whole))]
        )
        gate, up = finish(
            spots,
            links.reduce(*feed_parts),
            [
                (
                    model_rows,
                    FF,
                    [[(at, whole, number * quarter_ff, quarter_ff)] for number in range(4)],
                )
                for at in (0, quarter_ff)
            ],
        )
        out, attn = finish(
            spots,
            links.reduce(*out_parts),
            [
                (out_rows, BLOCK, plain(slice(0, out_rows))),
                (attn_rows, BLOCK, plain(slice(out_rows, out_rows + attn_rows))),
            ],
        )
        projection, query, key, value = finish(
            spots,
            links.reduce(*mixed_parts),
            [
                (model_rows, columns, moves)
                for columns, moves in zip(
                    (width + channels + MH, q_cols, k_cols, k_cols), mixed_moves
                )
            ],
            raw_part,
        )
    else:

        def joined(first, second):
            return jnp.concatenate([first, second], axis=1)

        def share(left, right):
            part = lax.psum_scatter(
                matmul_left(left, right).astype(jnp.bfloat16),
                "shard",
                scatter_dimension=0,
                tiled=True,
            )
            return lax.psum(part, "replica").astype(jnp.float32)

        half_ff = FF // 2
        branch = joined(branch_mine, branch_theirs)
        mixed = share(normed, joined(mixed_mine, mixed_theirs))
        down = share(hidden, joined(feed_mine, feed_theirs))
        gate = share(normed_two, joined(gu_mine[:, :half_ff], gu_theirs[:, :half_ff]))
        up = share(normed_two, joined(gu_mine[:, half_ff:], gu_theirs[:, half_ff:]))
        out = share(gated, branch)
        attn = share(heads_out, branch)
        at = width + channels
        projection = joined(mixed[:, :at], raw_part)
        query = mixed[:, at : at + q_cols]
        key = mixed[:, at + q_cols : at + q_cols + k_cols]
        value = mixed[:, at + q_cols + k_cols :]
    return (
        result,
        tokens_grad,
        mine(totals[0]),
        projection,
        mine(totals[1]),
        mine(totals[2]),
        totals[5],
        totals[6],
        totals[7],
        mine(totals[3]),
        out,
        query,
        key,
        value,
        attn,
        mine(totals[8]),
        gate,
        up,
        down,
    )


def solution(mesh):
    in_specs = (
        P(("shard", "replica"), None),
        P(("shard", "replica"), None),
        P(("shard", "replica"), None),
        P(("shard", "replica"), None),
        P("shard"),
        P("shard", None),
        P(None, "shard"),
        P("shard"),
        P(),
        P(),
        P(),
        P("shard"),
        P("shard", None),
        P("shard", None),
        P("shard", None),
        P("shard", None),
        P("shard", None),
        P("shard"),
        P("shard", None),
        P("shard", None),
        P("shard", None),
    )
    out_specs = (
        P(("shard", "replica"), None),
        P(("shard", "replica"), None),
        P("shard"),
        P("shard", None),
        P(None, "shard"),
        P("shard"),
        P(),
        P(),
        P(),
        P("shard"),
        P("shard", None),
        P("shard", None),
        P("shard", None),
        P("shard", None),
        P("shard", None),
        P("shard"),
        P("shard", None),
        P("shard", None),
        P("shard", None),
    )

    def local(*args):
        return shards(mesh.shape["replica"], *args)

    return jax.shard_map(local, mesh=mesh, in_specs=in_specs, out_specs=out_specs, check_vma=False)
```

```python
import jax
import jax.numpy as jnp
from jax import lax
from jax.experimental import pallas as pl
from jax.experimental.pallas import tpu as pltpu
from jax.sharding import PartitionSpec as P

FF = 2048
MH = 24
HD = 64
NS = 128
QH = 8
KVH = 2
ATTENTION_HEAD = 64
CONV_K = 4
MIXED = 2 * MH * HD + 2 * NS + (QH + 2 * KVH) * ATTENTION_HEAD
BLOCK = 1024


EPSILON = 1e-05
ROPE_BASE = 100000000000.0


def matmul_plain(left, right):
    return jnp.dot(left, right, preferred_element_type=jnp.float32)


def matmul_left(left, right):
    return lax.dot_general(
        left, right, (((0,), (0,)), ((), ())), preferred_element_type=jnp.float32
    )


def matmul_right(left, right):
    return lax.dot_general(
        left, right, (((1,), (1,)), ((), ())), preferred_element_type=jnp.float32
    )


def rms_scale(values, gain):
    return values * lax.rsqrt(jnp.mean(values * values, axis=-1, keepdims=True) + EPSILON) * gain


def layout(lengths, starts, extent):
    position = jnp.arange(extent, dtype=jnp.int32)
    inside = (position[:, None] >= starts[None, :]) & (
        position[:, None] < starts[None, :] + lengths[None, :]
    )
    number = jnp.arange(1, lengths.shape[0] + 1, dtype=jnp.int32)
    segment = jnp.sum(jnp.where(inside, number[None, :], 0), axis=1) - 1
    first = jnp.sum(jnp.where(inside, starts[None, :], 0), axis=1)
    return (segment, position - first)


def causal_allowed(segment):
    position = jnp.arange(segment.shape[0], dtype=jnp.int32)
    return (segment[:, None] == segment[None, :]) & (position[:, None] >= position[None, :])


def swiglu(gate_val, up_val):
    return jax.nn.silu(gate_val) * up_val


def sigmoid(value):
    return 1.0 / (1.0 + jnp.exp(-value))


def dot_exact(left, right, dims):
    return lax.dot_general(
        left,
        right,
        (dims, ((), ())),
        precision=lax.Precision.HIGHEST,
        preferred_element_type=jnp.float32,
    )


def lane_half(rows):
    return lax.broadcasted_iota(jnp.int32, (rows, 2 * HD), 1) < HD


def pick(half, first, second):
    return jnp.where(half, first, second)


def call_whole(body, outs, args, flops, scratch=(), name="kernel", after=()):
    moved = sum(arg.size * arg.dtype.itemsize for arg in args)
    moved += sum(out.size * out.dtype.itemsize for out in outs)
    count = len(args)

    def ordered(*refs):
        body(*refs[:count], *refs[count + len(after) :])

    return pl.pallas_call(
        ordered,
        out_shape=outs,
        in_specs=[
            pl.BlockSpec(memory_space=pltpu.SMEM if arg.dtype == jnp.int32 else pltpu.VMEM)
            for arg in args
        ]
        + [pl.BlockSpec(memory_space=pl.ANY)] * len(after),
        out_specs=[pl.BlockSpec(memory_space=pltpu.VMEM)] * len(outs),
        scratch_shapes=list(scratch),
        compiler_params=pltpu.CompilerParams(vmem_limit_bytes=40 * 1024 * 1024),
        cost_estimate=pl.CostEstimate(flops=flops, bytes_accessed=moved, transcendentals=0),
        name=name,
    )(*args, *after)


def shape(dims, kind=jnp.float32):
    return jax.ShapeDtypeStruct(dims, kind)


def turned(values, cosine, sine, back):
    width = values.shape[1]
    quarter = lax.broadcasted_iota(jnp.int32, values.shape, 1) % ATTENTION_HEAD
    half = ATTENTION_HEAD // 2
    swapped = jnp.where(
        quarter < half,
        -pltpu.roll(values, width - half, 1),
        pltpu.roll(values, half, 1),
    )
    return values * cosine - swapped * sine if back else values * cosine + swapped * sine


def doubled(values, half):
    moved = pltpu.roll(values, ATTENTION_HEAD, 1)
    return (pick(half, values, moved), pick(half, moved, values))


def masked_dot(pair, half, keep_first, other):
    zero = jnp.zeros_like(pair)
    chosen = jnp.where(half, pair, zero) if keep_first else jnp.where(half, zero, pair)
    return matmul_right(chosen, other)


def softmax_rows(scores, allowed):
    scores = jnp.where(allowed, scores * ATTENTION_HEAD ** (-0.5), -1e30)
    raised = jnp.exp(scores - jnp.max(scores, axis=-1, keepdims=True))
    return raised / jnp.sum(raised, axis=-1, keepdims=True)


def attention_front(qkv, cosine, sine, allowed):
    extent = qkv.shape[0]
    pair = 2 * ATTENTION_HEAD
    pairs = QH // 2

    def body(qkv_ref, cos_ref, sin_ref, allowed_ref, low_ref, out_ref):
        half = lane_half(extent)
        can = allowed_ref[...] > 0.0
        cos_val, sin_val = cos_ref[...], sin_ref[...]
        key = turned(qkv_ref[:, pairs * pair : (pairs + 1) * pair], cos_val, sin_val, False)
        key = key.astype(jnp.bfloat16)
        value = qkv_ref[:, (pairs + 1) * pair :].astype(jnp.bfloat16)
        low_ref[:, pairs * pair : (pairs + 1) * pair] = key
        low_ref[:, (pairs + 1) * pair :] = value
        keys = [k.astype(jnp.bfloat16) for k in doubled(key.astype(jnp.float32), half)]
        values = [v.astype(jnp.bfloat16) for v in doubled(value.astype(jnp.float32), half)]
        for number in range(pairs):
            spot = slice(number * pair, (number + 1) * pair)
            query = turned(qkv_ref[:, spot], cos_val, sin_val, False).astype(jnp.bfloat16)
            low_ref[:, spot] = query
            group = number * KVH // pairs
            results = []
            for first in (True, False):
                scores = masked_dot(query, half, first, keys[group])
                probs = softmax_rows(scores, can).astype(jnp.bfloat16)
                results.append(matmul_plain(probs, values[group]))
            out_ref[:, spot] = pick(half, *results).astype(jnp.bfloat16)

    return call_whole(
        body,
        (shape(qkv.shape, jnp.bfloat16), shape((extent, pairs * pair), jnp.bfloat16)),
        (qkv, cosine, sine, allowed),
        QH * 8 * extent**3,
        name="attention_front",
    )


def attention_back(low, heads_grad, cosine, sine, allowed):
    extent = low.shape[0]
    pair = 2 * ATTENTION_HEAD
    pairs = QH // 2
    scale = ATTENTION_HEAD ** (-0.5)

    def body(low_ref, grad_ref, cos_ref, sin_ref, allowed_ref, out_ref):
        half = lane_half(extent)
        can = allowed_ref[...] > 0.0
        cos_val, sin_val = cos_ref[...], sin_ref[...]
        key = low_ref[:, pairs * pair : (pairs + 1) * pair].astype(jnp.float32)
        value = low_ref[:, (pairs + 1) * pair :].astype(jnp.float32)
        keys = [k.astype(jnp.bfloat16) for k in doubled(key, half)]
        values = [v.astype(jnp.bfloat16) for v in doubled(value, half)]
        key_sums = [jnp.zeros((extent, pair), jnp.float32) for _ in range(KVH)]
        value_sums = [jnp.zeros((extent, pair), jnp.float32) for _ in range(KVH)]
        for number in range(pairs):
            spot = slice(number * pair, (number + 1) * pair)
            query = low_ref[:, spot]
            grad = grad_ref[:, spot]
            group = number * KVH // pairs
            q_parts, k_parts, v_parts = [], [], []
            for first in (True, False):
                probs = softmax_rows(masked_dot(query, half, first, keys[group]), can)
                prob_grad = masked_dot(grad, half, first, values[group])
                v_parts.append(matmul_left(probs.astype(jnp.bfloat16), grad))
                inner = jnp.sum(probs * prob_grad, axis=-1, keepdims=True)
                score_grad = (probs * (prob_grad - inner)).astype(jnp.bfloat16)
                q_parts.append(matmul_plain(score_grad, keys[group]))
                k_parts.append(matmul_left(score_grad, query))
            key_sums[group] = key_sums[group] + pick(half, *k_parts)
            value_sums[group] = value_sums[group] + pick(half, *v_parts)
            query_grad = turned(pick(half, *q_parts) * scale, cos_val, sin_val, True)
            out_ref[:, spot] = query_grad.astype(jnp.bfloat16)

        def both(sums):
            return pick(half, *[s + pltpu.roll(s, ATTENTION_HEAD, 1) for s in sums])

        key_grad = turned(both(key_sums) * scale, cos_val, sin_val, True)
        out_ref[:, pairs * pair : (pairs + 1) * pair] = key_grad.astype(jnp.bfloat16)
        out_ref[:, (pairs + 1) * pair :] = both(value_sums).astype(jnp.bfloat16)

    (out,) = call_whole(
        body,
        (shape(low.shape, jnp.bfloat16),),
        (low, heads_grad, cosine, sine, allowed),
        QH * 14 * extent**3,
        name="attention_back",
    )
    return out


def conv_sum(conv_ref, taps_ref, bias_ref, moves_ref, spot):
    value = conv_ref[:, spot]
    total = bias_ref[:, spot] + taps_ref[CONV_K - 1 : CONV_K, spot] * value
    for offset in range(1, CONV_K):
        moved = pltpu.roll(value, offset, 0) * moves_ref[:, offset : offset + 1]
        total = total + taps_ref[CONV_K - 1 - offset : CONV_K - offset, spot] * moved
    return total


def steps_of(raw_ref, shift_ref, rate_ref):
    moved = raw_ref[...] + shift_ref[...]
    step = jnp.maximum(moved, 0.0) + jnp.log1p(jnp.exp(-jnp.abs(moved)))
    rate = -jnp.exp(rate_ref[...])
    return moved, step, rate


def decay_sums(decay, extent):
    row = lax.broadcasted_iota(jnp.int32, (extent, extent), 0)
    column = lax.broadcasted_iota(jnp.int32, (extent, extent), 1)
    lower = jnp.where(row >= column, 1.0, 0.0)
    by_column = dot_exact(lower, decay, ((1,), (0,)))
    by_row = dot_exact(decay, lower, ((0,), (1,)))
    return by_column, by_row, lower


def decay_of(by_column, by_row, head, can):
    spread = by_column[:, head : head + 1] - by_row[head : head + 1, :]
    return jnp.where(can, jnp.exp(jnp.where(can, spread, 0.0)), 0.0)


def mixer_front(
    side,
    heads_out,
    normed,
    feed_grad,
    conv_in,
    raw_step,
    gate_z,
    taps,
    bias,
    shift,
    rate,
    skip,
    gain,
    moves,
    allowed,
):
    extent = conv_in.shape[0]
    at_normed = MH * HD + heads_out.shape[1]
    at_feed = at_normed + normed.shape[1]
    half_feed = feed_grad.shape[1] // 2
    width = MH * HD
    pair = 2 * HD

    def body(
        side_ref,
        heads_ref,
        normed_ref,
        feed_ref,
        conv_ref,
        raw_ref,
        gate_ref,
        taps_ref,
        bias_ref,
        shift_ref,
        rate_ref,
        skip_ref,
        gain_ref,
        moves_ref,
        allowed_ref,
        act_ref,
        scan_ref,
        mine_ref,
        theirs_ref,
    ):
        side_first = side_ref[0] == 0
        low, high = feed_ref[:, :half_feed], feed_ref[:, half_feed:]
        for ref in (mine_ref, theirs_ref):
            ref[:, MH * HD : at_normed] = heads_ref[...]
            ref[:, at_normed:at_feed] = normed_ref[...]
        mine_ref[:, at_feed:] = jnp.where(side_first, low, high)
        theirs_ref[:, at_feed:] = jnp.where(side_first, high, low)
        half = lane_half(extent)
        can = allowed_ref[...] > 0.0
        for at in range(0, width + 2 * NS, 256):
            spot = slice(at, at + 256)
            total = conv_sum(conv_ref, taps_ref, bias_ref, moves_ref, spot)
            act_ref[:, spot] = (total * sigmoid(total)).astype(jnp.bfloat16)
        _, step, step_rate = steps_of(raw_ref, shift_ref, rate_ref)
        by_column, by_row, _ = decay_sums(step * step_rate, extent)
        inner = matmul_right(act_ref[:, width + NS :], act_ref[:, width : width + NS])
        squares = jnp.zeros((extent, 1), jnp.float32)
        for number in range(MH // 2):
            spot = slice(number * pair, (number + 1) * pair)
            heads = act_ref[:, spot].astype(jnp.float32)
            steps = pick(half, step[:, 2 * number : 2 * number + 1], step[:, 2 * number + 1 : 2 * number + 2])
            scaled = (heads * steps).astype(jnp.bfloat16)
            results = []
            for head in (2 * number, 2 * number + 1):
                weights = (decay_of(by_column, by_row, head, can) * inner).astype(jnp.bfloat16)
                results.append(matmul_plain(weights, scaled))
            scan = pick(half, *results) + skip_ref[:, spot] * heads
            scan_ref[:, spot] = scan
            gate = gate_ref[:, spot]
            value = scan * (gate * sigmoid(gate))
            squares = squares + jnp.sum(value * value, axis=-1, keepdims=True)
        scale = lax.rsqrt(squares / width + EPSILON)
        for number in range(MH // 2):
            spot = slice(number * pair, (number + 1) * pair)
            gate = gate_ref[:, spot]
            value = scan_ref[:, spot] * (gate * sigmoid(gate))
            gated = (value * scale * gain_ref[:, spot]).astype(jnp.bfloat16)
            mine_ref[:, spot] = gated
            theirs_ref[:, spot] = gated

    return call_whole(
        body,
        (
            shape((extent, width + 2 * NS), jnp.bfloat16),
            shape((extent, width)),
            shape((extent, at_feed + half_feed), jnp.bfloat16),
            shape((extent, at_feed + half_feed), jnp.bfloat16),
        ),
        (side, heads_out, normed, feed_grad, conv_in, raw_step, gate_z, taps, bias, shift, rate, skip, gain, moves, allowed),
        MH * 16 * extent**3,
        name="mixer_front",
    )


def mixed_columns(z_ref, low_ref, qkv_ref, at):
    for ref in (z_ref, low_ref, qkv_ref):
        if at < ref.shape[1]:
            return ref[:, at : at + 256]
        at -= ref.shape[1]


def mixer_back(
    side,
    qkv_low,
    gated_grad,
    scan,
    act,
    conv_in,
    raw_step,
    gate_z,
    taps,
    bias,
    shift,
    rate,
    skip,
    gain,
    moves,
    allowed,
):
    extent = conv_in.shape[0]
    width = MH * HD
    channels = width + 2 * NS
    pair = 2 * HD

    def body(
        side_ref,
        qkv_ref,
        grad_ref,
        scan_ref,
        act_ref,
        conv_ref,
        raw_ref,
        gate_ref,
        taps_ref,
        bias_ref,
        shift_ref,
        rate_ref,
        skip_ref,
        gain_ref,
        moves_ref,
        allowed_ref,
        z_ref,
        low_ref,
        raw_low_ref,
        mine_ref,
        theirs_ref,
        gain_out,
        taps_out,
        bias_out,
        skip_out,
        shift_out,
        rate_out,
        scan_grad_ref,
        act_grad_ref,
        row_ref,
    ):
        half = lane_half(extent)
        can = allowed_ref[...] > 0.0
        squares = jnp.zeros((extent, 1), jnp.float32)
        dots = jnp.zeros((extent, 1), jnp.float32)
        for at in range(0, width, 256):
            spot = slice(at, at + 256)
            gate = gate_ref[:, spot]
            value = scan_ref[:, spot] * (gate * sigmoid(gate))
            squares = squares + jnp.sum(value * value, axis=-1, keepdims=True)
            dots = dots + jnp.sum(value * gain_ref[:, spot] * grad_ref[:, spot], axis=-1, keepdims=True)
        scale = lax.rsqrt(squares / width + EPSILON)
        common = scale * scale * scale * (dots / width)
        for at in range(0, width, 256):
            spot = slice(at, at + 256)
            gate = gate_ref[:, spot]
            sig = sigmoid(gate)
            silu = gate * sig
            scanned = scan_ref[:, spot]
            value = scanned * silu
            grad = grad_ref[:, spot]
            gain_out[:, spot] = jnp.sum(grad * value * scale, axis=0, keepdims=True)
            value_grad = scale * (gain_ref[:, spot] * grad) - value * common
            z_ref[:, spot] = (value_grad * scanned * (sig * (1.0 + gate * (1.0 - sig)))).astype(
                jnp.bfloat16
            )
            scan_grad_ref[:, spot] = (value_grad * silu).astype(jnp.bfloat16)
        moved, step, step_rate = steps_of(raw_ref, shift_ref, rate_ref)
        by_column, by_row, lower = decay_sums(step * step_rate, extent)
        b_state = act_ref[:, width : width + NS]
        c_state = act_ref[:, width + NS :]
        inner = matmul_right(c_state, b_state)
        inner_grad = jnp.zeros((extent, extent), jnp.float32)
        lane = lax.broadcasted_iota(jnp.int32, (extent, MH), 1)
        by_column_grad = jnp.zeros((extent, MH), jnp.float32)
        step_grad = jnp.zeros((extent, MH), jnp.float32)
        for number in range(MH // 2):
            spot = slice(number * pair, (number + 1) * pair)
            heads = act_ref[:, spot].astype(jnp.float32)
            steps = pick(half, step[:, 2 * number : 2 * number + 1], step[:, 2 * number + 1 : 2 * number + 2])
            scaled = (heads * steps).astype(jnp.bfloat16)
            grad = scan_grad_ref[:, spot]
            results = []
            for first in (True, False):
                head = 2 * number + (0 if first else 1)
                decay = decay_of(by_column, by_row, head, can)
                weight_grad = masked_dot(grad, half, first, scaled)
                mixed = decay * inner
                results.append(matmul_left(mixed.astype(jnp.bfloat16), grad))
                inner_grad = inner_grad + weight_grad * decay
                spread_grad = weight_grad * mixed
                column = jnp.sum(spread_grad, axis=1, keepdims=True)
                by_column_grad = by_column_grad + jnp.where(lane == head, column, 0.0)
                row_ref[head : head + 1, :] = jnp.sum(spread_grad, axis=0, keepdims=True)
            scaled_grad = pick(half, *results)
            grad = grad.astype(jnp.float32)
            act_grad_ref[:, spot] = scaled_grad * steps + skip_ref[:, spot] * grad
            product = scaled_grad * heads
            for first in (True, False):
                head = 2 * number + (0 if first else 1)
                chosen = jnp.where(half, product, 0.0) if first else jnp.where(half, 0.0, product)
                column = jnp.sum(chosen, axis=1, keepdims=True)
                step_grad = step_grad + jnp.where(lane == head, column, 0.0)
            skip_out[:, spot] = jnp.sum(grad * heads, axis=0, keepdims=True)
        inner_low = inner_grad.astype(jnp.bfloat16)
        act_grad_ref[:, width : width + NS] = matmul_left(inner_low, c_state)
        act_grad_ref[:, width + NS :] = matmul_plain(inner_low, b_state)
        decay_grad = dot_exact(lower, by_column_grad, ((0,), (0,))) - dot_exact(
            lower, row_ref[...], ((0,), (1,))
        )
        rate_out[...] = jnp.sum(decay_grad * step * step_rate, axis=0, keepdims=True)
        raw_grad = (step_grad + decay_grad * step_rate) * sigmoid(moved)
        shift_out[...] = jnp.sum(raw_grad, axis=0, keepdims=True)
        raw_low_ref[...] = raw_grad.astype(jnp.bfloat16)
        for at in range(0, channels, 256):
            spot = slice(at, at + 256)
            total = conv_sum(conv_ref, taps_ref, bias_ref, moves_ref, spot)
            sig = sigmoid(total)
            grad = act_grad_ref[:, spot] * (sig * (1.0 + total * (1.0 - sig)))
            bias_out[:, spot] = jnp.sum(grad, axis=0, keepdims=True)
            value = conv_ref[:, spot]
            taps_out[CONV_K - 1 : CONV_K, spot] = jnp.sum(grad * value, axis=0, keepdims=True)
            sums = taps_ref[CONV_K - 1 : CONV_K, spot] * grad
            for offset in range(1, CONV_K):
                kept = grad * moves_ref[:, offset : offset + 1]
                tap = slice(CONV_K - 1 - offset, CONV_K - offset)
                taps_out[tap, spot] = jnp.sum(
                    kept * pltpu.roll(value, offset, 0), axis=0, keepdims=True
                )
                sums = sums + taps_ref[tap, spot] * pltpu.roll(kept, extent - offset, 0)
            low_ref[:, spot] = sums.astype(jnp.bfloat16)
        first = side_ref[0] == 0
        for at in range(0, MIXED // 2, 256):
            spot = slice(at, at + 256)
            near = mixed_columns(z_ref, low_ref, qkv_ref, at)
            far = mixed_columns(z_ref, low_ref, qkv_ref, at + MIXED // 2)
            mine_ref[:, spot] = jnp.where(first, near, far)
            theirs_ref[:, spot] = jnp.where(first, far, near)

    return call_whole(
        body,
        (
            shape((extent, width), jnp.bfloat16),
            shape((extent, channels), jnp.bfloat16),
            shape((extent, MH), jnp.bfloat16),
            shape((extent, MIXED // 2), jnp.bfloat16),
            shape((extent, MIXED // 2), jnp.bfloat16),
            shape((1, width)),
            shape((CONV_K, channels)),
            shape((1, channels)),
            shape((1, width)),
            shape((1, MH)),
            shape((1, MH)),
        ),
        (
            side,
            qkv_low,
            gated_grad,
            scan,
            act,
            conv_in,
            raw_step,
            gate_z,
            taps,
            bias,
            shift,
            rate,
            skip,
            gain,
            moves,
            allowed,
        ),
        MH * 24 * extent**3,
        scratch=(
            pltpu.VMEM((extent, width), jnp.bfloat16),
            pltpu.VMEM((extent, channels), jnp.float32),
            pltpu.VMEM((MH, extent), jnp.float32),
        ),
        name="mixer_back",
    )


def middle(side, pack, spans, tokens, early, cotangent, valid, gain):
    extent, model = tokens.shape
    width = MH * HD
    q_cols = QH * ATTENTION_HEAD
    groups = pack.shape[0]
    half_ff = FF // 2

    def body(
        side_ref,
        pack_ref,
        tokens_ref,
        early_ref,
        cot_ref,
        valid_ref,
        gain_ref,
        result_ref,
        mine_ref,
        theirs_ref,
        grad_ref,
        gain_out,
        gated_out,
        heads_out,
        *rest,
    ):
        held, sems = rest[:-1], rest[-1]
        loads = []
        for number, (start, count) in enumerate(spans):
            load = pltpu.make_async_copy(
                pack_ref.at[:, pl.ds(start, count), :], held[number], sems.at[number]
            )
            load.start()
            loads.append(load)

        def matrix(number):
            return held[number][...].reshape(groups * spans[number][1], BLOCK)

        first = side_ref[0] == 0

        def both(at, low, high):
            mine_ref[:, at : at + low.shape[1]] = jnp.where(first, low, high)
            theirs_ref[:, at : at + low.shape[1]] = jnp.where(first, high, low)

        is_valid = valid_ref[...] > 0.0
        out_grad = jnp.where(is_valid, cot_ref[...].astype(jnp.float32), 0.0)
        feed_grad = out_grad.astype(jnp.bfloat16)
        loads[0].wait()
        loads[1].wait()
        residual = tokens_ref[...].astype(jnp.float32) + (
            matmul_plain(early_ref[:, :width], matrix(0))
            + matmul_plain(early_ref[:, width : width + q_cols], matrix(1))
        )
        scale = lax.rsqrt(jnp.mean(residual * residual, axis=-1, keepdims=True) + EPSILON)
        gain_val = gain_ref[...]
        normed = (residual * scale * gain_val).astype(jnp.bfloat16)
        mine_ref[:, :model] = normed
        theirs_ref[:, :model] = normed
        loads[6].wait()
        hidden_grad = matmul_right(feed_grad, matrix(6))
        normed_grad = jnp.zeros((extent, model), jnp.float32)
        feed_out = jnp.zeros((extent, model), jnp.float32)
        gates, ups = [], []
        for part in range(2):
            loads[2 + part].wait()
            loads[4 + part].wait()
            columns = slice(part * half_ff, (part + 1) * half_ff)
            gate = matmul_plain(normed, matrix(2 + part))
            up = matmul_plain(normed, matrix(4 + part))
            sig = sigmoid(gate)
            silu = gate * sig
            hidden = (silu * up).astype(jnp.bfloat16)
            at = model + FF + part * half_ff
            mine_ref[:, at : at + half_ff] = hidden
            theirs_ref[:, at : at + half_ff] = hidden
            grad = hidden_grad[:, columns]
            gate_low = (grad * up * (sig * (1.0 + gate * (1.0 - sig)))).astype(jnp.bfloat16)
            up_low = (grad * silu).astype(jnp.bfloat16)
            gates.append(gate_low)
            ups.append(up_low)
            normed_grad = normed_grad + (
                matmul_right(gate_low, matrix(2 + part)) + matmul_right(up_low, matrix(4 + part))
            )
            feed_out = feed_out + matmul_plain(hidden, matrix(6)[columns])
        both(model, *gates)
        both(model + half_ff, *ups)
        result_ref[...] = jnp.where(is_valid, residual + feed_out, 0.0).astype(jnp.bfloat16)
        gain_out[...] = jnp.sum(normed_grad * residual * scale, axis=0, keepdims=True)
        scaled = gain_val * normed_grad
        dots = jnp.mean(scaled * residual, axis=-1, keepdims=True)
        residual_grad = out_grad + (scale * scaled - residual * (scale * scale * scale * dots))
        grad_ref[...] = residual_grad
        branch = residual_grad.astype(jnp.bfloat16)
        both(model + 2 * FF, branch[:, : model // 2], branch[:, model // 2 :])
        gated_out[...] = matmul_right(branch, matrix(0))
        heads_out[...] = matmul_right(branch, matrix(1)).astype(jnp.bfloat16)

    low = jnp.bfloat16
    late = model + 2 * FF + model // 2
    outs = (
        shape((extent, model), low),
        shape((extent, late), low),
        shape((extent, late), low),
        shape((extent, model)),
        shape((1, model)),
        shape((extent, width)),
        shape((extent, q_cols), low),
    )
    args = (side, pack, tokens, early, cotangent, valid, gain)
    spaces = [pltpu.SMEM, pl.ANY] + [pltpu.VMEM] * 5
    return pl.pallas_call(
        body,
        out_shape=outs,
        in_specs=[pl.BlockSpec(memory_space=space) for space in spaces],
        out_specs=[pl.BlockSpec(memory_space=pltpu.VMEM)] * len(outs),
        scratch_shapes=[pltpu.VMEM((groups, count, BLOCK), low) for _, count in spans]
        + [pltpu.SemaphoreType.DMA((len(spans),))],
        compiler_params=pltpu.CompilerParams(vmem_limit_bytes=52 * 1024 * 1024),
        cost_estimate=pl.CostEstimate(
            flops=4 * extent * pack.size, bytes_accessed=2 * pack.size, transcendentals=0
        ),
        name="middle",
    )(*args)


def outer(spots, terms, z_size, apart, after=()):
    rows = [width // (2 * z_size) for _, _, width, _, _ in terms]
    columns = sum(size for _, size in terms[0][4])
    arrays = []
    for lefts, _, _, rights, _ in terms:
        for value in lefts + rights:
            if not any(value is held for held in arrays):
                arrays.append(value)

    def body(spots_ref, *refs):
        first = spots_ref[0] == 0
        quarter = spots_ref[1]

        def ref_of(value):
            return refs[[held is value for held in arrays].index(True)]

        at = 0
        for (lefts, begin, _, rights, segments), size in zip(terms, rows):
            right = jnp.concatenate(
                [
                    jnp.concatenate(
                        [
                            ref_of(value)[:, pl.ds(pl.multiple_of(start + quarter * width, 128), width)]
                            for start, width in segments
                        ],
                        axis=1,
                    )
                    for value in rights
                ],
                axis=0,
            )
            for z in range(z_size):
                low = begin + 2 * z * size
                left = jnp.concatenate(
                    [ref_of(value)[:, low : low + 2 * size] for value in lefts], axis=0
                )
                both = matmul_left(left, right).astype(jnp.bfloat16)
                even, odd = both[:size], both[size:]
                if apart:
                    refs[-2][z, at : at + size, :] = jnp.where(first, even, odd)
                    refs[-1][z, at : at + size, :] = jnp.where(first, odd, even)
                else:
                    refs[-1][z, 0, at : at + size, :] = even
                    refs[-1][z, 1, at : at + size, :] = odd
            at += size

    if apart:
        outs = (shape((z_size, sum(rows), columns), jnp.bfloat16),) * 2
    else:
        outs = (shape((z_size, 2, sum(rows), columns), jnp.bfloat16),)
    tokens = sum(value.shape[0] for value in terms[0][3])
    flops = 4 * z_size * tokens * sum(rows) * columns
    return call_whole(body, outs, (spots, *arrays), flops, name="outer", after=after)


def pack_grads(raw, in_gain, taps, bias, ssm_gain, ff_gain, heads, parts):
    def body(*refs):
        raw_ref, in_ref, taps_ref, bias_ref, ssm_ref, ff_ref = refs[:6]
        out = refs[-1]
        out[...] = jnp.zeros(out.shape, jnp.float32)

        def put(part, row, ref, size):
            begin = part * size
            rows = ref.shape[0]
            for at in range(0, size, 128):
                count = min(128, size - at)
                out[part, row : row + rows, :count] = ref[:, begin + at : begin + at + count]
                row += rows

        for part in range(parts):
            at = 0
            for ref in (raw_ref, in_ref, taps_ref, bias_ref, ssm_ref, ff_ref):
                size = ref.shape[1] // parts
                put(part, at, ref, size)
                at += ref.shape[0] * -(-size // 128)
            for number, ref in enumerate(refs[6:9]):
                out[part, 40 + number : 41 + number, :MH] = ref[...]

    (out,) = call_whole(
        body,
        (shape((parts, 48, 128)),),
        (raw, in_gain, taps, bias, ssm_gain, ff_gain) + tuple(heads),
        0,
        name="pack_grads",
    )
    return out


def unpack_grads(spots, block, heads, sizes):
    count = len(heads)

    def body(spots_ref, block_ref, *refs):
        z = spots_ref[0]
        head_refs, outs = refs[:count], refs[count:]
        total = jnp.zeros(heads[0].shape, jnp.float32)
        for at in range(count):
            step = lax.rem(z + (count - at), count)
            row = head_refs[0][...]
            for number in range(1, count):
                row = jnp.where(step == number, head_refs[number][...], row)
            total = total + row
        outs[0][...] = block_ref[:MH, :].T
        at = MH
        for out, (rows, size) in zip(outs[1:], sizes):
            for begin in range(0, size, 128):
                width = min(128, size - begin)
                out[:, begin : begin + width] = block_ref[at : at + rows, :width]
                at += rows
        for number, out in enumerate(outs[1 + len(sizes) :]):
            out[...] = total[number : number + 1, :MH]

    return call_whole(
        body,
        (shape((128, MH)),) + tuple(shape(size) for size in sizes) + (shape((1, MH)),) * 3,
        (spots, block) + tuple(heads),
        0,
        name="unpack_grads",
    )


def finish(spots, pieces, outs, extra=None):
    size = pieces[0].shape[1]

    def body(spots_ref, *refs):
        pieces_ref = refs[:4]
        out_refs = refs[4 + (extra is not None) :]
        y, c = spots_ref[0], spots_ref[1]
        for quarter in range(4):
            same_y = y == quarter // 2
            same_c = c == quarter % 2
            for out_ref, (_, _, moves) in zip(out_refs, outs):
                for source, rows, column, count in moves[quarter]:
                    own, by_c, by_y, by_yc = [
                        ref[rows, source : source + count] for ref in pieces_ref
                    ]
                    value = jnp.where(
                        same_y,
                        jnp.where(same_c, own, by_c),
                        jnp.where(same_c, by_y, by_yc),
                    )
                    out_ref[:, column : column + count] = value.astype(jnp.float32)
        if extra is not None:
            out_refs[0][:, outs[0][1] - extra.shape[1] :] = refs[4][...]

    args = (spots,) + tuple(pieces) + (() if extra is None else (extra,))
    return call_whole(
        body, tuple(shape((rows, columns)) for rows, columns, _ in outs), args, 0, name="finish"
    )


def block_masks(segment, position):
    extent = segment.shape[0]
    slot = jnp.arange(extent, dtype=jnp.int32)
    moves = [jnp.ones((extent,), jnp.bool_)]
    for offset in range(1, CONV_K):
        moves.append((slot >= offset) & (jnp.roll(segment, offset) == segment))
    half = ATTENTION_HEAD // 2
    inverse = ROPE_BASE ** (-jnp.arange(half, dtype=jnp.float32) / half)
    angle = position.astype(jnp.float32)[:, None] * inverse[None, :]
    return (
        jnp.stack(moves, axis=1).astype(jnp.float32),
        causal_allowed(segment).astype(jnp.float32),
        jnp.tile(jnp.cos(angle), (1, 4)),
        jnp.tile(jnp.sin(angle), (1, 4)),
    )


def forward_pass(side, feed_grad, tokens_f, gains, mats, a_log, dt_bias, skip_d, segment, position):
    in_gain, conv_w, conv_b, ssm_gain, _, w_raw = gains
    w_conv, w_z, w_qkv = mats
    moves, allowed, cosine, sine = block_masks(segment, position)
    normed_f, pull_norm_one = jax.vjp(rms_scale, tokens_f, in_gain.astype(jnp.float32))
    normed = normed_f.astype(jnp.bfloat16)
    qkv = matmul_plain(normed, w_qkv)
    low, heads_out = attention_front(qkv, cosine, sine, allowed)
    conv_in = matmul_plain(normed, w_conv)
    raw_step = matmul_right(normed, w_raw)
    gate_z = matmul_plain(normed, w_z)
    mixer_args = (
        conv_in,
        raw_step,
        gate_z,
        conv_w.astype(jnp.float32),
        conv_b.astype(jnp.float32)[None],
        dt_bias[None],
        a_log[None],
        jnp.repeat(skip_d, HD)[None],
        ssm_gain.astype(jnp.float32)[None],
        moves,
        allowed,
    )
    act, scan, early_mine, early_theirs = mixer_front(
        side, heads_out, normed, feed_grad, *mixer_args
    )
    kept = (pull_norm_one, normed, mixer_args, act, scan, low, (cosine, sine, allowed))
    return (early_mine, early_theirs, kept)


def backward_pass(side, grads, w_raw, mats, kept):
    w_conv, w_z, w_qkv = mats
    pull_norm_one, normed, mixer_args, act, scan, low, turn_args = kept
    residual_grad, gated_grad, heads_grad = grads
    qkv_low = attention_back(low, heads_grad, *turn_args)
    (
        z_low,
        conv_low,
        raw_low,
        mixed_mine,
        mixed_theirs,
        grad_ssm_gain,
        grad_conv_w,
        grad_conv_b,
        skip_lanes,
        grad_dt_bias,
        grad_a_log,
    ) = mixer_back(side, qkv_low, gated_grad, scan, act, *mixer_args)
    grad_skip = jnp.sum(skip_lanes.reshape(MH, HD), axis=1)
    normed_grad = (
        matmul_right(qkv_low, w_qkv)
        + matmul_right(z_low, w_z)
        + matmul_right(conv_low, w_conv)
        + matmul_plain(raw_low, w_raw)
    )
    token_part, grad_in_gain = pull_norm_one(normed_grad)
    tokens_grad = (residual_grad + token_part).astype(jnp.bfloat16)
    raw_rows = matmul_left(raw_low, normed)
    small = (
        raw_rows,
        grad_in_gain[None],
        grad_conv_w,
        grad_conv_b,
        grad_ssm_gain,
        grad_a_log,
        grad_dt_bias,
        grad_skip[None],
    )
    return (tokens_grad, (mixed_mine, mixed_theirs), small)


AXES = ("shard", "replica")


def place(pieces, positions, dim, count):
    shape = list(pieces[0].shape)
    shape[dim] = count
    total = len(pieces)

    def body(where, *refs):
        out, held, sems = refs[total], refs[total + 1 : 2 * total + 1], refs[-1]
        loads, stores = [], []
        for number in range(total):
            spot = (slice(None),) * dim + (pl.ds(where[number], 1),)
            loads.append(
                pltpu.make_async_copy(refs[number], held[number], sems.at[0, number])
            )
            stores.append(
                pltpu.make_async_copy(held[number], out.at[spot], sems.at[1, number])
            )
        for load in loads:
            load.start()
        for load, store in zip(loads, stores):
            load.wait()
            store.start()
        for store in stores:
            store.wait()

    moved = 2 * sum(piece.size * piece.dtype.itemsize for piece in pieces)
    return pl.pallas_call(
        body,
        out_shape=jax.ShapeDtypeStruct(tuple(shape), pieces[0].dtype),
        in_specs=[pl.BlockSpec(memory_space=pltpu.SMEM)]
        + [pl.BlockSpec(memory_space=pl.ANY)] * total,
        out_specs=pl.BlockSpec(memory_space=pl.ANY),
        scratch_shapes=[pltpu.VMEM(piece.shape, piece.dtype) for piece in pieces]
        + [pltpu.SemaphoreType.DMA((2, total))],
        compiler_params=pltpu.CompilerParams(vmem_limit_bytes=24 * 1024 * 1024),
        cost_estimate=pl.CostEstimate(flops=0, bytes_accessed=moved, transcendentals=0),
        name="place",
    )(jnp.stack(positions).astype(jnp.int32), *pieces)


class Links:
    def __init__(self, shards_of, copies):
        self.z_size = shards_of // 2
        shard = lax.axis_index("shard")
        replica = lax.axis_index("replica")
        self.z, self.x = shard // 2, shard % 2
        self.y, self.c = replica // 2, replica % 2
        everyone = [(s, r) for s in range(shards_of) for r in range(copies)]

        def table(step):
            return [(s * copies + r, step(s, r)) for s, r in everyone]

        self.tables = {
            "x": table(lambda s, r: (s ^ 1) * copies + r),
            "y": table(lambda s, r: s * copies + (r ^ 2)),
            "c": table(lambda s, r: s * copies + (r ^ 1)),
            "z": table(lambda s, r: ((s + 2) % shards_of) * copies + r),
        }

    def send(self, value, axis):
        return lax.ppermute(value, AXES, self.tables[axis])

    def spread(self, value, axis):
        if axis == "z":
            pieces, spots = [value], [self.z]
            for step in range(1, self.z_size):
                pieces.append(self.send(pieces[-1], "z"))
                spots.append((self.z + self.z_size - step) % self.z_size)
            return place(pieces, spots, 0, self.z_size)
        spot = {"x": self.x, "y": self.y, "c": self.c}[axis]
        return place([value, self.send(value, axis)], [spot, 1 - spot], "zxyc".index(axis), 2)

    def gather(self, own, order):
        rows, columns = own.shape
        cut = own.reshape(1, 1, 2, 2, rows // 4, columns)
        cut = lax.dynamic_slice_in_dim(cut, self.c, 1, 3)
        if "y" in order:
            cut = lax.dynamic_slice_in_dim(cut, self.y, 1, 2)
        for axis in order:
            cut = self.spread(cut, axis)
        return cut.reshape(-1, columns)

    def gather_small(self, own):
        other = self.send(own, "x")
        pair = jnp.stack(
            [jnp.where(self.x == 0, own, other), jnp.where(self.x == 0, other, own)]
        )
        pieces = [pair]
        for _ in range(1, self.z_size):
            pieces.append(self.send(pieces[-1], "z"))
        stacked = jnp.stack(pieces)
        return jnp.concatenate(
            [
                lax.dynamic_index_in_dim(stacked, (self.z + self.z_size - at) % self.z_size, 0, False)
                for at in range(self.z_size)
            ]
        )

    def near(self, mine, theirs):
        values = [mine, self.send(theirs, "y")]
        return values + [self.send(value, "c") for value in values]

    def around(self, block):
        total = block(0).astype(jnp.bfloat16)
        for step in range(1, self.z_size):
            arrived = self.send(total, "z")
            total = (arrived.astype(jnp.float32) + block(step)).astype(jnp.bfloat16)
        return total

    def at_step(self, value, step):
        at = (self.z + 2 * self.z_size - 1 - step) % self.z_size
        return lax.dynamic_index_in_dim(value, at, 0, False).astype(jnp.float32)

    def reduce_small(self, value):
        value = value + self.send(value, "c")
        value = value + self.send(value, "y")
        value = value.reshape(self.z_size, 2, 48, 128)
        mine = lax.dynamic_index_in_dim(value, self.x, 1, False)
        theirs = lax.dynamic_index_in_dim(value, 1 - self.x, 1, False)
        value = mine + self.send(theirs, "x")
        heads = [value[0, 40:]]
        total = self.at_step(value, 0)
        for step in range(1, self.z_size):
            arrived = self.send(total, "z")
            heads.append(arrived[40:])
            total = jnp.concatenate([arrived[:40] + self.at_step(value, step)[:40], arrived[40:]])
        return total, heads

    def quarters(self, total):
        by_y = self.send(total, "y")
        return (total, self.send(total, "c"), by_y, self.send(by_y, "c"))

    def reduce_xz(self, mine, theirs):
        moved = self.send(theirs, "x")
        return self.quarters(
            self.around(lambda step: self.at_step(mine, step) + self.at_step(moved, step))
        )

    def reduce_zx(self, value):
        total = self.around(lambda step: self.at_step(value, step))
        mine = lax.dynamic_index_in_dim(total, self.x, 0, False)
        theirs = lax.dynamic_index_in_dim(total, 1 - self.x, 0, False)
        moved = self.send(theirs, "x")
        return self.quarters(
            (mine.astype(jnp.float32) + moved.astype(jnp.float32)).astype(jnp.bfloat16)
        )


def pack_small(in_gain, conv_w, conv_b, ssm_gain, ff_gain, raw):
    def rows(value):
        flat = value.reshape(-1)
        return jnp.pad(flat, (0, -flat.shape[0] % 128)).reshape(-1, 128)

    packed = jnp.concatenate([rows(v) for v in (raw.T, in_gain, conv_w, conv_b, ssm_gain, ff_gain)])
    return jnp.pad(packed, ((0, -packed.shape[0] % 16), (0, 0)))


def unpack_small(gathered, own):
    in_gain, conv_w, conv_b, ssm_gain, ff_gain, raw = own
    parts = gathered.shape[0]
    at = 0
    out = []
    for value in (raw.T, in_gain, conv_w, conv_b, ssm_gain, ff_gain):
        count = -(-value.size // 128)
        flat = gathered[:, at : at + count].reshape(parts, -1)[:, : value.size]
        at += count
        shaped = flat.reshape((parts,) + value.shape)
        if value.ndim == 1:
            out.append(shaped.reshape(-1))
        else:
            out.append(shaped.transpose(1, 0, 2).reshape(value.shape[0], -1))
    return tuple(out[1:]) + (out[0],)


def shards(
    copies,
    tokens,
    cotangent,
    seq_lengths,
    seq_starts,
    in_gain,
    w_in,
    conv_w,
    conv_b,
    a_log,
    dt_bias,
    skip_d,
    ssm_gain,
    w_out,
    w_query,
    w_key,
    w_value,
    w_attn_out,
    ff_gain,
    w_gate,
    w_up,
    w_down,
):
    parts = MH * HD // w_out.shape[0]
    width = MH * HD
    channels = width + 2 * NS
    quick = parts == 8 and copies == 4
    links = Links(parts, copies)
    own_small = (in_gain, conv_w, conv_b, ssm_gain, ff_gain, w_in[:, width + channels :])
    own = (
        w_in[:, width : width + channels],
        w_in[:, :width],
        jnp.concatenate([w_query, w_key, w_value], axis=1),
    )
    blocks = (
        w_out,
        w_attn_out,
        w_gate[:, :BLOCK],
        w_gate[:, BLOCK:],
        w_up[:, :BLOCK],
        w_up[:, BLOCK:],
        w_down,
    )
    pieces = 4 if quick else 1
    turn = links.y * 2 + links.c if quick else 0
    cuts, spans, at = [], [], 0
    for value in blocks:
        count = value.shape[0] // pieces
        cuts.append(lax.dynamic_slice_in_dim(value, turn * count, count, 0))
        spans.append((at, count))
        at += count
    pack = jnp.concatenate(cuts, axis=0)
    if quick:
        orders = ("zxyc", "zyxc", "xzc")
        small_all = links.gather_small(pack_small(*own_small))
        mats = tuple(links.gather(value, order) for value, order in zip(own, orders))
        pack = lax.all_gather(pack, AXES, axis=0)
    else:
        small_all = lax.all_gather(pack_small(*own_small), "shard", axis=0)
        mats = tuple(lax.all_gather(value, "shard", axis=0, tiled=True) for value in own)
        pack = lax.all_gather(pack, "shard", axis=0)
    gains = unpack_small(small_all, own_small)
    segment, position = layout(seq_lengths[0], seq_starts[0], tokens.shape[0])
    side = jnp.stack([links.y if quick else jnp.int32(0)]).astype(jnp.int32)
    valid = (segment >= 0).astype(jnp.float32)[:, None]
    feed_grad = jnp.where(valid > 0.0, cotangent, 0.0).astype(jnp.bfloat16)
    early_mine, early_theirs, kept = forward_pass(
        side,
        feed_grad,
        tokens.astype(jnp.float32),
        gains,
        mats,
        a_log,
        dt_bias,
        skip_d,
        segment,
        position,
    )
    (
        result,
        late_mine,
        late_theirs,
        residual_grad,
        grad_ff_gain,
        gated_grad,
        heads_grad,
    ) = middle(
        side, pack, spans, tokens, early_mine, cotangent, valid, gains[4].astype(jnp.float32)[None]
    )
    tokens_grad, (mixed_mine, mixed_theirs), small = backward_pass(
        side, (residual_grad, gated_grad, heads_grad), gains[5], mats, kept
    )
    here = lax.axis_index("shard")
    model = w_in.shape[0] * parts

    def mine(value):
        size = value.shape[-1] // parts
        return lax.dynamic_slice_in_dim(value, here * size, size, value.ndim - 1)

    q_cols = QH * ATTENTION_HEAD
    k_cols = KVH * ATTENTION_HEAD
    out_rows, attn_rows = w_out.shape[0], w_attn_out.shape[0]
    down_rows, model_rows = w_down.shape[0], w_in.shape[0]
    if quick:
        quarter = BLOCK // 4
        whole = slice(None)

        def plain(rows):
            return [[(0, rows, number * quarter, quarter)] for number in range(4)]

        half_ff, quarter_ff = FF // 2, FF // 4
        edges = (0, width + channels, width + channels + q_cols, MIXED - k_cols, MIXED)
        mixed_moves = [[[] for _ in range(4)] for _ in range(4)]
        for number in range(4):
            for index in range(4):
                low = max(edges[index], number * BLOCK)
                high = min(edges[index + 1], (number + 1) * BLOCK)
                if low < high:
                    mixed_moves[index][number].append(
                        (low - number * BLOCK, whole, low - edges[index], high - low)
                    )
        spots = jnp.stack([links.y, links.c]).astype(jnp.int32)
        early_four = links.near(early_mine, early_theirs)
        late_four = links.near(late_mine, late_theirs)
        mixed_four = links.near(mixed_mine, mixed_theirs)
        place_spots = jnp.stack([links.x, links.c]).astype(jnp.int32)
        at_normed = width + q_cols
        at_hidden = model + FF
        packed = pack_grads(*small[:5], grad_ff_gain, small[5:], parts)
        feed_parts = outer(
            place_spots,
            [
                (
                    late_four,
                    0,
                    model,
                    late_four,
                    [(model, quarter_ff), (model + half_ff, quarter_ff)],
                )
            ],
            links.z_size,
            True,
        )
        out_right = (late_four, [(at_hidden + FF, quarter)])
        (out_parts,) = outer(
            place_spots,
            [
                (early_four, 0, width) + out_right,
                (early_four, width, q_cols) + out_right,
                (late_four, at_hidden, FF, early_four, [(at_normed + model, quarter)]),
            ],
            links.z_size,
            False,
        )
        mixed_parts = outer(
            place_spots,
            [(early_four, at_normed, model, mixed_four, [(0, BLOCK)])],
            links.z_size,
            True,
        )
        block, head_rows = links.reduce_small(packed)
        raw_part, *totals = unpack_grads(
            jnp.stack([links.z]).astype(jnp.int32),
            block,
            head_rows,
            [(value.shape[0], value.shape[1] // parts) for value in small[1:5]]
            + [(1, model // parts)],
        )
        totals = [totals[0][0], totals[1]] + [value[0] for value in totals[2:]]
        gate, up = finish(
            spots,
            links.reduce_xz(*feed_parts),
            [
                (
                    model_rows,
                    FF,
                    [[(at, whole, number * quarter_ff, quarter_ff)] for number in range(4)],
                )
                for at in (0, quarter_ff)
            ],
        )
        out, attn, down = finish(
            spots,
            links.reduce_zx(out_parts),
            [
                (rows, BLOCK, plain(slice(at, at + rows)))
                for rows, at in (
                    (out_rows, 0),
                    (attn_rows, out_rows),
                    (down_rows, out_rows + attn_rows),
                )
            ],
        )
        mixed_pieces = links.reduce_xz(*mixed_parts)
        projection, query, key, value = finish(
            spots,
            mixed_pieces,
            [
                (model_rows, columns, moves)
                for columns, moves in zip(
                    (width + channels + MH, q_cols, k_cols, k_cols), mixed_moves
                )
            ],
            raw_part,
        )
    else:

        def joined(first, second):
            return jnp.concatenate([first, second], axis=1)

        def share(left, right):
            part = lax.psum_scatter(
                matmul_left(left, right).astype(jnp.bfloat16),
                "shard",
                scatter_dimension=0,
                tiled=True,
            )
            return lax.psum(part, "replica").astype(jnp.float32)

        half_ff = FF // 2
        branch = joined(late_mine[:, model + 2 * FF :], late_theirs[:, model + 2 * FF :])
        mixed = share(kept[1], joined(mixed_mine, mixed_theirs))
        hidden = late_mine[:, model + FF : model + 2 * FF]
        down = share(hidden, feed_grad)
        normed_two = late_mine[:, :model]
        gate, up = [
            share(
                normed_two,
                joined(late_mine[:, at : at + half_ff], late_theirs[:, at : at + half_ff]),
            )
            for at in (model, model + half_ff)
        ]
        out = share(early_mine[:, :width], branch)
        attn = share(early_mine[:, width : width + q_cols], branch)
        summed = [lax.psum(value, AXES) for value in small + (grad_ff_gain,)]
        raw_part = mine(summed[0]).T
        totals = [mine(summed[1])[0], mine(summed[2])]
        totals += [mine(summed[at])[0] for at in (3, 4, 8)]
        totals += [value[0] for value in summed[5:8]]
        at = width + channels
        projection = joined(mixed[:, :at], raw_part)
        query = mixed[:, at : at + q_cols]
        key = mixed[:, at + q_cols : at + q_cols + k_cols]
        value = mixed[:, at + q_cols + k_cols :]
    return (
        result,
        tokens_grad,
        totals[0],
        projection,
        totals[1],
        totals[2],
        totals[5],
        totals[6],
        totals[7],
        totals[3],
        out,
        query,
        key,
        value,
        attn,
        totals[4],
        gate,
        up,
        down,
    )


def solution(mesh):
    in_specs = (
        P(("shard", "replica"), None),
        P(("shard", "replica"), None),
        P(("shard", "replica"), None),
        P(("shard", "replica"), None),
        P("shard"),
        P("shard", None),
        P(None, "shard"),
        P("shard"),
        P(),
        P(),
        P(),
        P("shard"),
        P("shard", None),
        P("shard", None),
        P("shard", None),
        P("shard", None),
        P("shard", None),
        P("shard"),
        P("shard", None),
        P("shard", None),
        P("shard", None),
    )
    out_specs = (
        P(("shard", "replica"), None),
        P(("shard", "replica"), None),
        P("shard"),
        P("shard", None),
        P(None, "shard"),
        P("shard"),
        P(),
        P(),
        P(),
        P("shard"),
        P("shard", None),
        P("shard", None),
        P("shard", None),
        P("shard", None),
        P("shard", None),
        P("shard"),
        P("shard", None),
        P("shard", None),
        P("shard", None),
    )

    def local(*args):
        return shards(mesh.shape["replica"], *args)

    return jax.shard_map(local, mesh=mesh, in_specs=in_specs, out_specs=out_specs, check_vma=False)
```

```python
import jax
import jax.numpy as jnp
from jax import lax
from jax.experimental import pallas as pl
from jax.experimental.pallas import tpu as pltpu
from jax.sharding import PartitionSpec as P

FF = 2048
MH = 24
HD = 64
NS = 128
QH = 8
KVH = 2
ATTENTION_HEAD = 64
CONV_K = 4
MIXED = 2 * MH * HD + 2 * NS + (QH + 2 * KVH) * ATTENTION_HEAD
BLOCK = 1024


EPSILON = 1e-05
ROPE_BASE = 100000000000.0


def matmul_plain(left, right):
    return jnp.dot(left, right, preferred_element_type=jnp.float32)


def matmul_left(left, right):
    return lax.dot_general(
        left, right, (((0,), (0,)), ((), ())), preferred_element_type=jnp.float32
    )


def matmul_right(left, right):
    return lax.dot_general(
        left, right, (((1,), (1,)), ((), ())), preferred_element_type=jnp.float32
    )


def rms_scale(values, gain):
    return values * lax.rsqrt(jnp.mean(values * values, axis=-1, keepdims=True) + EPSILON) * gain


def layout(lengths, starts, extent):
    position = jnp.arange(extent, dtype=jnp.int32)
    inside = (position[:, None] >= starts[None, :]) & (
        position[:, None] < starts[None, :] + lengths[None, :]
    )
    number = jnp.arange(1, lengths.shape[0] + 1, dtype=jnp.int32)
    segment = jnp.sum(jnp.where(inside, number[None, :], 0), axis=1) - 1
    first = jnp.sum(jnp.where(inside, starts[None, :], 0), axis=1)
    return (segment, position - first)


def causal_allowed(segment):
    position = jnp.arange(segment.shape[0], dtype=jnp.int32)
    return (segment[:, None] == segment[None, :]) & (position[:, None] >= position[None, :])


def swiglu(gate_val, up_val):
    return jax.nn.silu(gate_val) * up_val


def sigmoid(value):
    return 1.0 / (1.0 + jnp.exp(-value))


def dot_exact(left, right, dims):
    return lax.dot_general(
        left,
        right,
        (dims, ((), ())),
        precision=lax.Precision.HIGHEST,
        preferred_element_type=jnp.float32,
    )


def lane_half(rows):
    return lax.broadcasted_iota(jnp.int32, (rows, 2 * HD), 1) < HD


def pick(half, first, second):
    return jnp.where(half, first, second)


MICROS = {
    "attention_front": 2.9,
    "attention_back": 3.8,
    "mixer_front": 5.5,
    "mixer_back": 11.5,
    "outer": 3.2,
    "finish": 2.3,
    "pack_grads": 1.0,
    "unpack_grads": 1.0,
    "hold": 1.5,
    "stack": 1.5,
    "middle": 15.8,
    "place": 2.3,
    "cut_rows": 1.5,
}


def cost(name):
    return pl.CostEstimate(
        flops=int(MICROS[name] * 1.1e9), bytes_accessed=0, transcendentals=0
    )


def call_whole(body, outs, args, scratch=(), name="kernel", after=()):
    count = len(args)

    def ordered(*refs):
        body(*refs[:count], *refs[count + len(after) :])

    return pl.pallas_call(
        ordered,
        out_shape=outs,
        in_specs=[
            pl.BlockSpec(memory_space=pltpu.SMEM if arg.dtype == jnp.int32 else pltpu.VMEM)
            for arg in args
        ]
        + [pl.BlockSpec(memory_space=pl.ANY)] * len(after),
        out_specs=[pl.BlockSpec(memory_space=pltpu.VMEM)] * len(outs),
        scratch_shapes=list(scratch),
        compiler_params=pltpu.CompilerParams(vmem_limit_bytes=40 * 1024 * 1024),
        cost_estimate=cost(name),
        name=name,
    )(*args, *after)


def shape(dims, kind=jnp.float32):
    return jax.ShapeDtypeStruct(dims, kind)


def turned(values, cosine, sine, back):
    width = values.shape[1]
    quarter = lax.broadcasted_iota(jnp.int32, values.shape, 1) % ATTENTION_HEAD
    half = ATTENTION_HEAD // 2
    swapped = jnp.where(
        quarter < half,
        -pltpu.roll(values, width - half, 1),
        pltpu.roll(values, half, 1),
    )
    return values * cosine - swapped * sine if back else values * cosine + swapped * sine


def doubled(values, half):
    moved = pltpu.roll(values, ATTENTION_HEAD, 1)
    return (pick(half, values, moved), pick(half, moved, values))


def masked_dot(pair, half, keep_first, other):
    zero = jnp.zeros_like(pair)
    chosen = jnp.where(half, pair, zero) if keep_first else jnp.where(half, zero, pair)
    return matmul_right(chosen, other)


def softmax_rows(scores, allowed):
    scores = jnp.where(allowed, scores * ATTENTION_HEAD ** (-0.5), -1e30)
    raised = jnp.exp(scores - jnp.max(scores, axis=-1, keepdims=True))
    return raised / jnp.sum(raised, axis=-1, keepdims=True)


def attention_front(first, second, cosine, sine, allowed):
    extent = first.shape[0]
    pair = 2 * ATTENTION_HEAD
    pairs = QH // 2
    at_key = first.shape[1] - 2 * pair
    at_query = second.shape[1] - pairs * pair

    def body(first_ref, second_ref, cos_ref, sin_ref, allowed_ref, low_ref, out_ref):
        half = lane_half(extent)
        can = allowed_ref[...] > 0.0
        cos_val, sin_val = cos_ref[...], sin_ref[...]
        key = turned(first_ref[:, at_key : at_key + pair], cos_val, sin_val, False)
        key = key.astype(jnp.bfloat16)
        value = first_ref[:, at_key + pair :].astype(jnp.bfloat16)
        low_ref[:, pairs * pair : (pairs + 1) * pair] = key
        low_ref[:, (pairs + 1) * pair :] = value
        keys = [k.astype(jnp.bfloat16) for k in doubled(key.astype(jnp.float32), half)]
        values = [v.astype(jnp.bfloat16) for v in doubled(value.astype(jnp.float32), half)]
        for number in range(pairs):
            spot = slice(number * pair, (number + 1) * pair)
            begin = at_query + number * pair
            query = turned(second_ref[:, begin : begin + pair], cos_val, sin_val, False)
            query = query.astype(jnp.bfloat16)
            low_ref[:, spot] = query
            group = number * KVH // pairs
            results = []
            for first in (True, False):
                scores = masked_dot(query, half, first, keys[group])
                probs = softmax_rows(scores, can).astype(jnp.bfloat16)
                results.append(matmul_plain(probs, values[group]))
            out_ref[:, spot] = pick(half, *results).astype(jnp.bfloat16)

    return call_whole(
        body,
        (
            shape((extent, (pairs + 2) * pair), jnp.bfloat16),
            shape((extent, pairs * pair), jnp.bfloat16),
        ),
        (first, second, cosine, sine, allowed),
        name="attention_front",
    )


def attention_back(low, heads_grad, cosine, sine, allowed):
    extent = low.shape[0]
    pair = 2 * ATTENTION_HEAD
    pairs = QH // 2
    scale = ATTENTION_HEAD ** (-0.5)

    def body(low_ref, grad_ref, cos_ref, sin_ref, allowed_ref, out_ref):
        half = lane_half(extent)
        can = allowed_ref[...] > 0.0
        cos_val, sin_val = cos_ref[...], sin_ref[...]
        key = low_ref[:, pairs * pair : (pairs + 1) * pair].astype(jnp.float32)
        value = low_ref[:, (pairs + 1) * pair :].astype(jnp.float32)
        keys = [k.astype(jnp.bfloat16) for k in doubled(key, half)]
        values = [v.astype(jnp.bfloat16) for v in doubled(value, half)]
        key_sums = [jnp.zeros((extent, pair), jnp.float32) for _ in range(KVH)]
        value_sums = [jnp.zeros((extent, pair), jnp.float32) for _ in range(KVH)]
        for number in range(pairs):
            spot = slice(number * pair, (number + 1) * pair)
            query = low_ref[:, spot]
            grad = grad_ref[:, spot]
            group = number * KVH // pairs
            q_parts, k_parts, v_parts = [], [], []
            for first in (True, False):
                probs = softmax_rows(masked_dot(query, half, first, keys[group]), can)
                prob_grad = masked_dot(grad, half, first, values[group])
                v_parts.append(matmul_left(probs.astype(jnp.bfloat16), grad))
                inner = jnp.sum(probs * prob_grad, axis=-1, keepdims=True)
                score_grad = (probs * (prob_grad - inner)).astype(jnp.bfloat16)
                q_parts.append(matmul_plain(score_grad, keys[group]))
                k_parts.append(matmul_left(score_grad, query))
            key_sums[group] = key_sums[group] + pick(half, *k_parts)
            value_sums[group] = value_sums[group] + pick(half, *v_parts)
            query_grad = turned(pick(half, *q_parts) * scale, cos_val, sin_val, True)
            out_ref[:, spot] = query_grad.astype(jnp.bfloat16)

        def both(sums):
            return pick(half, *[s + pltpu.roll(s, ATTENTION_HEAD, 1) for s in sums])

        key_grad = turned(both(key_sums) * scale, cos_val, sin_val, True)
        out_ref[:, pairs * pair : (pairs + 1) * pair] = key_grad.astype(jnp.bfloat16)
        out_ref[:, (pairs + 1) * pair :] = both(value_sums).astype(jnp.bfloat16)

    (out,) = call_whole(
        body,
        (shape(low.shape, jnp.bfloat16),),
        (low, heads_grad, cosine, sine, allowed),
        name="attention_back",
    )
    return out


def conv_sum(conv_ref, taps_ref, bias_ref, moves_ref, spot):
    value = conv_ref[:, spot]
    total = bias_ref[:, spot] + taps_ref[CONV_K - 1 : CONV_K, spot] * value
    for offset in range(1, CONV_K):
        moved = pltpu.roll(value, offset, 0) * moves_ref[:, offset : offset + 1]
        total = total + taps_ref[CONV_K - 1 - offset : CONV_K - offset, spot] * moved
    return total


def steps_of(raw_ref, shift_ref, rate_ref):
    moved = raw_ref[...] + shift_ref[...]
    step = jnp.maximum(moved, 0.0) + jnp.log1p(jnp.exp(-jnp.abs(moved)))
    rate = -jnp.exp(rate_ref[...])
    return moved, step, rate


def decay_sums(decay, extent):
    row = lax.broadcasted_iota(jnp.int32, (extent, extent), 0)
    column = lax.broadcasted_iota(jnp.int32, (extent, extent), 1)
    lower = jnp.where(row >= column, 1.0, 0.0)
    by_column = dot_exact(lower, decay, ((1,), (0,)))
    by_row = dot_exact(decay, lower, ((0,), (1,)))
    return by_column, by_row, lower


def decay_of(by_column, by_row, head, can):
    spread = by_column[:, head : head + 1] - by_row[head : head + 1, :]
    return jnp.where(can, jnp.exp(jnp.where(can, spread, 0.0)), 0.0)


def mixer_front(
    side,
    heads_out,
    normed,
    feed_grad,
    conv_in,
    raw_step,
    gate_z,
    taps,
    bias,
    shift,
    rate,
    skip,
    gain,
    moves,
    allowed,
):
    extent = conv_in.shape[0]
    at_normed = MH * HD + heads_out.shape[1]
    at_feed = at_normed + normed.shape[1]
    half_feed = feed_grad.shape[1] // 2
    width = MH * HD
    pair = 2 * HD

    def body(
        side_ref,
        heads_ref,
        normed_ref,
        feed_ref,
        conv_ref,
        raw_ref,
        gate_ref,
        taps_ref,
        bias_ref,
        shift_ref,
        rate_ref,
        skip_ref,
        gain_ref,
        moves_ref,
        allowed_ref,
        act_ref,
        scan_ref,
        mine_ref,
        theirs_ref,
    ):
        side_first = side_ref[0] == 0
        low, high = feed_ref[:, :half_feed], feed_ref[:, half_feed:]
        for ref in (mine_ref, theirs_ref):
            ref[:, MH * HD : at_normed] = heads_ref[...]
            ref[:, at_normed:at_feed] = normed_ref[...]
        mine_ref[:, at_feed:] = jnp.where(side_first, low, high)
        theirs_ref[:, at_feed:] = jnp.where(side_first, high, low)
        half = lane_half(extent)
        can = allowed_ref[...] > 0.0
        for at in range(0, width + 2 * NS, 256):
            spot = slice(at, at + 256)
            total = conv_sum(conv_ref, taps_ref, bias_ref, moves_ref, spot)
            act_ref[:, spot] = (total * sigmoid(total)).astype(jnp.bfloat16)
        _, step, step_rate = steps_of(raw_ref, shift_ref, rate_ref)
        by_column, by_row, _ = decay_sums(step * step_rate, extent)
        inner = matmul_right(act_ref[:, width + NS :], act_ref[:, width : width + NS])
        squares = jnp.zeros((extent, 1), jnp.float32)
        for number in range(MH // 2):
            spot = slice(number * pair, (number + 1) * pair)
            heads = act_ref[:, spot].astype(jnp.float32)
            steps = pick(half, step[:, 2 * number : 2 * number + 1], step[:, 2 * number + 1 : 2 * number + 2])
            scaled = (heads * steps).astype(jnp.bfloat16)
            results = []
            for head in (2 * number, 2 * number + 1):
                weights = (decay_of(by_column, by_row, head, can) * inner).astype(jnp.bfloat16)
                results.append(matmul_plain(weights, scaled))
            scan = pick(half, *results) + skip_ref[:, spot] * heads
            scan_ref[:, spot] = scan
            gate = gate_ref[:, spot]
            value = scan * (gate * sigmoid(gate))
            squares = squares + jnp.sum(value * value, axis=-1, keepdims=True)
        scale = lax.rsqrt(squares / width + EPSILON)
        for number in range(MH // 2):
            spot = slice(number * pair, (number + 1) * pair)
            gate = gate_ref[:, spot]
            value = scan_ref[:, spot] * (gate * sigmoid(gate))
            gated = (value * scale * gain_ref[:, spot]).astype(jnp.bfloat16)
            mine_ref[:, spot] = gated
            theirs_ref[:, spot] = gated

    return call_whole(
        body,
        (
            shape((extent, width + 2 * NS), jnp.bfloat16),
            shape((extent, width)),
            shape((extent, at_feed + half_feed), jnp.bfloat16),
            shape((extent, at_feed + half_feed), jnp.bfloat16),
        ),
        (side, heads_out, normed, feed_grad, conv_in, raw_step, gate_z, taps, bias, shift, rate, skip, gain, moves, allowed),
        name="mixer_front",
    )


def mixer_back(
    after,
    side,
    normed,
    qkv_low,
    gated_grad,
    scan,
    act,
    conv_in,
    raw_step,
    gate_z,
    taps,
    bias,
    shift,
    rate,
    skip,
    gain,
    moves,
    allowed,
):
    extent = conv_in.shape[0]
    width = MH * HD
    channels = width + 2 * NS
    pair = 2 * HD

    def body(
        side_ref,
        normed_ref,
        qkv_ref,
        grad_ref,
        scan_ref,
        act_ref,
        conv_ref,
        raw_ref,
        gate_ref,
        taps_ref,
        bias_ref,
        shift_ref,
        rate_ref,
        skip_ref,
        gain_ref,
        moves_ref,
        allowed_ref,
        z_ref,
        low_ref,
        raw_low_ref,
        raw_out,
        mine_ref,
        theirs_ref,
        gain_out,
        taps_out,
        bias_out,
        skip_out,
        shift_out,
        rate_out,
        scan_grad_ref,
        act_grad_ref,
        row_ref,
    ):
        half = lane_half(extent)
        can = allowed_ref[...] > 0.0
        squares = jnp.zeros((extent, 1), jnp.float32)
        dots = jnp.zeros((extent, 1), jnp.float32)
        for at in range(0, width, 256):
            spot = slice(at, at + 256)
            gate = gate_ref[:, spot]
            value = scan_ref[:, spot] * (gate * sigmoid(gate))
            squares = squares + jnp.sum(value * value, axis=-1, keepdims=True)
            dots = dots + jnp.sum(value * gain_ref[:, spot] * grad_ref[:, spot], axis=-1, keepdims=True)
        scale = lax.rsqrt(squares / width + EPSILON)
        common = scale * scale * scale * (dots / width)
        for at in range(0, width, 256):
            spot = slice(at, at + 256)
            gate = gate_ref[:, spot]
            sig = sigmoid(gate)
            silu = gate * sig
            scanned = scan_ref[:, spot]
            value = scanned * silu
            grad = grad_ref[:, spot]
            gain_out[:, spot] = jnp.sum(grad * value * scale, axis=0, keepdims=True)
            value_grad = scale * (gain_ref[:, spot] * grad) - value * common
            z_ref[:, spot] = (value_grad * scanned * (sig * (1.0 + gate * (1.0 - sig)))).astype(
                jnp.bfloat16
            )
            scan_grad_ref[:, spot] = (value_grad * silu).astype(jnp.bfloat16)
        moved, step, step_rate = steps_of(raw_ref, shift_ref, rate_ref)
        by_column, by_row, lower = decay_sums(step * step_rate, extent)
        b_state = act_ref[:, width : width + NS]
        c_state = act_ref[:, width + NS :]
        inner = matmul_right(c_state, b_state)
        inner_grad = jnp.zeros((extent, extent), jnp.float32)
        lane = lax.broadcasted_iota(jnp.int32, (extent, MH), 1)
        by_column_grad = jnp.zeros((extent, MH), jnp.float32)
        step_grad = jnp.zeros((extent, MH), jnp.float32)
        for number in range(MH // 2):
            spot = slice(number * pair, (number + 1) * pair)
            heads = act_ref[:, spot].astype(jnp.float32)
            steps = pick(half, step[:, 2 * number : 2 * number + 1], step[:, 2 * number + 1 : 2 * number + 2])
            scaled = (heads * steps).astype(jnp.bfloat16)
            grad = scan_grad_ref[:, spot]
            results = []
            for first in (True, False):
                head = 2 * number + (0 if first else 1)
                decay = decay_of(by_column, by_row, head, can)
                weight_grad = masked_dot(grad, half, first, scaled)
                mixed = decay * inner
                results.append(matmul_left(mixed.astype(jnp.bfloat16), grad))
                inner_grad = inner_grad + weight_grad * decay
                spread_grad = weight_grad * mixed
                column = jnp.sum(spread_grad, axis=1, keepdims=True)
                by_column_grad = by_column_grad + jnp.where(lane == head, column, 0.0)
                row_ref[head : head + 1, :] = jnp.sum(spread_grad, axis=0, keepdims=True)
            scaled_grad = pick(half, *results)
            grad = grad.astype(jnp.float32)
            act_grad_ref[:, spot] = scaled_grad * steps + skip_ref[:, spot] * grad
            product = scaled_grad * heads
            for first in (True, False):
                head = 2 * number + (0 if first else 1)
                chosen = jnp.where(half, product, 0.0) if first else jnp.where(half, 0.0, product)
                column = jnp.sum(chosen, axis=1, keepdims=True)
                step_grad = step_grad + jnp.where(lane == head, column, 0.0)
            skip_out[:, spot] = jnp.sum(grad * heads, axis=0, keepdims=True)
        inner_low = inner_grad.astype(jnp.bfloat16)
        act_grad_ref[:, width : width + NS] = matmul_left(inner_low, c_state)
        act_grad_ref[:, width + NS :] = matmul_plain(inner_low, b_state)
        decay_grad = dot_exact(lower, by_column_grad, ((0,), (0,))) - dot_exact(
            lower, row_ref[...], ((0,), (1,))
        )
        rate_out[...] = jnp.sum(decay_grad * step * step_rate, axis=0, keepdims=True)
        raw_grad = (step_grad + decay_grad * step_rate) * sigmoid(moved)
        shift_out[...] = jnp.sum(raw_grad, axis=0, keepdims=True)
        raw_low = raw_grad.astype(jnp.bfloat16)
        raw_low_ref[...] = raw_low
        raw_out[...] = matmul_left(raw_low, normed_ref[...])
        for at in range(0, channels, 256):
            spot = slice(at, at + 256)
            total = conv_sum(conv_ref, taps_ref, bias_ref, moves_ref, spot)
            sig = sigmoid(total)
            grad = act_grad_ref[:, spot] * (sig * (1.0 + total * (1.0 - sig)))
            bias_out[:, spot] = jnp.sum(grad, axis=0, keepdims=True)
            value = conv_ref[:, spot]
            taps_out[CONV_K - 1 : CONV_K, spot] = jnp.sum(grad * value, axis=0, keepdims=True)
            sums = taps_ref[CONV_K - 1 : CONV_K, spot] * grad
            for offset in range(1, CONV_K):
                kept = grad * moves_ref[:, offset : offset + 1]
                tap = slice(CONV_K - 1 - offset, CONV_K - offset)
                taps_out[tap, spot] = jnp.sum(
                    kept * pltpu.roll(value, offset, 0), axis=0, keepdims=True
                )
                sums = sums + taps_ref[tap, spot] * pltpu.roll(kept, extent - offset, 0)
            low_ref[:, spot] = sums.astype(jnp.bfloat16)
        q_cols = QH * ATTENTION_HEAD
        z_ref[:, width:] = qkv_ref[:, :q_cols]
        low_ref[:, channels:] = qkv_ref[:, q_cols:]
        first = side_ref[0] == 0
        for at in range(0, MIXED // 2, 256):
            spot = slice(at, at + 256)
            mine_ref[:, spot] = jnp.where(first, z_ref[:, spot], low_ref[:, spot])
            theirs_ref[:, spot] = jnp.where(first, low_ref[:, spot], z_ref[:, spot])

    return call_whole(
        body,
        (
            shape((extent, MIXED // 2), jnp.bfloat16),
            shape((extent, MIXED // 2), jnp.bfloat16),
            shape((extent, MH), jnp.bfloat16),
            shape((MH, normed.shape[1])),
            shape((extent, MIXED // 2), jnp.bfloat16),
            shape((extent, MIXED // 2), jnp.bfloat16),
            shape((1, width)),
            shape((CONV_K, channels)),
            shape((1, channels)),
            shape((1, width)),
            shape((1, MH)),
            shape((1, MH)),
        ),
        (
            side,
            normed,
            qkv_low,
            gated_grad,
            scan,
            act,
            conv_in,
            raw_step,
            gate_z,
            taps,
            bias,
            shift,
            rate,
            skip,
            gain,
            moves,
            allowed,
        ),
        scratch=(
            pltpu.VMEM((extent, width), jnp.bfloat16),
            pltpu.VMEM((extent, channels), jnp.float32),
            pltpu.VMEM((MH, extent), jnp.float32),
        ),
        name="mixer_back",
        after=after,
    )


def middle(side, pack, spans, tokens, early, cotangent, valid, gain):
    extent, model = tokens.shape
    width = MH * HD
    q_cols = QH * ATTENTION_HEAD
    groups = pack.shape[0]
    half_ff = FF // 2

    def body(
        side_ref,
        pack_ref,
        tokens_ref,
        early_ref,
        cot_ref,
        valid_ref,
        gain_ref,
        result_ref,
        mine_ref,
        theirs_ref,
        grad_ref,
        gain_out,
        gated_out,
        heads_out,
        *rest,
    ):
        held, sems = rest[:-1], rest[-1]
        loads = []
        for number, (start, count) in enumerate(spans):
            load = pltpu.make_async_copy(
                pack_ref.at[:, pl.ds(start, count), :], held[number], sems.at[number]
            )
            load.start()
            loads.append(load)

        def matrix(number):
            return held[number][...].reshape(groups * spans[number][1], BLOCK)

        first = side_ref[0] == 0

        def both(at, low, high):
            mine_ref[:, at : at + low.shape[1]] = jnp.where(first, low, high)
            theirs_ref[:, at : at + low.shape[1]] = jnp.where(first, high, low)

        is_valid = valid_ref[...] > 0.0
        out_grad = jnp.where(is_valid, cot_ref[...].astype(jnp.float32), 0.0)
        feed_grad = out_grad.astype(jnp.bfloat16)
        loads[0].wait()
        loads[1].wait()
        residual = tokens_ref[...].astype(jnp.float32) + (
            matmul_plain(early_ref[:, :width], matrix(0))
            + matmul_plain(early_ref[:, width : width + q_cols], matrix(1))
        )
        scale = lax.rsqrt(jnp.mean(residual * residual, axis=-1, keepdims=True) + EPSILON)
        gain_val = gain_ref[...]
        normed = (residual * scale * gain_val).astype(jnp.bfloat16)
        mine_ref[:, :model] = normed
        theirs_ref[:, :model] = normed
        loads[6].wait()
        hidden_grad = matmul_right(feed_grad, matrix(6))
        normed_grad = jnp.zeros((extent, model), jnp.float32)
        feed_out = jnp.zeros((extent, model), jnp.float32)
        gates, ups = [], []
        for part in range(2):
            loads[2 + part].wait()
            loads[4 + part].wait()
            columns = slice(part * half_ff, (part + 1) * half_ff)
            gate = matmul_plain(normed, matrix(2 + part))
            up = matmul_plain(normed, matrix(4 + part))
            sig = sigmoid(gate)
            silu = gate * sig
            hidden = (silu * up).astype(jnp.bfloat16)
            at = model + FF + part * half_ff
            mine_ref[:, at : at + half_ff] = hidden
            theirs_ref[:, at : at + half_ff] = hidden
            grad = hidden_grad[:, columns]
            gate_low = (grad * up * (sig * (1.0 + gate * (1.0 - sig)))).astype(jnp.bfloat16)
            up_low = (grad * silu).astype(jnp.bfloat16)
            gates.append(gate_low)
            ups.append(up_low)
            normed_grad = normed_grad + (
                matmul_right(gate_low, matrix(2 + part)) + matmul_right(up_low, matrix(4 + part))
            )
            feed_out = feed_out + matmul_plain(hidden, matrix(6)[columns])
        both(model, *gates)
        both(model + half_ff, *ups)
        result_ref[...] = jnp.where(is_valid, residual + feed_out, 0.0).astype(jnp.bfloat16)
        gain_out[...] = jnp.sum(normed_grad * residual * scale, axis=0, keepdims=True)
        scaled = gain_val * normed_grad
        dots = jnp.mean(scaled * residual, axis=-1, keepdims=True)
        residual_grad = out_grad + (scale * scaled - residual * (scale * scale * scale * dots))
        grad_ref[...] = residual_grad
        branch = residual_grad.astype(jnp.bfloat16)
        both(model + 2 * FF, branch[:, : model // 2], branch[:, model // 2 :])
        gated_out[...] = matmul_right(branch, matrix(0))
        heads_out[...] = matmul_right(branch, matrix(1)).astype(jnp.bfloat16)

    low = jnp.bfloat16
    outs = (
        shape((extent, model), low),
        shape((extent, model + 2 * FF + model // 2), low),
        shape((extent, model + 2 * FF + model // 2), low),
        shape((extent, model)),
        shape((1, model)),
        shape((extent, width)),
        shape((extent, q_cols), low),
    )
    args = (side, pack, tokens, early, cotangent, valid, gain)
    spaces = [pltpu.SMEM, pl.ANY] + [pltpu.VMEM] * 5
    return pl.pallas_call(
        body,
        out_shape=outs,
        in_specs=[pl.BlockSpec(memory_space=space) for space in spaces],
        out_specs=[pl.BlockSpec(memory_space=pltpu.VMEM)] * len(outs),
        scratch_shapes=[pltpu.VMEM((groups, count, BLOCK), low) for _, count in spans]
        + [pltpu.SemaphoreType.DMA((len(spans),))],
        compiler_params=pltpu.CompilerParams(vmem_limit_bytes=52 * 1024 * 1024),
        cost_estimate=cost("middle"),
        name="middle",
    )(*args)


def outer(spots, terms, z_size, apart, after=(), extra=None):
    more = 16 if extra is not None else 0
    rows = [width // (2 * z_size) for _, _, width, _, _ in terms]
    columns = sum(size for _, size in terms[0][4])
    arrays = []
    for lefts, _, _, rights, _ in terms:
        for value in lefts + rights:
            if not any(value is held for held in arrays):
                arrays.append(value)

    def body(spots_ref, *refs):
        first = spots_ref[0] == 0
        quarter = spots_ref[1]

        def ref_of(value):
            return refs[[held is value for held in arrays].index(True)]

        at = 0
        for (lefts, begin, _, rights, segments), size in zip(terms, rows):
            right = jnp.concatenate(
                [
                    jnp.concatenate(
                        [
                            ref_of(value)[:, pl.ds(pl.multiple_of(start + quarter * width, 128), width)]
                            for start, width in segments
                        ],
                        axis=1,
                    )
                    for value in rights
                ],
                axis=0,
            )
            for z in range(z_size):
                low = begin + 2 * z * size
                left = jnp.concatenate(
                    [ref_of(value)[:, low : low + 2 * size] for value in lefts], axis=0
                )
                both = matmul_left(left, right).astype(jnp.bfloat16)
                even, odd = both[:size], both[size:]
                if apart:
                    refs[-2][z, at : at + size, :] = jnp.where(first, even, odd)
                    refs[-1][z, at : at + size, :] = jnp.where(first, odd, even)
                else:
                    refs[-1][z, 0, at : at + size, :] = even
                    refs[-1][z, 1, at : at + size, :] = odd
            at += size
        if extra is not None:
            source = refs[len(arrays)]
            blank = jnp.zeros((more, columns), jnp.bfloat16)
            for z in range(z_size):
                refs[-2][z, at : at + more, :] = blank
                refs[-1][z, at : at + more, :] = blank
                for row in range(extra.shape[2]):
                    put = (z, slice(at + row // 8, at + row // 8 + 1), slice(row % 8 * 128, row % 8 * 128 + 128))
                    even = source[z, 0, row : row + 1, :].astype(jnp.bfloat16)
                    odd = source[z, 1, row : row + 1, :].astype(jnp.bfloat16)
                    refs[-2][put] = jnp.where(first, even, odd)
                    refs[-1][put] = jnp.where(first, odd, even)

    if apart:
        outs = (shape((z_size, sum(rows) + more, columns), jnp.bfloat16),) * 2
    else:
        outs = (shape((z_size, 2, sum(rows), columns), jnp.bfloat16),)
    return call_whole(
        body,
        outs,
        (spots, *arrays) + (() if extra is None else (extra,)),
        name="outer",
        after=after,
    )


def stack(mine, other, after):
    rows, columns = mine.shape

    def body(mine_ref, other_ref, out):
        out[:rows, :] = mine_ref[...]
        out[rows:, :] = other_ref[...]

    (out,) = call_whole(
        body, (shape((2 * rows, columns), mine.dtype),), (mine, other), name="stack", after=after
    )
    return out


def hold(value, after):
    def body(value_ref, out):
        out[...] = value_ref[...]

    (out,) = call_whole(
        body, (shape(value.shape, value.dtype),), (value,), name="hold", after=after
    )
    return out


def cut_rows(turn, pieces, weights, groups):
    sizes = []
    moves = []
    for number, (rows, columns, parts) in enumerate(groups):
        sizes.append((rows, columns))
        moves += [(number,) + part for part in parts]

    def body(turn_ref, *refs):
        outs, sems = refs[len(weights) : -1], refs[-1]
        copies = []
        for number, (group, index, column, columns, row, place_at) in enumerate(moves):
            count = weights[index].shape[0] // pieces
            begin = pl.multiple_of(turn_ref[0] * count, 16)
            copy = pltpu.make_async_copy(
                refs[index].at[pl.ds(begin, count), pl.ds(column, columns)],
                outs[group].at[pl.ds(row, count), pl.ds(place_at, columns)],
                sems.at[number],
            )
            copy.start()
            copies.append(copy)
        for copy in copies:
            copy.wait()

    return pl.pallas_call(
        body,
        out_shape=tuple(shape(size, jnp.bfloat16) for size in sizes),
        in_specs=[pl.BlockSpec(memory_space=pltpu.SMEM)]
        + [pl.BlockSpec(memory_space=pl.ANY)] * len(weights),
        out_specs=[pl.BlockSpec(memory_space=pltpu.VMEM)] * len(sizes),
        scratch_shapes=[pltpu.SemaphoreType.DMA((len(moves),))],
        compiler_params=pltpu.CompilerParams(vmem_limit_bytes=24 * 1024 * 1024),
        cost_estimate=cost("cut_rows"),
        name="cut_rows",
    )(turn, *weights)


def pack_grads(raw, in_gain, taps, bias, ssm_gain, ff_gain, heads, parts):
    def body(*refs):
        raw_ref, in_ref, taps_ref, bias_ref, ssm_ref, ff_ref = refs[:6]
        out = refs[-1]
        out[...] = jnp.zeros(out.shape, jnp.float32)

        def put(part, row, ref, size):
            begin = part * size
            rows = ref.shape[0]
            for at in range(0, size, 128):
                count = min(128, size - at)
                out[part, row : row + rows, :count] = ref[:, begin + at : begin + at + count]
                row += rows

        for part in range(parts):
            at = 0
            for ref in (raw_ref, in_ref, taps_ref, bias_ref, ssm_ref, ff_ref):
                size = ref.shape[1] // parts
                put(part, at, ref, size)
                at += ref.shape[0] * -(-size // 128)
            for number, ref in enumerate(refs[6:9]):
                out[part, 40 + number : 41 + number, :MH] = ref[...]

    (out,) = call_whole(
        body,
        (shape((parts, 48, 128)),),
        (raw, in_gain, taps, bias, ssm_gain, ff_gain) + tuple(heads),
        name="pack_grads",
    )
    return out


def unpack_grads(spots, block, heads, sizes):
    count = len(heads)

    def body(spots_ref, block_ref, *refs):
        z = spots_ref[0]
        head_refs, outs = refs[:count], refs[count:]
        total = jnp.zeros(heads[0].shape, jnp.float32)

        def take(row, count, width):
            parts = [
                block_ref[at // 8 : at // 8 + 1, at % 8 * 128 : at % 8 * 128 + width]
                for at in range(row, row + count)
            ]
            return jnp.concatenate(parts, axis=0).astype(jnp.float32)

        for at in range(count):
            step = lax.rem(z + (count - at), count)
            row = head_refs[0][...]
            for number in range(1, count):
                row = jnp.where(step == number, head_refs[number][...], row)
            total = total + row.astype(jnp.float32)
        outs[0][...] = take(0, MH, 128).T
        at = MH
        for out, (rows, size) in zip(outs[1:], sizes):
            for begin in range(0, size, 128):
                width = min(128, size - begin)
                out[:, begin : begin + width] = take(at, rows, width)
                at += rows
        for number, out in enumerate(outs[1 + len(sizes) :]):
            out[...] = total[:, number * 128 : number * 128 + MH]

    return call_whole(
        body,
        (shape((128, MH)),) + tuple(shape(size) for size in sizes) + (shape((1, MH)),) * 3,
        (spots, block) + tuple(heads),
        name="unpack_grads",
    )


def finish(spots, pieces, outs, extra=None):
    size = pieces[0].shape[1]

    def body(spots_ref, *refs):
        pieces_ref = refs[:4]
        out_refs = refs[4 + (extra is not None) :]
        y, c = spots_ref[0], spots_ref[1]
        for quarter in range(4):
            same_y = y == quarter // 2
            same_c = c == quarter % 2
            for out_ref, (_, _, moves) in zip(out_refs, outs):
                for source, rows, column, count in moves[quarter]:
                    own, by_c, by_y, by_yc = [
                        ref[rows, source : source + count] for ref in pieces_ref
                    ]
                    value = jnp.where(
                        same_y,
                        jnp.where(same_c, own, by_c),
                        jnp.where(same_c, by_y, by_yc),
                    )
                    out_ref[:, column : column + count] = value.astype(jnp.float32)
        if extra is not None:
            out_refs[0][:, outs[0][1] - extra.shape[1] :] = refs[4][...]

    args = (spots,) + tuple(pieces) + (() if extra is None else (extra,))
    return call_whole(
        body, tuple(shape((rows, columns)) for rows, columns, _ in outs), args, name="finish"
    )


def block_masks(segment, position):
    extent = segment.shape[0]
    slot = jnp.arange(extent, dtype=jnp.int32)
    moves = [jnp.ones((extent,), jnp.bool_)]
    for offset in range(1, CONV_K):
        moves.append((slot >= offset) & (jnp.roll(segment, offset) == segment))
    half = ATTENTION_HEAD // 2
    inverse = ROPE_BASE ** (-jnp.arange(half, dtype=jnp.float32) / half)
    angle = position.astype(jnp.float32)[:, None] * inverse[None, :]
    return (
        jnp.stack(moves, axis=1).astype(jnp.float32),
        causal_allowed(segment).astype(jnp.float32),
        jnp.tile(jnp.cos(angle), (1, 4)),
        jnp.tile(jnp.sin(angle), (1, 4)),
    )


def forward_pass(side, feed_grad, tokens_f, gains, mats, a_log, dt_bias, skip_d, segment, position):
    in_gain, conv_w, conv_b, ssm_gain, _, w_raw = gains
    w_first, w_second = mats
    moves, allowed, cosine, sine = block_masks(segment, position)
    normed_f, pull_norm_one = jax.vjp(rms_scale, tokens_f, in_gain.astype(jnp.float32))
    normed = normed_f.astype(jnp.bfloat16)
    conv_in = matmul_plain(normed, w_first)
    gate_z = matmul_plain(normed, w_second)
    raw_step = matmul_right(normed, w_raw)
    low, heads_out = attention_front(conv_in, gate_z, cosine, sine, allowed)
    mixer_args = (
        conv_in,
        raw_step,
        gate_z,
        conv_w.astype(jnp.float32),
        conv_b.astype(jnp.float32)[None],
        dt_bias[None],
        a_log[None],
        jnp.repeat(skip_d, HD)[None],
        ssm_gain.astype(jnp.float32)[None],
        moves,
        allowed,
    )
    act, scan, early_mine, early_theirs = mixer_front(
        side, heads_out, normed, feed_grad, *mixer_args
    )
    kept = (pull_norm_one, normed, mixer_args, act, scan, low, (cosine, sine, allowed))
    return (early_mine, early_theirs, kept)


def backward_pass(after, side, grads, w_raw, mats, kept):
    w_first, w_second = mats
    pull_norm_one, normed, mixer_args, act, scan, low, turn_args = kept
    residual_grad, gated_grad, heads_grad = grads
    qkv_low = attention_back(low, heads_grad, *turn_args)
    (
        z_low,
        conv_low,
        raw_low,
        raw_rows,
        mixed_mine,
        mixed_theirs,
        grad_ssm_gain,
        grad_conv_w,
        grad_conv_b,
        skip_lanes,
        grad_dt_bias,
        grad_a_log,
    ) = mixer_back(after, side, normed, qkv_low, gated_grad, scan, act, *mixer_args)
    grad_skip = jnp.sum(skip_lanes.reshape(MH, HD), axis=1)
    normed_grad = (
        matmul_right(z_low, w_second)
        + matmul_right(conv_low, w_first)
        + matmul_plain(raw_low, w_raw)
    )
    token_part, grad_in_gain = pull_norm_one(normed_grad)
    tokens_grad = (residual_grad + token_part).astype(jnp.bfloat16)
    small = (
        raw_rows,
        grad_in_gain[None],
        grad_conv_w,
        grad_conv_b,
        grad_ssm_gain,
        grad_a_log,
        grad_dt_bias,
        grad_skip[None],
    )
    return (tokens_grad, (mixed_mine, mixed_theirs), small)


AXES = ("shard", "replica")


def place(pieces, positions, dim, count):
    shape = list(pieces[0].shape)
    shape[dim] = count
    total = len(pieces)

    def body(where, *refs):
        out, held, sems = refs[total], refs[total + 1 : 2 * total + 1], refs[-1]
        loads, stores = [], []
        for number in range(total):
            spot = (slice(None),) * dim + (pl.ds(where[number], 1),)
            loads.append(
                pltpu.make_async_copy(refs[number], held[number], sems.at[0, number])
            )
            stores.append(
                pltpu.make_async_copy(held[number], out.at[spot], sems.at[1, number])
            )
        for load in loads:
            load.start()
        for load, store in zip(loads, stores):
            load.wait()
            store.start()
        for store in stores:
            store.wait()

    return pl.pallas_call(
        body,
        out_shape=jax.ShapeDtypeStruct(tuple(shape), pieces[0].dtype),
        in_specs=[pl.BlockSpec(memory_space=pltpu.SMEM)]
        + [pl.BlockSpec(memory_space=pl.ANY)] * total,
        out_specs=pl.BlockSpec(memory_space=pl.ANY),
        scratch_shapes=[pltpu.VMEM(piece.shape, piece.dtype) for piece in pieces]
        + [pltpu.SemaphoreType.DMA((2, total))],
        compiler_params=pltpu.CompilerParams(vmem_limit_bytes=24 * 1024 * 1024),
        cost_estimate=cost("place"),
        name="place",
    )(jnp.stack(positions).astype(jnp.int32), *pieces)


class Links:
    def __init__(self, shards_of, copies):
        self.z_size = shards_of // 2
        shard = lax.axis_index("shard")
        replica = lax.axis_index("replica")
        self.z, self.x = shard // 2, shard % 2
        self.y, self.c = replica // 2, replica % 2
        everyone = [(s, r) for s in range(shards_of) for r in range(copies)]

        def table(step):
            return [(s * copies + r, step(s, r)) for s, r in everyone]

        self.tables = {
            "x": table(lambda s, r: (s ^ 1) * copies + r),
            "y": table(lambda s, r: s * copies + (r ^ 2)),
            "c": table(lambda s, r: s * copies + (r ^ 1)),
            "z": table(lambda s, r: ((s + 2) % shards_of) * copies + r),
        }

    def send(self, value, axis):
        return lax.ppermute(value, AXES, self.tables[axis])

    def spread(self, value, axis):
        if axis == "z":
            pieces, spots = [value], [self.z]
            for step in range(1, self.z_size):
                pieces.append(self.send(pieces[-1], "z"))
                spots.append((self.z + self.z_size - step) % self.z_size)
            return place(pieces, spots, 0, self.z_size)
        spot = {"x": self.x, "y": self.y, "c": self.c}[axis]
        return place([value, self.send(value, axis)], [spot, 1 - spot], "zxyc".index(axis), 2)

    def gather(self, value, order):
        if value.ndim == 2:
            value = value[None, None, None, None]
        for axis in order:
            value = self.spread(value, axis)
        return value

    def gather_small(self, own):
        other = self.send(own, "x")
        pair = jnp.stack(
            [jnp.where(self.x == 0, own, other), jnp.where(self.x == 0, other, own)]
        )
        pieces = [pair]
        for _ in range(1, self.z_size):
            pieces.append(self.send(pieces[-1], "z"))
        stacked = jnp.stack(pieces)
        return jnp.concatenate(
            [
                lax.dynamic_index_in_dim(stacked, (self.z + self.z_size - at) % self.z_size, 0, False)
                for at in range(self.z_size)
            ]
        )

    def near(self, mine, theirs, after=()):
        both = stack(mine, self.send(theirs, "y"), after)
        return [both, self.send(both, "c")]

    def around(self, block):
        total = block(0).astype(jnp.bfloat16)
        for step in range(1, self.z_size):
            arrived = self.send(total, "z")
            total = (arrived.astype(jnp.float32) + block(step)).astype(jnp.bfloat16)
        return total

    def at_step(self, value, step):
        at = (self.z + 2 * self.z_size - 1 - step) % self.z_size
        return lax.dynamic_index_in_dim(value, at, 0, False).astype(jnp.float32)

    def add_small(self, value):
        value = value + self.send(value, "c")
        value = value + self.send(value, "y")
        return value.reshape(self.z_size, 2, 48, 128)

    def reduce_mixed(self, mine, theirs, after):
        moved = self.send(theirs, "x")
        total = (self.at_step(mine, 0) + self.at_step(moved, 0)).astype(jnp.bfloat16)
        heads = [total[133:134]]
        for step in range(1, self.z_size):
            arrived = self.send(total, "z")
            heads.append(arrived[133:134])
            block = self.at_step(mine, step) + self.at_step(moved, step)
            row = lax.broadcasted_iota(jnp.int32, block.shape, 0)
            block = jnp.where(row == 133, 0.0, block)
            total = (arrived.astype(jnp.float32) + block).astype(jnp.bfloat16)
        return moved, self.quarters(total[:128], after), total[128:], heads

    def quarters(self, total, after=()):
        by_y = self.send(total, "y")
        if after:
            by_y = hold(by_y, after)
        return (total, self.send(total, "c"), by_y, self.send(by_y, "c"))

    def reduce_xz(self, mine, theirs):
        moved = self.send(theirs, "x")
        return moved, self.quarters(
            self.around(lambda step: self.at_step(mine, step) + self.at_step(moved, step))
        )


    def reduce_zx(self, value, after):
        total = self.around(lambda step: self.at_step(value, step))
        mine = lax.dynamic_index_in_dim(total, self.x, 0, False)
        theirs = lax.dynamic_index_in_dim(total, 1 - self.x, 0, False)
        moved = self.send(theirs, "x")
        mine = hold(mine, after)
        return self.quarters(
            (mine.astype(jnp.float32) + moved.astype(jnp.float32)).astype(jnp.bfloat16)
        )


def pack_small(in_gain, conv_w, conv_b, ssm_gain, ff_gain, raw):
    def rows(value):
        flat = value.reshape(-1)
        return jnp.pad(flat, (0, -flat.shape[0] % 128)).reshape(-1, 128)

    packed = jnp.concatenate([rows(v) for v in (raw.T, in_gain, conv_w, conv_b, ssm_gain, ff_gain)])
    return jnp.pad(packed, ((0, -packed.shape[0] % 16), (0, 0)))


def unpack_small(gathered, own):
    in_gain, conv_w, conv_b, ssm_gain, ff_gain, raw = own
    parts = gathered.shape[0]
    at = 0
    out = []
    for value in (raw.T, in_gain, conv_w, conv_b, ssm_gain, ff_gain):
        count = -(-value.size // 128)
        flat = gathered[:, at : at + count].reshape(parts, -1)[:, : value.size]
        at += count
        shaped = flat.reshape((parts,) + value.shape)
        if value.ndim == 1:
            out.append(shaped.reshape(-1))
        else:
            out.append(shaped.transpose(1, 0, 2).reshape(value.shape[0], -1))
    return tuple(out[1:]) + (out[0],)


def shards(
    copies,
    tokens,
    cotangent,
    seq_lengths,
    seq_starts,
    in_gain,
    w_in,
    conv_w,
    conv_b,
    a_log,
    dt_bias,
    skip_d,
    ssm_gain,
    w_out,
    w_query,
    w_key,
    w_value,
    w_attn_out,
    ff_gain,
    w_gate,
    w_up,
    w_down,
):
    parts = MH * HD // w_out.shape[0]
    width = MH * HD
    channels = width + 2 * NS
    quick = parts == 8 and copies == 4
    links = Links(parts, copies)
    own_small = (in_gain, conv_w, conv_b, ssm_gain, ff_gain, w_in[:, width + channels :])
    pieces = 4 if quick else 1
    turn = jnp.stack([links.y * 2 + links.c if quick else jnp.int32(0)]).astype(jnp.int32)
    weights = (w_in, w_query, w_key, w_value, w_out, w_attn_out, w_gate, w_up, w_down)
    q_cols = QH * ATTENTION_HEAD
    k_cols = KVH * ATTENTION_HEAD
    spans, blocks, at = [], [], 0
    for index, column in ((0, 0), (1, 0), (2, 0), (2, BLOCK), (3, 0), (3, BLOCK), (4, 0)):
        count = weights[index + 4].shape[0] // pieces
        blocks.append((index, column, BLOCK, at, 0))
        spans.append((at, count))
        at += count
    (pack,) = cut_rows(turn, pieces, weights[4:], [(at, BLOCK, blocks)])
    cut_in = w_in.shape[0] // pieces
    first, second = cut_rows(
        turn,
        pieces,
        weights[:4],
        [
            (
                cut_in,
                MIXED // 2,
                [
                    (0, width, channels, 0, 0),
                    (2, 0, k_cols, 0, channels),
                    (3, 0, k_cols, 0, channels + k_cols),
                ],
            ),
            (cut_in, MIXED // 2, [(0, 0, width, 0, 0), (1, 0, q_cols, 0, width)]),
        ],
    )
    if quick:
        small_all = links.gather_small(pack_small(*own_small))
        mats = tuple(
            links.gather(value, order).reshape(-1, MIXED // 2)
            for value, order in ((first, "zxyc"), (second, "zyxc"))
        )
        pack = lax.all_gather(pack, AXES, axis=0)
    else:
        small_all = lax.all_gather(pack_small(*own_small), "shard", axis=0)
        mats = tuple(
            lax.all_gather(value, "shard", axis=0, tiled=True) for value in (first, second)
        )
        pack = lax.all_gather(pack, "shard", axis=0)
    gains = unpack_small(small_all, own_small)
    segment, position = layout(seq_lengths[0], seq_starts[0], tokens.shape[0])
    side = jnp.stack([links.y if quick else jnp.int32(0)]).astype(jnp.int32)
    valid = (segment >= 0).astype(jnp.float32)[:, None]
    feed_grad = jnp.where(valid > 0.0, cotangent, 0.0).astype(jnp.bfloat16)
    early_mine, early_theirs, kept = forward_pass(
        side,
        feed_grad,
        tokens.astype(jnp.float32),
        gains,
        mats,
        a_log,
        dt_bias,
        skip_d,
        segment,
        position,
    )
    (
        result,
        late_mine,
        late_theirs,
        residual_grad,
        grad_ff_gain,
        gated_grad,
        heads_grad,
    ) = middle(
        side, pack, spans, tokens, early_mine, cotangent, valid, gains[4].astype(jnp.float32)[None]
    )
    model = w_in.shape[0] * parts
    quarter = BLOCK // 4
    half_ff, quarter_ff = FF // 2, FF // 4
    place_spots = jnp.stack([links.x, links.c]).astype(jnp.int32)
    at_normed = width + q_cols
    early_four = links.near(early_mine, early_theirs) if quick else ()
    tokens_grad, (mixed_mine, mixed_theirs), small = backward_pass(
        early_four[:1], side, (residual_grad, gated_grad, heads_grad), gains[5], mats, kept
    )
    here = lax.axis_index("shard")

    def mine(value):
        size = value.shape[-1] // parts
        return lax.dynamic_slice_in_dim(value, here * size, size, value.ndim - 1)

    out_rows, attn_rows = w_out.shape[0], w_attn_out.shape[0]
    down_rows, model_rows = w_down.shape[0], w_in.shape[0]
    if quick:
        whole = slice(None)

        def plain(rows):
            return [[(0, rows, number * quarter, quarter)] for number in range(4)]

        mixed_moves = [[[] for _ in range(4)] for _ in range(4)]
        begin = 0
        for index, column, columns in (
            (0, 0, width),
            (1, 0, q_cols),
            (0, width, channels),
            (2, 0, k_cols),
            (3, 0, k_cols),
        ):
            for number in range(4):
                low = max(begin, number * BLOCK)
                high = min(begin + columns, (number + 1) * BLOCK)
                if low < high:
                    mixed_moves[index][number].append(
                        (low - number * BLOCK, whole, column + low - begin, high - low)
                    )
            begin += columns
        spots = jnp.stack([links.y, links.c]).astype(jnp.int32)
        late_four = links.near(late_mine, late_theirs, (mixed_theirs,))
        packed = pack_grads(*small[:5], grad_ff_gain, small[5:], parts)
        feed_parts = outer(
            place_spots,
            [
                (
                    late_four,
                    0,
                    model,
                    late_four,
                    [(model, quarter_ff), (model + half_ff, quarter_ff)],
                )
            ],
            links.z_size,
            True,
        )
        at_hidden = model + FF
        out_right = (late_four, [(at_hidden + FF, quarter)])
        (out_parts,) = outer(
            place_spots,
            [
                (early_four, 0, width) + out_right,
                (early_four, width, q_cols) + out_right,
                (late_four, at_hidden, FF, early_four, [(at_normed + model, quarter)]),
            ],
            links.z_size,
            False,
            feed_parts[1:],
        )
        mixed_four = links.near(mixed_mine, mixed_theirs, (out_parts,))
        mixed_parts = outer(
            place_spots,
            [(early_four, at_normed, model, mixed_four, [(0, BLOCK)])],
            links.z_size,
            True,
            (),
            links.add_small(packed),
        )
        _, feed_pieces = links.reduce_xz(*feed_parts)
        gate, up = finish(
            spots,
            feed_pieces,
            [
                (
                    model_rows,
                    FF,
                    [[(at, whole, number * quarter_ff, quarter_ff)] for number in range(4)],
                )
                for at in (0, quarter_ff)
            ],
        )
        out, attn, down = finish(
            spots,
            links.reduce_zx(out_parts, mixed_parts[1:]),
            [
                (rows, BLOCK, plain(slice(at, at + rows)))
                for rows, at in (
                    (out_rows, 0),
                    (attn_rows, out_rows),
                    (down_rows, out_rows + attn_rows),
                )
            ],
        )
        mixed_moved, mixed_pieces, small_rows, head_rows = links.reduce_mixed(
            *mixed_parts, (gate, out)
        )
        raw_part, *totals = unpack_grads(
            jnp.stack([links.z]).astype(jnp.int32),
            small_rows,
            head_rows,
            [(value.shape[0], value.shape[1] // parts) for value in small[1:5]]
            + [(1, model // parts)],
        )
        totals = [totals[0][0], totals[1]] + [value[0] for value in totals[2:]]
        projection, query, key, value = finish(
            spots,
            mixed_pieces,
            [
                (model_rows, columns, moves)
                for columns, moves in zip(
                    (width + channels + MH, q_cols, k_cols, k_cols), mixed_moves
                )
            ],
            raw_part,
        )
    else:

        def joined(first, second):
            return jnp.concatenate([first, second], axis=1)

        def share(left, right):
            part = lax.psum_scatter(
                matmul_left(left, right).astype(jnp.bfloat16),
                "shard",
                scatter_dimension=0,
                tiled=True,
            )
            return lax.psum(part, "replica").astype(jnp.float32)

        branch = joined(late_mine[:, model + 2 * FF :], late_theirs[:, model + 2 * FF :])
        mixed = share(kept[1], joined(mixed_mine, mixed_theirs))
        down = share(late_mine[:, model + FF : model + 2 * FF], feed_grad)
        normed_two = late_mine[:, :model]
        gate, up = [
            share(
                normed_two,
                joined(late_mine[:, at : at + half_ff], late_theirs[:, at : at + half_ff]),
            )
            for at in (model, model + half_ff)
        ]
        out = share(early_mine[:, :width], branch)
        attn = share(early_mine[:, width : width + q_cols], branch)
        summed = [lax.psum(value, AXES) for value in small + (grad_ff_gain,)]
        raw_part = mine(summed[0]).T
        totals = [mine(summed[1])[0], mine(summed[2])]
        totals += [mine(summed[at])[0] for at in (3, 4, 8)]
        totals += [value[0] for value in summed[5:8]]
        at = width + q_cols
        projection = jnp.concatenate(
            [mixed[:, :width], mixed[:, at : at + channels], raw_part], axis=1
        )
        query = mixed[:, width:at]
        at += channels
        key = mixed[:, at : at + k_cols]
        value = mixed[:, at + k_cols :]
    return (
        result,
        tokens_grad,
        totals[0],
        projection,
        totals[1],
        totals[2],
        totals[5],
        totals[6],
        totals[7],
        totals[3],
        out,
        query,
        key,
        value,
        attn,
        totals[4],
        gate,
        up,
        down,
    )


def solution(mesh):
    in_specs = (
        P(("shard", "replica"), None),
        P(("shard", "replica"), None),
        P(("shard", "replica"), None),
        P(("shard", "replica"), None),
        P("shard"),
        P("shard", None),
        P(None, "shard"),
        P("shard"),
        P(),
        P(),
        P(),
        P("shard"),
        P("shard", None),
        P("shard", None),
        P("shard", None),
        P("shard", None),
        P("shard", None),
        P("shard"),
        P("shard", None),
        P("shard", None),
        P("shard", None),
    )
    out_specs = (
        P(("shard", "replica"), None),
        P(("shard", "replica"), None),
        P("shard"),
        P("shard", None),
        P(None, "shard"),
        P("shard"),
        P(),
        P(),
        P(),
        P("shard"),
        P("shard", None),
        P("shard", None),
        P("shard", None),
        P("shard", None),
        P("shard", None),
        P("shard"),
        P("shard", None),
        P("shard", None),
        P("shard", None),
    )

    def local(*args):
        return shards(mesh.shape["replica"], *args)

    return jax.shard_map(local, mesh=mesh, in_specs=in_specs, out_specs=out_specs, check_vma=False)
```

```python
import jax
import jax.numpy as jnp
from jax import lax
from jax.experimental import pallas as pl
from jax.experimental.pallas import tpu as pltpu
from jax.sharding import PartitionSpec as P

FF = 2048
MH = 24
HD = 64
NS = 128
QH = 8
KVH = 2
ATTENTION_HEAD = 64
CONV_K = 4
MIXED = 2 * MH * HD + 2 * NS + (QH + 2 * KVH) * ATTENTION_HEAD
BLOCK = 1024


EPSILON = 1e-05
ROPE_BASE = 100000000000.0


def matmul_plain(left, right):
    return jnp.dot(left, right, preferred_element_type=jnp.float32)


def matmul_left(left, right):
    return lax.dot_general(
        left, right, (((0,), (0,)), ((), ())), preferred_element_type=jnp.float32
    )


def matmul_right(left, right):
    return lax.dot_general(
        left, right, (((1,), (1,)), ((), ())), preferred_element_type=jnp.float32
    )


def rms_scale(values, gain):
    return values * lax.rsqrt(jnp.mean(values * values, axis=-1, keepdims=True) + EPSILON) * gain


def layout(lengths, starts, extent):
    position = jnp.arange(extent, dtype=jnp.int32)
    inside = (position[:, None] >= starts[None, :]) & (
        position[:, None] < starts[None, :] + lengths[None, :]
    )
    number = jnp.arange(1, lengths.shape[0] + 1, dtype=jnp.int32)
    segment = jnp.sum(jnp.where(inside, number[None, :], 0), axis=1) - 1
    first = jnp.sum(jnp.where(inside, starts[None, :], 0), axis=1)
    return (segment, position - first)


def causal_allowed(segment):
    position = jnp.arange(segment.shape[0], dtype=jnp.int32)
    return (segment[:, None] == segment[None, :]) & (position[:, None] >= position[None, :])


def swiglu(gate_val, up_val):
    return jax.nn.silu(gate_val) * up_val


def sigmoid(value):
    return 1.0 / (1.0 + jnp.exp(-value))


def dot_exact(left, right, dims):
    return lax.dot_general(
        left,
        right,
        (dims, ((), ())),
        precision=lax.Precision.HIGHEST,
        preferred_element_type=jnp.float32,
    )


def lane_half(rows):
    return lax.broadcasted_iota(jnp.int32, (rows, 2 * HD), 1) < HD


def pick(half, first, second):
    return jnp.where(half, first, second)


MICROS = {
    "attention_front": 2.9,
    "attention_back": 3.8,
    "mixer_front": 5.5,
    "mixer_back": 11.5,
    "outer": 3.2,
    "finish": 2.3,
    "pack_grads": 1.0,
    "unpack_grads": 1.0,
    "hold": 1.5,
    "stack": 1.5,
    "middle": 15.8,
    "place": 2.3,
    "cut_rows": 1.5,
}


def cost(name):
    return pl.CostEstimate(
        flops=int(MICROS[name] * 1.1e9), bytes_accessed=0, transcendentals=0
    )


def call_whole(body, outs, args, scratch=(), name="kernel", after=()):
    count = len(args)

    def ordered(*refs):
        body(*refs[:count], *refs[count + len(after) :])

    return pl.pallas_call(
        ordered,
        out_shape=outs,
        in_specs=[
            pl.BlockSpec(memory_space=pltpu.SMEM if arg.dtype == jnp.int32 else pltpu.VMEM)
            for arg in args
        ]
        + [pl.BlockSpec(memory_space=pl.ANY)] * len(after),
        out_specs=[pl.BlockSpec(memory_space=pltpu.VMEM)] * len(outs),
        scratch_shapes=list(scratch),
        compiler_params=pltpu.CompilerParams(vmem_limit_bytes=40 * 1024 * 1024),
        cost_estimate=cost(name),
        name=name,
    )(*args, *after)


def shape(dims, kind=jnp.float32):
    return jax.ShapeDtypeStruct(dims, kind)


def turned(values, cosine, sine, back):
    width = values.shape[1]
    quarter = lax.broadcasted_iota(jnp.int32, values.shape, 1) % ATTENTION_HEAD
    half = ATTENTION_HEAD // 2
    swapped = jnp.where(
        quarter < half,
        -pltpu.roll(values, width - half, 1),
        pltpu.roll(values, half, 1),
    )
    return values * cosine - swapped * sine if back else values * cosine + swapped * sine


def doubled(values, half):
    moved = pltpu.roll(values, ATTENTION_HEAD, 1)
    return (pick(half, values, moved), pick(half, moved, values))


def masked_dot(pair, half, keep_first, other):
    zero = jnp.zeros_like(pair)
    chosen = jnp.where(half, pair, zero) if keep_first else jnp.where(half, zero, pair)
    return matmul_right(chosen, other)


def softmax_rows(scores, allowed):
    scores = jnp.where(allowed, scores * ATTENTION_HEAD ** (-0.5), -1e30)
    raised = jnp.exp(scores - jnp.max(scores, axis=-1, keepdims=True))
    return raised / jnp.sum(raised, axis=-1, keepdims=True)


def attention_front(first, second, cosine, sine, allowed):
    extent = first.shape[0]
    pair = 2 * ATTENTION_HEAD
    pairs = QH // 2
    at_key = first.shape[1] - 2 * pair
    at_query = second.shape[1] - pairs * pair

    def body(first_ref, second_ref, cos_ref, sin_ref, allowed_ref, low_ref, out_ref):
        half = lane_half(extent)
        can = allowed_ref[...] > 0.0
        cos_val, sin_val = cos_ref[...], sin_ref[...]
        key = turned(first_ref[:, at_key : at_key + pair], cos_val, sin_val, False)
        key = key.astype(jnp.bfloat16)
        value = first_ref[:, at_key + pair :].astype(jnp.bfloat16)
        low_ref[:, pairs * pair : (pairs + 1) * pair] = key
        low_ref[:, (pairs + 1) * pair :] = value
        keys = [k.astype(jnp.bfloat16) for k in doubled(key.astype(jnp.float32), half)]
        values = [v.astype(jnp.bfloat16) for v in doubled(value.astype(jnp.float32), half)]
        for number in range(pairs):
            spot = slice(number * pair, (number + 1) * pair)
            begin = at_query + number * pair
            query = turned(second_ref[:, begin : begin + pair], cos_val, sin_val, False)
            query = query.astype(jnp.bfloat16)
            low_ref[:, spot] = query
            group = number * KVH // pairs
            results = []
            for first in (True, False):
                scores = masked_dot(query, half, first, keys[group])
                probs = softmax_rows(scores, can).astype(jnp.bfloat16)
                results.append(matmul_plain(probs, values[group]))
            out_ref[:, spot] = pick(half, *results).astype(jnp.bfloat16)

    return call_whole(
        body,
        (
            shape((extent, (pairs + 2) * pair), jnp.bfloat16),
            shape((extent, pairs * pair), jnp.bfloat16),
        ),
        (first, second, cosine, sine, allowed),
        name="attention_front",
    )


def attention_back(low, heads_grad, cosine, sine, allowed):
    extent = low.shape[0]
    pair = 2 * ATTENTION_HEAD
    pairs = QH // 2
    scale = ATTENTION_HEAD ** (-0.5)

    def body(low_ref, grad_ref, cos_ref, sin_ref, allowed_ref, out_ref):
        half = lane_half(extent)
        can = allowed_ref[...] > 0.0
        cos_val, sin_val = cos_ref[...], sin_ref[...]
        key = low_ref[:, pairs * pair : (pairs + 1) * pair].astype(jnp.float32)
        value = low_ref[:, (pairs + 1) * pair :].astype(jnp.float32)
        keys = [k.astype(jnp.bfloat16) for k in doubled(key, half)]
        values = [v.astype(jnp.bfloat16) for v in doubled(value, half)]
        key_sums = [jnp.zeros((extent, pair), jnp.float32) for _ in range(KVH)]
        value_sums = [jnp.zeros((extent, pair), jnp.float32) for _ in range(KVH)]
        for number in range(pairs):
            spot = slice(number * pair, (number + 1) * pair)
            query = low_ref[:, spot]
            grad = grad_ref[:, spot]
            group = number * KVH // pairs
            q_parts, k_parts, v_parts = [], [], []
            for first in (True, False):
                probs = softmax_rows(masked_dot(query, half, first, keys[group]), can)
                prob_grad = masked_dot(grad, half, first, values[group])
                v_parts.append(matmul_left(probs.astype(jnp.bfloat16), grad))
                inner = jnp.sum(probs * prob_grad, axis=-1, keepdims=True)
                score_grad = (probs * (prob_grad - inner)).astype(jnp.bfloat16)
                q_parts.append(matmul_plain(score_grad, keys[group]))
                k_parts.append(matmul_left(score_grad, query))
            key_sums[group] = key_sums[group] + pick(half, *k_parts)
            value_sums[group] = value_sums[group] + pick(half, *v_parts)
            query_grad = turned(pick(half, *q_parts) * scale, cos_val, sin_val, True)
            out_ref[:, spot] = query_grad.astype(jnp.bfloat16)

        def both(sums):
            return pick(half, *[s + pltpu.roll(s, ATTENTION_HEAD, 1) for s in sums])

        key_grad = turned(both(key_sums) * scale, cos_val, sin_val, True)
        out_ref[:, pairs * pair : (pairs + 1) * pair] = key_grad.astype(jnp.bfloat16)
        out_ref[:, (pairs + 1) * pair :] = both(value_sums).astype(jnp.bfloat16)

    (out,) = call_whole(
        body,
        (shape(low.shape, jnp.bfloat16),),
        (low, heads_grad, cosine, sine, allowed),
        name="attention_back",
    )
    return out


def conv_sum(conv_ref, taps_ref, bias_ref, moves_ref, spot):
    value = conv_ref[:, spot]
    total = bias_ref[:, spot] + taps_ref[CONV_K - 1 : CONV_K, spot] * value
    for offset in range(1, CONV_K):
        moved = pltpu.roll(value, offset, 0) * moves_ref[:, offset : offset + 1]
        total = total + taps_ref[CONV_K - 1 - offset : CONV_K - offset, spot] * moved
    return total


def steps_of(raw_ref, shift_ref, rate_ref):
    moved = raw_ref[...] + shift_ref[...]
    step = jnp.maximum(moved, 0.0) + jnp.log1p(jnp.exp(-jnp.abs(moved)))
    rate = -jnp.exp(rate_ref[...])
    return moved, step, rate


def decay_sums(decay, extent):
    row = lax.broadcasted_iota(jnp.int32, (extent, extent), 0)
    column = lax.broadcasted_iota(jnp.int32, (extent, extent), 1)
    lower = jnp.where(row >= column, 1.0, 0.0)
    by_column = dot_exact(lower, decay, ((1,), (0,)))
    by_row = dot_exact(decay, lower, ((0,), (1,)))
    return by_column, by_row, lower


def decay_of(by_column, by_row, head, can):
    spread = by_column[:, head : head + 1] - by_row[head : head + 1, :]
    return jnp.where(can, jnp.exp(jnp.where(can, spread, 0.0)), 0.0)


def mixer_front(
    side,
    heads_out,
    normed,
    feed_grad,
    conv_in,
    raw_step,
    gate_z,
    taps,
    bias,
    shift,
    rate,
    skip,
    gain,
    moves,
    allowed,
):
    extent = conv_in.shape[0]
    at_normed = MH * HD + heads_out.shape[1]
    at_feed = at_normed + normed.shape[1]
    half_feed = feed_grad.shape[1] // 2
    width = MH * HD
    pair = 2 * HD

    def body(
        side_ref,
        heads_ref,
        normed_ref,
        feed_ref,
        conv_ref,
        raw_ref,
        gate_ref,
        taps_ref,
        bias_ref,
        shift_ref,
        rate_ref,
        skip_ref,
        gain_ref,
        moves_ref,
        allowed_ref,
        act_ref,
        scan_ref,
        mine_ref,
        theirs_ref,
    ):
        side_first = side_ref[0] == 0
        low, high = feed_ref[:, :half_feed], feed_ref[:, half_feed:]
        for ref in (mine_ref, theirs_ref):
            ref[:, MH * HD : at_normed] = heads_ref[...]
            ref[:, at_normed:at_feed] = normed_ref[...]
        mine_ref[:, at_feed:] = jnp.where(side_first, low, high)
        theirs_ref[:, at_feed:] = jnp.where(side_first, high, low)
        half = lane_half(extent)
        can = allowed_ref[...] > 0.0
        for at in range(0, width + 2 * NS, 256):
            spot = slice(at, at + 256)
            total = conv_sum(conv_ref, taps_ref, bias_ref, moves_ref, spot)
            act_ref[:, spot] = (total * sigmoid(total)).astype(jnp.bfloat16)
        _, step, step_rate = steps_of(raw_ref, shift_ref, rate_ref)
        by_column, by_row, _ = decay_sums(step * step_rate, extent)
        inner = matmul_right(act_ref[:, width + NS :], act_ref[:, width : width + NS])
        squares = jnp.zeros((extent, 1), jnp.float32)
        for number in range(MH // 2):
            spot = slice(number * pair, (number + 1) * pair)
            heads = act_ref[:, spot].astype(jnp.float32)
            steps = pick(half, step[:, 2 * number : 2 * number + 1], step[:, 2 * number + 1 : 2 * number + 2])
            scaled = (heads * steps).astype(jnp.bfloat16)
            results = []
            for head in (2 * number, 2 * number + 1):
                weights = (decay_of(by_column, by_row, head, can) * inner).astype(jnp.bfloat16)
                results.append(matmul_plain(weights, scaled))
            scan = pick(half, *results) + skip_ref[:, spot] * heads
            scan_ref[:, spot] = scan
            gate = gate_ref[:, spot]
            value = scan * (gate * sigmoid(gate))
            squares = squares + jnp.sum(value * value, axis=-1, keepdims=True)
        scale = lax.rsqrt(squares / width + EPSILON)
        for number in range(MH // 2):
            spot = slice(number * pair, (number + 1) * pair)
            gate = gate_ref[:, spot]
            value = scan_ref[:, spot] * (gate * sigmoid(gate))
            gated = (value * scale * gain_ref[:, spot]).astype(jnp.bfloat16)
            mine_ref[:, spot] = gated
            theirs_ref[:, spot] = gated

    return call_whole(
        body,
        (
            shape((extent, width + 2 * NS), jnp.bfloat16),
            shape((extent, width)),
            shape((extent, at_feed + half_feed), jnp.bfloat16),
            shape((extent, at_feed + half_feed), jnp.bfloat16),
        ),
        (side, heads_out, normed, feed_grad, conv_in, raw_step, gate_z, taps, bias, shift, rate, skip, gain, moves, allowed),
        name="mixer_front",
    )


def mixer_back(
    after,
    side,
    normed,
    qkv_low,
    gated_grad,
    scan,
    act,
    conv_in,
    raw_step,
    gate_z,
    taps,
    bias,
    shift,
    rate,
    skip,
    gain,
    moves,
    allowed,
):
    extent = conv_in.shape[0]
    width = MH * HD
    channels = width + 2 * NS
    pair = 2 * HD

    def body(
        side_ref,
        normed_ref,
        qkv_ref,
        grad_ref,
        scan_ref,
        act_ref,
        conv_ref,
        raw_ref,
        gate_ref,
        taps_ref,
        bias_ref,
        shift_ref,
        rate_ref,
        skip_ref,
        gain_ref,
        moves_ref,
        allowed_ref,
        z_ref,
        low_ref,
        raw_low_ref,
        raw_out,
        mine_ref,
        theirs_ref,
        gain_out,
        taps_out,
        bias_out,
        skip_out,
        shift_out,
        rate_out,
        scan_grad_ref,
        act_grad_ref,
        row_ref,
    ):
        half = lane_half(extent)
        can = allowed_ref[...] > 0.0
        squares = jnp.zeros((extent, 1), jnp.float32)
        dots = jnp.zeros((extent, 1), jnp.float32)
        for at in range(0, width, 256):
            spot = slice(at, at + 256)
            gate = gate_ref[:, spot]
            value = scan_ref[:, spot] * (gate * sigmoid(gate))
            squares = squares + jnp.sum(value * value, axis=-1, keepdims=True)
            dots = dots + jnp.sum(value * gain_ref[:, spot] * grad_ref[:, spot], axis=-1, keepdims=True)
        scale = lax.rsqrt(squares / width + EPSILON)
        common = scale * scale * scale * (dots / width)
        for at in range(0, width, 256):
            spot = slice(at, at + 256)
            gate = gate_ref[:, spot]
            sig = sigmoid(gate)
            silu = gate * sig
            scanned = scan_ref[:, spot]
            value = scanned * silu
            grad = grad_ref[:, spot]
            gain_out[:, spot] = jnp.sum(grad * value * scale, axis=0, keepdims=True)
            value_grad = scale * (gain_ref[:, spot] * grad) - value * common
            z_ref[:, spot] = (value_grad * scanned * (sig * (1.0 + gate * (1.0 - sig)))).astype(
                jnp.bfloat16
            )
            scan_grad_ref[:, spot] = (value_grad * silu).astype(jnp.bfloat16)
        moved, step, step_rate = steps_of(raw_ref, shift_ref, rate_ref)
        by_column, by_row, lower = decay_sums(step * step_rate, extent)
        b_state = act_ref[:, width : width + NS]
        c_state = act_ref[:, width + NS :]
        inner = matmul_right(c_state, b_state)
        inner_grad = jnp.zeros((extent, extent), jnp.float32)
        lane = lax.broadcasted_iota(jnp.int32, (extent, MH), 1)
        by_column_grad = jnp.zeros((extent, MH), jnp.float32)
        step_grad = jnp.zeros((extent, MH), jnp.float32)
        for number in range(MH // 2):
            spot = slice(number * pair, (number + 1) * pair)
            heads = act_ref[:, spot].astype(jnp.float32)
            steps = pick(half, step[:, 2 * number : 2 * number + 1], step[:, 2 * number + 1 : 2 * number + 2])
            scaled = (heads * steps).astype(jnp.bfloat16)
            grad = scan_grad_ref[:, spot]
            results = []
            for first in (True, False):
                head = 2 * number + (0 if first else 1)
                decay = decay_of(by_column, by_row, head, can)
                weight_grad = masked_dot(grad, half, first, scaled)
                mixed = decay * inner
                results.append(matmul_left(mixed.astype(jnp.bfloat16), grad))
                inner_grad = inner_grad + weight_grad * decay
                spread_grad = weight_grad * mixed
                column = jnp.sum(spread_grad, axis=1, keepdims=True)
                by_column_grad = by_column_grad + jnp.where(lane == head, column, 0.0)
                row_ref[head : head + 1, :] = jnp.sum(spread_grad, axis=0, keepdims=True)
            scaled_grad = pick(half, *results)
            grad = grad.astype(jnp.float32)
            act_grad_ref[:, spot] = scaled_grad * steps + skip_ref[:, spot] * grad
            product = scaled_grad * heads
            for first in (True, False):
                head = 2 * number + (0 if first else 1)
                chosen = jnp.where(half, product, 0.0) if first else jnp.where(half, 0.0, product)
                column = jnp.sum(chosen, axis=1, keepdims=True)
                step_grad = step_grad + jnp.where(lane == head, column, 0.0)
            skip_out[:, spot] = jnp.sum(grad * heads, axis=0, keepdims=True)
        inner_low = inner_grad.astype(jnp.bfloat16)
        act_grad_ref[:, width : width + NS] = matmul_left(inner_low, c_state)
        act_grad_ref[:, width + NS :] = matmul_plain(inner_low, b_state)
        decay_grad = dot_exact(lower, by_column_grad, ((0,), (0,))) - dot_exact(
            lower, row_ref[...], ((0,), (1,))
        )
        rate_out[...] = jnp.sum(decay_grad * step * step_rate, axis=0, keepdims=True)
        raw_grad = (step_grad + decay_grad * step_rate) * sigmoid(moved)
        shift_out[...] = jnp.sum(raw_grad, axis=0, keepdims=True)
        raw_low = raw_grad.astype(jnp.bfloat16)
        raw_low_ref[...] = raw_low
        raw_out[...] = matmul_left(raw_low, normed_ref[...])
        for at in range(0, channels, 256):
            spot = slice(at, at + 256)
            total = conv_sum(conv_ref, taps_ref, bias_ref, moves_ref, spot)
            sig = sigmoid(total)
            grad = act_grad_ref[:, spot] * (sig * (1.0 + total * (1.0 - sig)))
            bias_out[:, spot] = jnp.sum(grad, axis=0, keepdims=True)
            value = conv_ref[:, spot]
            taps_out[CONV_K - 1 : CONV_K, spot] = jnp.sum(grad * value, axis=0, keepdims=True)
            sums = taps_ref[CONV_K - 1 : CONV_K, spot] * grad
            for offset in range(1, CONV_K):
                kept = grad * moves_ref[:, offset : offset + 1]
                tap = slice(CONV_K - 1 - offset, CONV_K - offset)
                taps_out[tap, spot] = jnp.sum(
                    kept * pltpu.roll(value, offset, 0), axis=0, keepdims=True
                )
                sums = sums + taps_ref[tap, spot] * pltpu.roll(kept, extent - offset, 0)
            low_ref[:, spot] = sums.astype(jnp.bfloat16)
        q_cols = QH * ATTENTION_HEAD
        z_ref[:, width:] = qkv_ref[:, :q_cols]
        low_ref[:, channels:] = qkv_ref[:, q_cols:]
        first = side_ref[0] == 0
        for at in range(0, MIXED // 2, 256):
            spot = slice(at, at + 256)
            mine_ref[:, spot] = jnp.where(first, z_ref[:, spot], low_ref[:, spot])
            theirs_ref[:, spot] = jnp.where(first, low_ref[:, spot], z_ref[:, spot])

    return call_whole(
        body,
        (
            shape((extent, MIXED // 2), jnp.bfloat16),
            shape((extent, MIXED // 2), jnp.bfloat16),
            shape((extent, MH), jnp.bfloat16),
            shape((MH, normed.shape[1])),
            shape((extent, MIXED // 2), jnp.bfloat16),
            shape((extent, MIXED // 2), jnp.bfloat16),
            shape((1, width)),
            shape((CONV_K, channels)),
            shape((1, channels)),
            shape((1, width)),
            shape((1, MH)),
            shape((1, MH)),
        ),
        (
            side,
            normed,
            qkv_low,
            gated_grad,
            scan,
            act,
            conv_in,
            raw_step,
            gate_z,
            taps,
            bias,
            shift,
            rate,
            skip,
            gain,
            moves,
            allowed,
        ),
        scratch=(
            pltpu.VMEM((extent, width), jnp.bfloat16),
            pltpu.VMEM((extent, channels), jnp.float32),
            pltpu.VMEM((MH, extent), jnp.float32),
        ),
        name="mixer_back",
        after=after,
    )


def middle(side, pack, spans, tokens, early, cotangent, valid, gain):
    extent, model = tokens.shape
    width = MH * HD
    q_cols = QH * ATTENTION_HEAD
    groups = pack.shape[0]
    half_ff = FF // 2

    def body(
        side_ref,
        pack_ref,
        tokens_ref,
        early_ref,
        cot_ref,
        valid_ref,
        gain_ref,
        result_ref,
        mine_ref,
        theirs_ref,
        grad_ref,
        gain_out,
        gated_out,
        heads_out,
        *rest,
    ):
        held, sems = rest[:-1], rest[-1]
        loads = []
        for number, (start, count) in enumerate(spans):
            load = pltpu.make_async_copy(
                pack_ref.at[:, pl.ds(start, count), :], held[number], sems.at[number]
            )
            load.start()
            loads.append(load)

        def matrix(number):
            return held[number][...].reshape(groups * spans[number][1], BLOCK)

        first = side_ref[0] == 0

        def both(at, low, high):
            mine_ref[:, at : at + low.shape[1]] = jnp.where(first, low, high)
            theirs_ref[:, at : at + low.shape[1]] = jnp.where(first, high, low)

        is_valid = valid_ref[...] > 0.0
        out_grad = jnp.where(is_valid, cot_ref[...].astype(jnp.float32), 0.0)
        feed_grad = out_grad.astype(jnp.bfloat16)
        loads[0].wait()
        loads[1].wait()
        residual = tokens_ref[...].astype(jnp.float32) + (
            matmul_plain(early_ref[:, :width], matrix(0))
            + matmul_plain(early_ref[:, width : width + q_cols], matrix(1))
        )
        scale = lax.rsqrt(jnp.mean(residual * residual, axis=-1, keepdims=True) + EPSILON)
        gain_val = gain_ref[...]
        normed = (residual * scale * gain_val).astype(jnp.bfloat16)
        mine_ref[:, :model] = normed
        theirs_ref[:, :model] = normed
        loads[6].wait()
        hidden_grad = matmul_right(feed_grad, matrix(6))
        normed_grad = jnp.zeros((extent, model), jnp.float32)
        feed_out = jnp.zeros((extent, model), jnp.float32)
        gates, ups = [], []
        for part in range(2):
            loads[2 + part].wait()
            loads[4 + part].wait()
            columns = slice(part * half_ff, (part + 1) * half_ff)
            gate = matmul_plain(normed, matrix(2 + part))
            up = matmul_plain(normed, matrix(4 + part))
            sig = sigmoid(gate)
            silu = gate * sig
            hidden = (silu * up).astype(jnp.bfloat16)
            at = model + FF + part * half_ff
            mine_ref[:, at : at + half_ff] = hidden
            theirs_ref[:, at : at + half_ff] = hidden
            grad = hidden_grad[:, columns]
            gate_low = (grad * up * (sig * (1.0 + gate * (1.0 - sig)))).astype(jnp.bfloat16)
            up_low = (grad * silu).astype(jnp.bfloat16)
            gates.append(gate_low)
            ups.append(up_low)
            normed_grad = normed_grad + (
                matmul_right(gate_low, matrix(2 + part)) + matmul_right(up_low, matrix(4 + part))
            )
            feed_out = feed_out + matmul_plain(hidden, matrix(6)[columns])
        both(model, *gates)
        both(model + half_ff, *ups)
        result_ref[...] = jnp.where(is_valid, residual + feed_out, 0.0).astype(jnp.bfloat16)
        gain_out[...] = jnp.sum(normed_grad * residual * scale, axis=0, keepdims=True)
        scaled = gain_val * normed_grad
        dots = jnp.mean(scaled * residual, axis=-1, keepdims=True)
        residual_grad = out_grad + (scale * scaled - residual * (scale * scale * scale * dots))
        grad_ref[...] = residual_grad
        branch = residual_grad.astype(jnp.bfloat16)
        both(model + 2 * FF, branch[:, : model // 2], branch[:, model // 2 :])
        gated_out[...] = matmul_right(branch, matrix(0))
        heads_out[...] = matmul_right(branch, matrix(1)).astype(jnp.bfloat16)

    low = jnp.bfloat16
    outs = (
        shape((extent, model), low),
        shape((extent, model + 2 * FF + model // 2), low),
        shape((extent, model + 2 * FF + model // 2), low),
        shape((extent, model)),
        shape((1, model)),
        shape((extent, width)),
        shape((extent, q_cols), low),
    )
    args = (side, pack, tokens, early, cotangent, valid, gain)
    spaces = [pltpu.SMEM, pl.ANY] + [pltpu.VMEM] * 5
    return pl.pallas_call(
        body,
        out_shape=outs,
        in_specs=[pl.BlockSpec(memory_space=space) for space in spaces],
        out_specs=[pl.BlockSpec(memory_space=pltpu.VMEM)] * len(outs),
        scratch_shapes=[pltpu.VMEM((groups, count, BLOCK), low) for _, count in spans]
        + [pltpu.SemaphoreType.DMA((len(spans),))],
        compiler_params=pltpu.CompilerParams(vmem_limit_bytes=52 * 1024 * 1024),
        cost_estimate=cost("middle"),
        name="middle",
    )(*args)


def outer(spots, terms, z_size, apart, after=(), extra=None):
    more = 16 if extra is not None else 0
    rows = [width // (2 * z_size) for _, _, width, _, _ in terms]
    columns = sum(size for _, size in terms[0][4])
    arrays = []
    for lefts, _, _, rights, _ in terms:
        for value in lefts + rights:
            if not any(value is held for held in arrays):
                arrays.append(value)

    def body(spots_ref, *refs):
        first = spots_ref[0] == 0
        quarter = spots_ref[1]

        def ref_of(value):
            return refs[[held is value for held in arrays].index(True)]

        at = 0
        for (lefts, begin, _, rights, segments), size in zip(terms, rows):
            right = jnp.concatenate(
                [
                    jnp.concatenate(
                        [
                            ref_of(value)[:, pl.ds(pl.multiple_of(start + quarter * width, 128), width)]
                            for start, width in segments
                        ],
                        axis=1,
                    )
                    for value in rights
                ],
                axis=0,
            )
            for z in range(z_size):
                low = begin + 2 * z * size
                left = jnp.concatenate(
                    [ref_of(value)[:, low : low + 2 * size] for value in lefts], axis=0
                )
                both = matmul_left(left, right).astype(jnp.bfloat16)
                even, odd = both[:size], both[size:]
                if apart:
                    refs[-2][z, at : at + size, :] = jnp.where(first, even, odd)
                    refs[-1][z, at : at + size, :] = jnp.where(first, odd, even)
                else:
                    refs[-1][z, 0, at : at + size, :] = even
                    refs[-1][z, 1, at : at + size, :] = odd
            at += size
        if extra is not None:
            source = refs[len(arrays)]
            blank = jnp.zeros((more, columns), jnp.bfloat16)
            for z in range(z_size):
                refs[-2][z, at : at + more, :] = blank
                refs[-1][z, at : at + more, :] = blank
                for row in range(extra.shape[2]):
                    put = (z, slice(at + row // 8, at + row // 8 + 1), slice(row % 8 * 128, row % 8 * 128 + 128))
                    even = source[z, 0, row : row + 1, :].astype(jnp.bfloat16)
                    odd = source[z, 1, row : row + 1, :].astype(jnp.bfloat16)
                    refs[-2][put] = jnp.where(first, even, odd)
                    refs[-1][put] = jnp.where(first, odd, even)

    if apart:
        outs = (shape((z_size, sum(rows) + more, columns), jnp.bfloat16),) * 2
    else:
        outs = (shape((z_size, 2, sum(rows), columns), jnp.bfloat16),)
    return call_whole(
        body,
        outs,
        (spots, *arrays) + (() if extra is None else (extra,)),
        name="outer",
        after=after,
    )


def stack(mine, other, after):
    rows, columns = mine.shape

    def body(mine_ref, other_ref, out):
        out[:rows, :] = mine_ref[...]
        out[rows:, :] = other_ref[...]

    (out,) = call_whole(
        body, (shape((2 * rows, columns), mine.dtype),), (mine, other), name="stack", after=after
    )
    return out


def hold(value, after):
    def body(value_ref, out):
        out[...] = value_ref[...]

    (out,) = call_whole(
        body, (shape(value.shape, value.dtype),), (value,), name="hold", after=after
    )
    return out


def cut_rows(turn, pieces, weights, groups):
    sizes = []
    moves = []
    for number, (rows, columns, parts) in enumerate(groups):
        sizes.append((rows, columns))
        moves += [(number,) + part for part in parts]

    def body(turn_ref, *refs):
        outs, sems = refs[len(weights) : -1], refs[-1]
        copies = []
        for number, (group, index, column, columns, row, place_at) in enumerate(moves):
            count = weights[index].shape[0] // pieces
            begin = pl.multiple_of(turn_ref[0] * count, 16)
            copy = pltpu.make_async_copy(
                refs[index].at[pl.ds(begin, count), pl.ds(column, columns)],
                outs[group].at[pl.ds(row, count), pl.ds(place_at, columns)],
                sems.at[number],
            )
            copy.start()
            copies.append(copy)
        for copy in copies:
            copy.wait()

    return pl.pallas_call(
        body,
        out_shape=tuple(shape(size, jnp.bfloat16) for size in sizes),
        in_specs=[pl.BlockSpec(memory_space=pltpu.SMEM)]
        + [pl.BlockSpec(memory_space=pltpu.HBM)] * len(weights),
        out_specs=[pl.BlockSpec(memory_space=pltpu.VMEM)] * len(sizes),
        scratch_shapes=[pltpu.SemaphoreType.DMA((len(moves),))],
        compiler_params=pltpu.CompilerParams(vmem_limit_bytes=24 * 1024 * 1024),
        cost_estimate=cost("cut_rows"),
        name="cut_rows",
    )(turn, *weights)


def pack_grads(raw, in_gain, taps, bias, ssm_gain, ff_gain, heads, parts):
    def body(*refs):
        raw_ref, in_ref, taps_ref, bias_ref, ssm_ref, ff_ref = refs[:6]
        out = refs[-1]
        out[...] = jnp.zeros(out.shape, jnp.float32)

        def put(part, row, ref, size):
            begin = part * size
            rows = ref.shape[0]
            for at in range(0, size, 128):
                count = min(128, size - at)
                out[part, row : row + rows, :count] = ref[:, begin + at : begin + at + count]
                row += rows

        for part in range(parts):
            at = 0
            for ref in (raw_ref, in_ref, taps_ref, bias_ref, ssm_ref, ff_ref):
                size = ref.shape[1] // parts
                put(part, at, ref, size)
                at += ref.shape[0] * -(-size // 128)
            for number, ref in enumerate(refs[6:9]):
                out[part, 40 + number : 41 + number, :MH] = ref[...]

    (out,) = call_whole(
        body,
        (shape((parts, 48, 128)),),
        (raw, in_gain, taps, bias, ssm_gain, ff_gain) + tuple(heads),
        name="pack_grads",
    )
    return out


def unpack_grads(spots, block, heads, sizes):
    count = len(heads)

    def body(spots_ref, block_ref, *refs):
        z = spots_ref[0]
        head_refs, outs = refs[:count], refs[count:]
        total = jnp.zeros(heads[0].shape, jnp.float32)

        def take(row, count, width):
            parts = [
                block_ref[at // 8 : at // 8 + 1, at % 8 * 128 : at % 8 * 128 + width]
                for at in range(row, row + count)
            ]
            return jnp.concatenate(parts, axis=0).astype(jnp.float32)

        for at in range(count):
            step = lax.rem(z + (count - at), count)
            row = head_refs[0][...]
            for number in range(1, count):
                row = jnp.where(step == number, head_refs[number][...], row)
            total = total + row.astype(jnp.float32)
        outs[0][...] = take(0, MH, 128).T
        at = MH
        for out, (rows, size) in zip(outs[1:], sizes):
            for begin in range(0, size, 128):
                width = min(128, size - begin)
                out[:, begin : begin + width] = take(at, rows, width)
                at += rows
        for number, out in enumerate(outs[1 + len(sizes) :]):
            out[...] = total[:, number * 128 : number * 128 + MH]

    return call_whole(
        body,
        (shape((128, MH)),) + tuple(shape(size) for size in sizes) + (shape((1, MH)),) * 3,
        (spots, block) + tuple(heads),
        name="unpack_grads",
    )


def finish(spots, pieces, outs, extra=None):
    size = pieces[0].shape[1]

    def body(spots_ref, *refs):
        pieces_ref = refs[:4]
        out_refs = refs[4 + (extra is not None) :]
        y, c = spots_ref[0], spots_ref[1]
        for quarter in range(4):
            same_y = y == quarter // 2
            same_c = c == quarter % 2
            for out_ref, (_, _, moves) in zip(out_refs, outs):
                for source, rows, column, count in moves[quarter]:
                    own, by_c, by_y, by_yc = [
                        ref[rows, source : source + count] for ref in pieces_ref
                    ]
                    value = jnp.where(
                        same_y,
                        jnp.where(same_c, own, by_c),
                        jnp.where(same_c, by_y, by_yc),
                    )
                    out_ref[:, column : column + count] = value.astype(jnp.float32)
        if extra is not None:
            out_refs[0][:, outs[0][1] - extra.shape[1] :] = refs[4][...]

    args = (spots,) + tuple(pieces) + (() if extra is None else (extra,))
    return call_whole(
        body, tuple(shape((rows, columns)) for rows, columns, _ in outs), args, name="finish"
    )


def block_masks(segment, position):
    extent = segment.shape[0]
    slot = jnp.arange(extent, dtype=jnp.int32)
    moves = [jnp.ones((extent,), jnp.bool_)]
    for offset in range(1, CONV_K):
        moves.append((slot >= offset) & (jnp.roll(segment, offset) == segment))
    half = ATTENTION_HEAD // 2
    inverse = ROPE_BASE ** (-jnp.arange(half, dtype=jnp.float32) / half)
    angle = position.astype(jnp.float32)[:, None] * inverse[None, :]
    return (
        jnp.stack(moves, axis=1).astype(jnp.float32),
        causal_allowed(segment).astype(jnp.float32),
        jnp.tile(jnp.cos(angle), (1, 4)),
        jnp.tile(jnp.sin(angle), (1, 4)),
    )


def forward_pass(side, feed_grad, tokens_f, gains, mats, a_log, dt_bias, skip_d, segment, position):
    in_gain, conv_w, conv_b, ssm_gain, _, w_raw = gains
    w_first, w_second = mats
    moves, allowed, cosine, sine = block_masks(segment, position)
    normed_f, pull_norm_one = jax.vjp(rms_scale, tokens_f, in_gain.astype(jnp.float32))
    normed = normed_f.astype(jnp.bfloat16)
    conv_in = matmul_plain(normed, w_first)
    gate_z = matmul_plain(normed, w_second)
    raw_step = matmul_right(normed, w_raw)
    low, heads_out = attention_front(conv_in, gate_z, cosine, sine, allowed)
    mixer_args = (
        conv_in,
        raw_step,
        gate_z,
        conv_w.astype(jnp.float32),
        conv_b.astype(jnp.float32)[None],
        dt_bias[None],
        a_log[None],
        jnp.repeat(skip_d, HD)[None],
        ssm_gain.astype(jnp.float32)[None],
        moves,
        allowed,
    )
    act, scan, early_mine, early_theirs = mixer_front(
        side, heads_out, normed, feed_grad, *mixer_args
    )
    kept = (pull_norm_one, normed, mixer_args, act, scan, low, (cosine, sine, allowed))
    return (early_mine, early_theirs, kept)


def backward_pass(after, side, grads, w_raw, mats, kept):
    w_first, w_second = mats
    pull_norm_one, normed, mixer_args, act, scan, low, turn_args = kept
    residual_grad, gated_grad, heads_grad = grads
    qkv_low = attention_back(low, heads_grad, *turn_args)
    (
        z_low,
        conv_low,
        raw_low,
        raw_rows,
        mixed_mine,
        mixed_theirs,
        grad_ssm_gain,
        grad_conv_w,
        grad_conv_b,
        skip_lanes,
        grad_dt_bias,
        grad_a_log,
    ) = mixer_back(after, side, normed, qkv_low, gated_grad, scan, act, *mixer_args)
    grad_skip = jnp.sum(skip_lanes.reshape(MH, HD), axis=1)
    normed_grad = (
        matmul_right(z_low, w_second)
        + matmul_right(conv_low, w_first)
        + matmul_plain(raw_low, w_raw)
    )
    token_part, grad_in_gain = pull_norm_one(normed_grad)
    tokens_grad = (residual_grad + token_part).astype(jnp.bfloat16)
    small = (
        raw_rows,
        grad_in_gain[None],
        grad_conv_w,
        grad_conv_b,
        grad_ssm_gain,
        grad_a_log,
        grad_dt_bias,
        grad_skip[None],
    )
    return (tokens_grad, (mixed_mine, mixed_theirs), small)


AXES = ("shard", "replica")


def place(pieces, positions, dim, count):
    shape = list(pieces[0].shape)
    shape[dim] = count
    total = len(pieces)

    def body(where, *refs):
        out, held, sems = refs[total], refs[total + 1 : 2 * total + 1], refs[-1]
        loads, stores = [], []
        for number in range(total):
            spot = (slice(None),) * dim + (pl.ds(where[number], 1),)
            loads.append(
                pltpu.make_async_copy(refs[number], held[number], sems.at[0, number])
            )
            stores.append(
                pltpu.make_async_copy(held[number], out.at[spot], sems.at[1, number])
            )
        for load in loads:
            load.start()
        for load, store in zip(loads, stores):
            load.wait()
            store.start()
        for store in stores:
            store.wait()

    return pl.pallas_call(
        body,
        out_shape=jax.ShapeDtypeStruct(tuple(shape), pieces[0].dtype),
        in_specs=[pl.BlockSpec(memory_space=pltpu.SMEM)]
        + [pl.BlockSpec(memory_space=pl.ANY)] * total,
        out_specs=pl.BlockSpec(memory_space=pl.ANY),
        scratch_shapes=[pltpu.VMEM(piece.shape, piece.dtype) for piece in pieces]
        + [pltpu.SemaphoreType.DMA((2, total))],
        compiler_params=pltpu.CompilerParams(vmem_limit_bytes=24 * 1024 * 1024),
        cost_estimate=cost("place"),
        name="place",
    )(jnp.stack(positions).astype(jnp.int32), *pieces)


class Links:
    def __init__(self, shards_of, copies):
        self.z_size = shards_of // 2
        shard = lax.axis_index("shard")
        replica = lax.axis_index("replica")
        self.z, self.x = shard // 2, shard % 2
        self.y, self.c = replica // 2, replica % 2
        everyone = [(s, r) for s in range(shards_of) for r in range(copies)]

        def table(step):
            return [(s * copies + r, step(s, r)) for s, r in everyone]

        self.tables = {
            "x": table(lambda s, r: (s ^ 1) * copies + r),
            "y": table(lambda s, r: s * copies + (r ^ 2)),
            "c": table(lambda s, r: s * copies + (r ^ 1)),
            "z": table(lambda s, r: ((s + 2) % shards_of) * copies + r),
        }

    def send(self, value, axis):
        return lax.ppermute(value, AXES, self.tables[axis])

    def spread(self, value, axis):
        if axis == "z":
            pieces, spots = [value], [self.z]
            for step in range(1, self.z_size):
                pieces.append(self.send(pieces[-1], "z"))
                spots.append((self.z + self.z_size - step) % self.z_size)
            return place(pieces, spots, 0, self.z_size)
        spot = {"x": self.x, "y": self.y, "c": self.c}[axis]
        return place([value, self.send(value, axis)], [spot, 1 - spot], "zxyc".index(axis), 2)

    def gather(self, value, order):
        if value.ndim == 2:
            value = value[None, None, None, None]
        for axis in order:
            value = self.spread(value, axis)
        return value

    def gather_small(self, own):
        other = self.send(own, "x")
        pair = jnp.stack(
            [jnp.where(self.x == 0, own, other), jnp.where(self.x == 0, other, own)]
        )
        pieces = [pair]
        for _ in range(1, self.z_size):
            pieces.append(self.send(pieces[-1], "z"))
        stacked = jnp.stack(pieces)
        return jnp.concatenate(
            [
                lax.dynamic_index_in_dim(stacked, (self.z + self.z_size - at) % self.z_size, 0, False)
                for at in range(self.z_size)
            ]
        )

    def near(self, mine, theirs, after=()):
        both = stack(mine, self.send(theirs, "y"), after)
        return [both, self.send(both, "c")]

    def around(self, block):
        total = block(0).astype(jnp.bfloat16)
        for step in range(1, self.z_size):
            arrived = self.send(total, "z")
            total = (arrived.astype(jnp.float32) + block(step)).astype(jnp.bfloat16)
        return total

    def at_step(self, value, step):
        at = (self.z + 2 * self.z_size - 1 - step) % self.z_size
        return lax.dynamic_index_in_dim(value, at, 0, False).astype(jnp.float32)

    def add_small(self, value):
        value = value + self.send(value, "y")
        return value.reshape(self.z_size, 2, 48, 128)

    def reduce_mixed(self, mine, theirs, after):
        moved = self.send(theirs, "x")
        total = (self.at_step(mine, 0) + self.at_step(moved, 0)).astype(jnp.bfloat16)
        heads = [total[133:134]]
        for step in range(1, self.z_size):
            arrived = self.send(total, "z")
            heads.append(arrived[133:134])
            block = self.at_step(mine, step) + self.at_step(moved, step)
            row = lax.broadcasted_iota(jnp.int32, block.shape, 0)
            block = jnp.where(row == 133, 0.0, block)
            total = (arrived.astype(jnp.float32) + block).astype(jnp.bfloat16)
        return moved, self.quarters(total[:128], after), total[128:], heads

    def quarters(self, total, after=()):
        by_y = self.send(total, "y")
        if after:
            by_y = hold(by_y, after)
        return (total, self.send(total, "c"), by_y, self.send(by_y, "c"))

    def reduce_xz(self, mine, theirs):
        moved = self.send(theirs, "x")
        return moved, self.quarters(
            self.around(lambda step: self.at_step(mine, step) + self.at_step(moved, step))
        )


    def reduce_zx(self, value, after):
        total = self.around(lambda step: self.at_step(value, step))
        mine = lax.dynamic_index_in_dim(total, self.x, 0, False)
        theirs = lax.dynamic_index_in_dim(total, 1 - self.x, 0, False)
        moved = self.send(theirs, "x")
        mine = hold(mine, after)
        return self.quarters(
            (mine.astype(jnp.float32) + moved.astype(jnp.float32)).astype(jnp.bfloat16)
        )


def pack_small(in_gain, conv_w, conv_b, ssm_gain, ff_gain, raw):
    def rows(value):
        flat = value.reshape(-1)
        return jnp.pad(flat, (0, -flat.shape[0] % 128)).reshape(-1, 128)

    packed = jnp.concatenate([rows(v) for v in (raw.T, in_gain, conv_w, conv_b, ssm_gain, ff_gain)])
    return jnp.pad(packed, ((0, -packed.shape[0] % 16), (0, 0)))


def unpack_small(gathered, own):
    in_gain, conv_w, conv_b, ssm_gain, ff_gain, raw = own
    parts = gathered.shape[0]
    at = 0
    out = []
    for value in (raw.T, in_gain, conv_w, conv_b, ssm_gain, ff_gain):
        count = -(-value.size // 128)
        flat = gathered[:, at : at + count].reshape(parts, -1)[:, : value.size]
        at += count
        shaped = flat.reshape((parts,) + value.shape)
        if value.ndim == 1:
            out.append(shaped.reshape(-1))
        else:
            out.append(shaped.transpose(1, 0, 2).reshape(value.shape[0], -1))
    return tuple(out[1:]) + (out[0],)


def shards(
    copies,
    tokens,
    cotangent,
    seq_lengths,
    seq_starts,
    in_gain,
    w_in,
    conv_w,
    conv_b,
    a_log,
    dt_bias,
    skip_d,
    ssm_gain,
    w_out,
    w_query,
    w_key,
    w_value,
    w_attn_out,
    ff_gain,
    w_gate,
    w_up,
    w_down,
):
    parts = MH * HD // w_out.shape[0]
    width = MH * HD
    channels = width + 2 * NS
    quick = parts == 8 and copies == 4
    links = Links(parts, copies)
    own_small = (in_gain, conv_w, conv_b, ssm_gain, ff_gain, w_in[:, width + channels :])
    pieces = 4 if quick else 1
    turn = jnp.stack([links.y * 2 + links.c if quick else jnp.int32(0)]).astype(jnp.int32)
    weights = (w_in, w_query, w_key, w_value, w_out, w_attn_out, w_gate, w_up, w_down)
    q_cols = QH * ATTENTION_HEAD
    k_cols = KVH * ATTENTION_HEAD
    spans, blocks, at = [], [], 0
    for index, column in ((0, 0), (1, 0), (2, 0), (2, BLOCK), (3, 0), (3, BLOCK), (4, 0)):
        count = weights[index + 4].shape[0] // pieces
        blocks.append((index, column, BLOCK, at, 0))
        spans.append((at, count))
        at += count
    (pack,) = cut_rows(turn, pieces, weights[4:], [(at, BLOCK, blocks)])
    cut_in = w_in.shape[0] // pieces
    first, second = cut_rows(
        turn,
        pieces,
        weights[:4],
        [
            (
                cut_in,
                MIXED // 2,
                [
                    (0, width, channels, 0, 0),
                    (2, 0, k_cols, 0, channels),
                    (3, 0, k_cols, 0, channels + k_cols),
                ],
            ),
            (cut_in, MIXED // 2, [(0, 0, width, 0, 0), (1, 0, q_cols, 0, width)]),
        ],
    )
    if quick:
        small_all = links.gather_small(pack_small(*own_small))
        mats = tuple(
            links.gather(value, order).reshape(-1, MIXED // 2)
            for value, order in ((first, "zxyc"), (second, "zyxc"))
        )
        pack = lax.all_gather(pack, AXES, axis=0)
    else:
        small_all = lax.all_gather(pack_small(*own_small), "shard", axis=0)
        mats = tuple(
            lax.all_gather(value, "shard", axis=0, tiled=True) for value in (first, second)
        )
        pack = lax.all_gather(pack, "shard", axis=0)
    gains = unpack_small(small_all, own_small)
    segment, position = layout(seq_lengths[0], seq_starts[0], tokens.shape[0])
    side = jnp.stack([links.y if quick else jnp.int32(0)]).astype(jnp.int32)
    valid = (segment >= 0).astype(jnp.float32)[:, None]
    feed_grad = jnp.where(valid > 0.0, cotangent, 0.0).astype(jnp.bfloat16)
    early_mine, early_theirs, kept = forward_pass(
        side,
        feed_grad,
        tokens.astype(jnp.float32),
        gains,
        mats,
        a_log,
        dt_bias,
        skip_d,
        segment,
        position,
    )
    (
        result,
        late_mine,
        late_theirs,
        residual_grad,
        grad_ff_gain,
        gated_grad,
        heads_grad,
    ) = middle(
        side, pack, spans, tokens, early_mine, cotangent, valid, gains[4].astype(jnp.float32)[None]
    )
    model = w_in.shape[0] * parts
    quarter = BLOCK // 4
    half_ff, quarter_ff = FF // 2, FF // 4
    place_spots = jnp.stack([links.x, links.c]).astype(jnp.int32)
    at_normed = width + q_cols
    early_four = links.near(early_mine, early_theirs) if quick else ()
    tokens_grad, (mixed_mine, mixed_theirs), small = backward_pass(
        early_four[:1], side, (residual_grad, gated_grad, heads_grad), gains[5], mats, kept
    )
    here = lax.axis_index("shard")

    def mine(value):
        size = value.shape[-1] // parts
        return lax.dynamic_slice_in_dim(value, here * size, size, value.ndim - 1)

    out_rows, attn_rows = w_out.shape[0], w_attn_out.shape[0]
    down_rows, model_rows = w_down.shape[0], w_in.shape[0]
    if quick:
        whole = slice(None)

        def plain(rows):
            return [[(0, rows, number * quarter, quarter)] for number in range(4)]

        mixed_moves = [[[] for _ in range(4)] for _ in range(4)]
        begin = 0
        for index, column, columns in (
            (0, 0, width),
            (1, 0, q_cols),
            (0, width, channels),
            (2, 0, k_cols),
            (3, 0, k_cols),
        ):
            for number in range(4):
                low = max(begin, number * BLOCK)
                high = min(begin + columns, (number + 1) * BLOCK)
                if low < high:
                    mixed_moves[index][number].append(
                        (low - number * BLOCK, whole, column + low - begin, high - low)
                    )
            begin += columns
        spots = jnp.stack([links.y, links.c]).astype(jnp.int32)
        packed = pack_grads(*small[:5], grad_ff_gain, small[5:], parts)
        packed = packed + links.send(packed, "c")
        late_four = links.near(late_mine, late_theirs, (packed,))
        feed_parts = outer(
            place_spots,
            [
                (
                    late_four,
                    0,
                    model,
                    late_four,
                    [(model, quarter_ff), (model + half_ff, quarter_ff)],
                )
            ],
            links.z_size,
            True,
        )
        at_hidden = model + FF
        out_right = (late_four, [(at_hidden + FF, quarter)])
        (out_parts,) = outer(
            place_spots,
            [
                (early_four, 0, width) + out_right,
                (early_four, width, q_cols) + out_right,
                (late_four, at_hidden, FF, early_four, [(at_normed + model, quarter)]),
            ],
            links.z_size,
            False,
            feed_parts[1:],
        )
        mixed_four = links.near(mixed_mine, mixed_theirs, (out_parts,))
        mixed_parts = outer(
            place_spots,
            [(early_four, at_normed, model, mixed_four, [(0, BLOCK)])],
            links.z_size,
            True,
            (),
            links.add_small(packed),
        )
        _, feed_pieces = links.reduce_xz(*feed_parts)
        gate, up = finish(
            spots,
            feed_pieces,
            [
                (
                    model_rows,
                    FF,
                    [[(at, whole, number * quarter_ff, quarter_ff)] for number in range(4)],
                )
                for at in (0, quarter_ff)
            ],
        )
        out, attn, down = finish(
            spots,
            links.reduce_zx(out_parts, mixed_parts[1:]),
            [
                (rows, BLOCK, plain(slice(at, at + rows)))
                for rows, at in (
                    (out_rows, 0),
                    (attn_rows, out_rows),
                    (down_rows, out_rows + attn_rows),
                )
            ],
        )
        mixed_moved, mixed_pieces, small_rows, head_rows = links.reduce_mixed(
            *mixed_parts, (gate, out)
        )
        raw_part, *totals = unpack_grads(
            jnp.stack([links.z]).astype(jnp.int32),
            small_rows,
            head_rows,
            [(value.shape[0], value.shape[1] // parts) for value in small[1:5]]
            + [(1, model // parts)],
        )
        totals = [totals[0][0], totals[1]] + [value[0] for value in totals[2:]]
        projection, query, key, value = finish(
            spots,
            mixed_pieces,
            [
                (model_rows, columns, moves)
                for columns, moves in zip(
                    (width + channels + MH, q_cols, k_cols, k_cols), mixed_moves
                )
            ],
            raw_part,
        )
    else:

        def joined(first, second):
            return jnp.concatenate([first, second], axis=1)

        def share(left, right):
            part = lax.psum_scatter(
                matmul_left(left, right).astype(jnp.bfloat16),
                "shard",
                scatter_dimension=0,
                tiled=True,
            )
            return lax.psum(part, "replica").astype(jnp.float32)

        branch = joined(late_mine[:, model + 2 * FF :], late_theirs[:, model + 2 * FF :])
        mixed = share(kept[1], joined(mixed_mine, mixed_theirs))
        down = share(late_mine[:, model + FF : model + 2 * FF], feed_grad)
        normed_two = late_mine[:, :model]
        gate, up = [
            share(
                normed_two,
                joined(late_mine[:, at : at + half_ff], late_theirs[:, at : at + half_ff]),
            )
            for at in (model, model + half_ff)
        ]
        out = share(early_mine[:, :width], branch)
        attn = share(early_mine[:, width : width + q_cols], branch)
        summed = [lax.psum(value, AXES) for value in small + (grad_ff_gain,)]
        raw_part = mine(summed[0]).T
        totals = [mine(summed[1])[0], mine(summed[2])]
        totals += [mine(summed[at])[0] for at in (3, 4, 8)]
        totals += [value[0] for value in summed[5:8]]
        at = width + q_cols
        projection = jnp.concatenate(
            [mixed[:, :width], mixed[:, at : at + channels], raw_part], axis=1
        )
        query = mixed[:, width:at]
        at += channels
        key = mixed[:, at : at + k_cols]
        value = mixed[:, at + k_cols :]
    return (
        result,
        tokens_grad,
        totals[0],
        projection,
        totals[1],
        totals[2],
        totals[5],
        totals[6],
        totals[7],
        totals[3],
        out,
        query,
        key,
        value,
        attn,
        totals[4],
        gate,
        up,
        down,
    )


def solution(mesh):
    in_specs = (
        P(("shard", "replica"), None),
        P(("shard", "replica"), None),
        P(("shard", "replica"), None),
        P(("shard", "replica"), None),
        P("shard"),
        P("shard", None),
        P(None, "shard"),
        P("shard"),
        P(),
        P(),
        P(),
        P("shard"),
        P("shard", None),
        P("shard", None),
        P("shard", None),
        P("shard", None),
        P("shard", None),
        P("shard"),
        P("shard", None),
        P("shard", None),
        P("shard", None),
    )
    out_specs = (
        P(("shard", "replica"), None),
        P(("shard", "replica"), None),
        P("shard"),
        P("shard", None),
        P(None, "shard"),
        P("shard"),
        P(),
        P(),
        P(),
        P("shard"),
        P("shard", None),
        P("shard", None),
        P("shard", None),
        P("shard", None),
        P("shard", None),
        P("shard"),
        P("shard", None),
        P("shard", None),
        P("shard", None),
    )

    def local(*args):
        return shards(mesh.shape["replica"], *args)

    return jax.shard_map(local, mesh=mesh, in_specs=in_specs, out_specs=out_specs, check_vma=False)
```
